512 devices in a mesh: wide: 64 (over y, z), narrow: 8 (over x, core).
Axes of the slice: x: 4, y: 4, z: 16, core: 2. Of those that a mesh axis runs over, the one named last changes fastest.
Arguments:
- right_side: float32 [16384, 1024], P(('wide', 'narrow')), may hold values from -6 to 6
- start_guess: float32 [16384, 1024], P(('wide', 'narrow')), may hold values from -6 to 6
- block_diag: float32 [16384, 4096], P(('wide', 'narrow')), may hold values from -0.375 to 0.375
- face_lift: float32 [6, 64, 64], replicated, may hold values from -0.75 to 0.75
- face_scale: float32 [16384, 6], P(('wide', 'narrow')), may hold values from 0.05 to 0.2
- neighbors: int32 [16384, 6], P(('wide', 'narrow')), may hold values from 0 to 40, as said below
- ghost_send: int32 [512, 8], P(('wide', 'narrow')), may hold values from 0 to 31, as said below
Outputs:
- solution: float32 [16384, 1024], P(('wide', 'narrow'))
- new_residual: float32 [16384, 1024], P(('wide', 'narrow'))
The draws below stay inside these ranges and needn't reach their ends.
Inputs may be any that keep to these rules, and one draw needn't show every extreme that they name: `neighbors`: values below 32 name the device's own elements, 32 + k the k-th ghost from the previous device, 36 + k the k-th ghost from the next device, 40 the zero row; the first device names no ghost of a previous device and the last none of a next device. `ghost_send`: each row holds 8 distinct own elements of that device.
All inputs are finite; a program needn't handle non-finite values.
Results may differ from the reference program's by a relative error of at most 0.0003.
Values sent between devices are 32-bit elements; how exact they have to be, the bound alone decides.
No kernel may reach another device: no remote copies, remote signals or barrier semaphores. Data moves between devices by JAX's collectives and lax.ppermute only.
A program may use at most 64 MiB of HBM per device.

```python
import math
import jax
import jax.numpy as jnp
from jax import lax

NODES = 64
RHS = 16
STEPS = 4
FACES = 6
E_DEV = 32
GHOST = 4
ELEMS = 16384
BASIS = 80


def draw_neighbors(key, part):
    key = jax.random.fold_in(key, 11)
    device_count = ELEMS // E_DEV
    perm_key, rand_key = jax.random.split(key)
    device_keys = jax.random.split(perm_key, device_count)
    first_face = jax.vmap(lambda device_key: jax.random.permutation(device_key, E_DEV).astype(jnp.int32))(device_keys)
    others = jax.random.randint(rand_key, (device_count, E_DEV, 3), 0, E_DEV).astype(jnp.int32)
    slots = jnp.arange(E_DEV, dtype=jnp.int32) % GHOST
    device_ids = jnp.arange(device_count, dtype=jnp.int32)[:, None]
    boundary = E_DEV + 2 * GHOST
    before = jnp.where(device_ids == 0, boundary, E_DEV + slots[None, :]).astype(jnp.int32)
    after = jnp.where(device_ids == device_count - 1, boundary, E_DEV + GHOST + slots[None, :]).astype(jnp.int32)
    joined = jnp.concatenate([first_face[:, :, None], others, before[:, :, None], after[:, :, None]], axis=2)
    return joined.reshape(ELEMS, 6)


def draw_ghost_send(key, part):
    key = jax.random.fold_in(key, 23)
    device_count = ELEMS // E_DEV
    device_keys = jax.random.split(key, device_count)

    def single_device(device_key):
        pick_key, second = jax.random.split(device_key)
        middle = jax.random.permutation(pick_key, E_DEV - 2)[:2 * GHOST - 2].astype(jnp.int32) + 1
        chosen = jnp.concatenate([jnp.array([0, E_DEV - 1], jnp.int32), middle])
        return chosen[jax.random.permutation(second, 2 * GHOST)]
    return jax.vmap(single_device)(device_keys)


def block_scale(rng, dims, cuts, least, largest):
    loudness = 1.0
    for position, shards_of in cuts:
        heights = jax.random.uniform(jax.random.fold_in(jax.random.fold_in(rng, 6), position), (shards_of,), jnp.float32, least / len(cuts), largest / len(cuts))
        loudness = loudness * jnp.repeat(jnp.exp(heights), dims[position] // shards_of).reshape((-1,) + (1,) * (len(dims) - 1 - position))
    return loudness


def normal_values(own_key, extent, width, most, cuts=(), kind=jnp.bfloat16):
    values = width * jax.random.normal(own_key, extent, jnp.float32)
    if cuts:
        values = values * block_scale(own_key, extent, cuts, -0.22, 0.18)
    return jnp.clip(values, -most, most).astype(kind)


def setup_inputs(seed: int = 0) -> dict:
    streams_of = jax.random.split(jax.random.key(seed), 8)
    right_side = normal_values(streams_of[0], (ELEMS, RHS * NODES), 1.0, 6.0, ((0, 512),), jnp.float32)
    start_guess = normal_values(streams_of[1], (ELEMS, RHS * NODES), 0.5, 6.0, ((0, 512),), jnp.float32)
    block_diag = normal_values(streams_of[2], (ELEMS, NODES * NODES), 256 ** -0.5, 0.375, ((0, 512),), jnp.float32)
    face_lift = normal_values(streams_of[3], (FACES, NODES, NODES), 64 ** -0.5, 0.75, (), jnp.float32)
    face_scale = jnp.clip(jnp.exp(math.log(0.2) - 1.3862944 * jax.random.uniform(streams_of[4], (ELEMS, FACES), jnp.float32) ** block_scale(streams_of[4], (ELEMS, FACES), ((0, 512),), -0.2, 0.2)), 0.05, 0.2)
    neighbors = draw_neighbors(jax.random.fold_in(streams_of[7], 71), 0)
    ghost_send = draw_ghost_send(jax.random.fold_in(streams_of[7], 71), 0)
    return {"right_side": right_side, "start_guess": start_guess, "block_diag": block_diag, "face_lift": face_lift, "face_scale": face_scale, "neighbors": neighbors, "ghost_send": ghost_send}


basis_gain = 1.5

def operate(vector, workspace, blocks, face_lift, face_scale, neighbors):
    elem_count, row_width = vector.shape
    node_count = face_lift.shape[1]
    rhs_count = row_width // node_count
    own_block = vector.reshape(elem_count, rhs_count, node_count)
    matrices = blocks.reshape(elem_count, node_count, node_count)
    nearby = workspace[neighbors].reshape(elem_count, neighbors.shape[1], rhs_count, node_count)
    nearby = nearby * face_scale[:, :, None, None]
    result = own_block + jnp.einsum('eij,erj->eri', matrices, own_block, precision=lax.Precision.HIGHEST)
    result = result + jnp.einsum('fij,efrj->eri', face_lift, nearby, precision=lax.Precision.HIGHEST)
    return result.reshape(elem_count, row_width)

def apply_all(vector, block_diag, face_lift, face_scale, neighbors, ghost_send):
    device_count = ghost_send.shape[0]
    ghost_rows = ghost_send.shape[1] // 2
    row_width = vector.shape[1]
    per_device = vector.reshape(device_count, -1, row_width)
    outgoing = jnp.take_along_axis(per_device, ghost_send[:, :, None], axis=1)
    empty = jnp.zeros((1, ghost_rows, row_width), jnp.float32)
    from_prev = jnp.concatenate([empty, outgoing[:-1, ghost_rows:]], 0)
    from_next = jnp.concatenate([outgoing[1:, :ghost_rows], empty], 0)
    workspace = jnp.concatenate([per_device, from_prev, from_next, jnp.zeros((device_count, 1, row_width), jnp.float32)], 1)

    def single(pieces):
        return operate(pieces[0], pieces[1], pieces[2], face_lift, pieces[3], pieces[4])
    result = lax.map(single, (per_device, workspace, block_diag.reshape(device_count, -1, block_diag.shape[1]), face_scale.reshape(device_count, -1, face_scale.shape[1]), neighbors.reshape(device_count, -1, neighbors.shape[1])))
    return result.reshape(vector.shape)

def least_squares(gram_total, rhs_count, steps_count):
    pattern = jnp.eye(steps_count + 1, steps_count, dtype=jnp.float32)
    pattern = pattern + jnp.eye(steps_count + 1, steps_count, k=-1, dtype=jnp.float32) / basis_gain
    combine = jnp.kron(pattern, jnp.eye(rhs_count, dtype=jnp.float32))
    weighted = jnp.dot(gram_total, combine, precision=lax.Precision.HIGHEST)
    normal_matrix = jnp.dot(combine.T, weighted, precision=lax.Precision.HIGHEST)
    target = weighted[:rhs_count].T
    factor = jnp.linalg.cholesky(normal_matrix)
    coeffs = jax.scipy.linalg.cho_solve((factor, True), target)
    return (coeffs, jnp.dot(combine, coeffs, precision=lax.Precision.HIGHEST))

def reference(right_side, start_guess, block_diag, face_lift, face_scale, neighbors, ghost_send):

    def apply_operator(vector):
        return apply_all(vector, block_diag, face_lift, face_scale, neighbors, ghost_send)
    krylov_basis = [right_side - apply_operator(start_guess)]
    for power_index in range(STEPS):
        latest = krylov_basis[-1]
        krylov_basis.append(basis_gain * (apply_operator(latest) - latest))
    stacked = jnp.stack([item.reshape(ELEMS, RHS, NODES) for item in krylov_basis])
    gram_total = jnp.einsum('aeri,besi->arbs', stacked, stacked, precision=lax.Precision.HIGHEST).reshape(BASIS, BASIS)
    coeffs, mixed = least_squares(gram_total, RHS, STEPS)
    update = jnp.einsum('aeri,ars->esi', stacked[:STEPS], coeffs.reshape(STEPS, RHS, RHS), precision=lax.Precision.HIGHEST)
    solution = start_guess + update.reshape(ELEMS, RHS * NODES)
    change = jnp.einsum('aeri,ars->esi', stacked, mixed.reshape(STEPS + 1, RHS, RHS), precision=lax.Precision.HIGHEST)
    new_residual = krylov_basis[0] - change.reshape(ELEMS, RHS * NODES)
    return (solution, new_residual)
```

```python
import functools

import jax
import jax.numpy as jnp
from jax import lax
from jax.experimental import pallas as pl
from jax.experimental.pallas import tpu as pltpu
from jax.sharding import Mesh, PartitionSpec as P

STEPS = 4
GAIN = 1.5
RHS = 16
NODES = 64
FACES = 6
ELEMS = 32
GHOST = 4
F32 = jnp.float32
BF16 = jnp.bfloat16


VMEM = pl.BlockSpec(memory_space=pltpu.VMEM)
SMEM = pl.BlockSpec(memory_space=pltpu.SMEM)
PARAMS = pltpu.CompilerParams(vmem_limit_bytes=32 * 1024 * 1024)


def tiles(count):
    return jax.ShapeDtypeStruct((count, 8, 128), F32)


def dot_nt(left, right):
    return lax.dot_general(left, right, (((1,), (1,)), ((), ())), preferred_element_type=F32)


def split(value):
    high = value.astype(BF16)
    low = (value - high.astype(F32)).astype(BF16)
    return high, low


def swap(value):
    return pltpu.roll(value, 64, 1)


def left_half(shape):
    return lax.broadcasted_iota(jnp.int32, shape, len(shape) - 1) < 64


def to_tiles(ref, out):
    for t in range(8):
        out[:, t, :] = ref[:, t * 128 : (t + 1) * 128]


def send_rows(send, source, to_prev, to_next):
    for k in range(GHOST):
        to_prev[k] = source[send[k]]
        to_next[k] = source[send[GHOST + k]]


def pack_kernel(send, guess, tiled, to_prev, to_next):
    to_tiles(guess, tiled)
    send_rows(send, tiled, to_prev, to_next)


def prep_kernel(blocks, lift, right, block_parts, lift_parts, right_tiled):
    high, low = split(blocks[...])
    block_parts[:, :128] = high
    block_parts[:, 128:] = low
    high, low = split(lift[...])
    lift_parts[:, :128] = high
    lift_parts[:, 128:256] = high
    lift_parts[:, 256:] = low
    to_tiles(right, right_tiled)


def lifted(vector, lift_parts):
    high, low = split(vector)
    return dot_nt(jnp.concatenate([high, low, high], 1), lift_parts[...])


def gather_faces(total, element, neighbors, scale, source, place):
    for f in range(FACES):
        row = element * FACES + f
        total = total + scale[row] * source[f, place(neighbors[row])]
    return total


def dense(vector):
    upper, lower = [], []
    mask = left_half((8, 128))
    for pair in range(ELEMS // 2):
        first, second = vector[2 * pair], vector[2 * pair + 1]
        upper.append(jnp.where(mask, first, swap(second)))
        lower.append(jnp.where(mask, swap(first), second))
    return jnp.concatenate([jnp.concatenate(upper, 1), jnp.concatenate(lower, 1)], 0)


def own_part(vector, block_parts, lift_parts, neighbors, scale, out, own_lifted):
    value = vector[...].reshape(ELEMS * 8, 128)
    product = lifted(value, lift_parts)
    for f in range(FACES):
        own_lifted[f, :ELEMS] = product[:, f * 128 : (f + 1) * 128].reshape(ELEMS, 8, 128)
        own_lifted[f, ELEMS] = jnp.zeros((8, 128), F32)
    mask = left_half((ELEMS * 8, 128))
    high, low = split(value)
    high, low = high.astype(F32), low.astype(F32)
    turned_high, turned_low = swap(high), swap(low)
    first = jnp.where(mask, low, turned_high).astype(BF16)
    second = jnp.where(mask, turned_low, high).astype(BF16)
    first_rest = jnp.where(mask, high, 0.0).astype(BF16)
    second_rest = jnp.where(mask, 0.0, high).astype(BF16)
    first = jnp.concatenate([first, first_rest], 1)
    second = jnp.concatenate([second, second_rest], 1)
    mask = left_half((8, 128))
    for group in range(ELEMS // 4):
        rows = slice(group * 32, (group + 1) * 32)
        both = jnp.concatenate([first[rows], second[rows]], 0)
        result = dot_nt(both, block_parts[group * 256 : (group + 1) * 256, :])
        for part in range(4):
            lanes = slice((part // 2) * 128, (part // 2) * 128 + 128)
            top = result[part * 8 : part * 8 + 8, lanes]
            bottom = result[32 + part * 8 : 40 + part * 8, lanes]
            if part % 2 == 0:
                total = jnp.where(mask, top, swap(bottom))
            else:
                total = jnp.where(mask, swap(top), bottom)
            element = group * 4 + part
            out[element] = gather_faces(
                total, element, neighbors, scale, own_lifted, lambda n: jnp.minimum(n, ELEMS)
            )


def gram_rows(stack_high, stack_low, newest, count):
    high, low = split(newest)
    left = jnp.concatenate([high, high, low], 1)
    right = jnp.concatenate([stack_high, stack_low, stack_high], 1)
    return dot_nt(left, right)


def first_own_kernel(neighbors, scale, vector, block_parts, lift_parts, out, own_lifted):
    own_part(vector, block_parts, lift_parts, neighbors, scale, out, own_lifted)


def own_kernel(index, neighbors, scale, vector, block_parts, lift_parts, *rest):
    if index:
        old_high, old_low, out, gram, high_out, low_out, own_lifted = rest
    else:
        out, gram, high_out, low_out, own_lifted = rest
    own_part(vector, block_parts, lift_parts, neighbors, scale, out, own_lifted)
    new_gram(index, vector, old_high if index else None, old_low if index else None, gram, high_out, low_out)


def new_gram(index, vector, old_high, old_low, gram, high_out, low_out):
    newest = dense(vector)
    high, low = split(newest)
    if index:
        high_out[: 16 * index] = old_high[...]
        low_out[: 16 * index] = old_low[...]
    high_out[16 * index :] = high
    low_out[16 * index :] = low
    gram[...] = gram_rows(high_out[...], low_out[...], newest, index + 1)


def ghost_total(own, from_prev, from_next, lift_parts, neighbors, scale, ghost_lifted):
    ghosts = jnp.concatenate([from_prev[...], from_next[...]], 0).reshape(2 * GHOST * 8, 128)
    product = lifted(ghosts, lift_parts)
    for f in range(FACES):
        ghost_lifted[f, : 2 * GHOST] = product[:, f * 128 : (f + 1) * 128].reshape(2 * GHOST, 8, 128)
        ghost_lifted[f, 2 * GHOST] = jnp.zeros((8, 128), F32)
    place = lambda n: jnp.where(n >= ELEMS, n - ELEMS, 2 * GHOST)
    for element in range(ELEMS):
        yield element, gather_faces(own[element], element, neighbors, scale, ghost_lifted, place)


def first_ghost_kernel(
    neighbors, scale, send, own, from_prev, from_next, lift_parts, right, guess,
    out, to_prev, to_next, ghost_lifted,
):
    for element, total in ghost_total(own, from_prev, from_next, lift_parts, neighbors, scale, ghost_lifted):
        out[element] = right[element] - (guess[element] + total)
    send_rows(send, out, to_prev, to_next)


def ghost_kernel(
    neighbors, scale, send, own, from_prev, from_next, lift_parts,
    out, to_prev, to_next, ghost_lifted,
):
    for element, total in ghost_total(own, from_prev, from_next, lift_parts, neighbors, scale, ghost_lifted):
        out[element] = GAIN * total
    send_rows(send, out, to_prev, to_next)


def last_kernel(
    neighbors, scale, own, from_prev, from_next, lift_parts, old_high, old_low,
    gram0, gram1, gram2, gram3, high_out, low_out, packed, ghost_lifted, newest, gram4,
):
    for element, total in ghost_total(own, from_prev, from_next, lift_parts, neighbors, scale, ghost_lifted):
        newest[element] = GAIN * total
    new_gram(STEPS, newest, old_high, old_low, gram4, high_out, low_out)
    packed[0:16] = jnp.concatenate([gram4[...], gram1[...], gram0[...]], 1)
    packed[16:32] = jnp.concatenate([gram3[...], gram2[...], jnp.zeros((16, 16), F32)], 1)


def solve_spd(system):
    size, block = 64, 4
    row_id = lax.broadcasted_iota(jnp.int32, (size, 128), 0)
    for start in range(0, size, block):
        columns = [jnp.broadcast_to(system[:, start + j : start + j + 1], (size, 128)) for j in range(block)]
        rows = [system[start + i : start + i + 1, :] for i in range(block)]
        pivots = [[columns[j][start + i : start + i + 1, :] for j in range(block)] for i in range(block)]
        for j in range(block):
            inverse = 1.0 / pivots[j][j]
            rows[j] = rows[j] * inverse
            for l in range(j + 1, block):
                pivots[j][l] = pivots[j][l] * inverse
            for i in range(block):
                if i != j:
                    factor = pivots[i][j]
                    rows[i] = rows[i] - factor * rows[j]
                    for l in range(j + 1, block):
                        pivots[i][l] = pivots[i][l] - factor * pivots[j][l]
        update = system
        for j in range(block):
            update = update - columns[j] * rows[j]
        for j in range(block):
            update = jnp.where(row_id == start + j, rows[j], update)
        system = update
    return system


def solve_kernel(packed, high, low, first, guess, solution, residual, gram_low, tiled):
    total = jnp.sum(packed[...], 0)
    upper, lower = total[:16], total[16:]
    lane = lax.broadcasted_iota(jnp.int32, (16, 128), 1)
    pieces = [
        (pltpu.roll(upper, 16, 1), 16),
        (pltpu.roll(upper, 48, 1), 32),
        (pltpu.roll(lower, 64, 1), 48),
        (lower, 64),
        (upper, 80),
    ]
    for a, (piece, width) in enumerate(pieces):
        gram_low[16 * a : 16 * a + 16, :] = jnp.where(lane < width, piece, 0.0)
    gram_low[80:, :] = jnp.zeros((48, 128), F32)
    lower_part = gram_low[...]
    row = lax.broadcasted_iota(jnp.int32, (128, 128), 0) // 16
    column = lax.broadcasted_iota(jnp.int32, (128, 128), 1) // 16
    gram = jnp.where(row >= column, lower_part, lower_part.T)
    weighted = gram[:64] + gram[16:80] * (1.0 / GAIN)
    lane = lax.broadcasted_iota(jnp.int32, (64, 128), 1)
    normal = weighted + pltpu.roll(weighted, 112, 1) * (1.0 / GAIN)
    system = jnp.where(lane < 64, normal, pltpu.roll(weighted, 64, 1))
    system = jnp.where(lane < 80, system, 0.0)
    coeffs = pltpu.roll(solve_spd(system), 64, 1)
    empty = jnp.zeros((16, 128), F32)
    padded = jnp.concatenate([coeffs, empty], 0)
    mixed = padded + jnp.concatenate([empty, coeffs], 0) * (1.0 / GAIN)
    lane = lax.broadcasted_iota(jnp.int32, (80, 128), 1)
    both = jnp.where(lane < 16, padded, pltpu.roll(mixed, 16, 1))
    both = jnp.where(lane < 32, both, 0.0)
    both = jnp.concatenate([both, jnp.zeros((48, 128), F32)], 0).T[:32]
    mask_high, mask_low = split(both)
    change = jnp.dot(mask_high[:, :80], high[...], preferred_element_type=F32)
    change = change + jnp.dot(mask_high[:, :80], low[...], preferred_element_type=F32)
    change = change + jnp.dot(mask_low[:, :80], high[...], preferred_element_type=F32)
    mask = left_half((8, 128))
    for pair in range(ELEMS // 2):
        lanes = slice(pair * 128, pair * 128 + 128)
        top, bottom = change[0:8, lanes], change[8:16, lanes]
        tiled[0, 2 * pair] = jnp.where(mask, top, swap(bottom))
        tiled[0, 2 * pair + 1] = jnp.where(mask, swap(top), bottom)
        top, bottom = change[16:24, lanes], change[24:32, lanes]
        tiled[1, 2 * pair] = first[2 * pair] - jnp.where(mask, top, swap(bottom))
        tiled[1, 2 * pair + 1] = first[2 * pair + 1] - jnp.where(mask, swap(top), bottom)
    for t in range(8):
        lanes = slice(t * 128, t * 128 + 128)
        solution[:, lanes] = guess[:, lanes] + tiled[0, :, t, :]
        residual[:, lanes] = tiled[1, :, t, :]


def call(kernel, outs, scratch, specs):
    return pl.pallas_call(
        kernel,
        out_shape=outs,
        in_specs=specs,
        out_specs=[VMEM] * len(outs),
        scratch_shapes=scratch,
        compiler_params=PARAMS,
    )


def shifted(block, axes, distance):
    devices = range(lax.axis_size(axes))
    route = [(i - distance, i) for i in devices if i - distance in devices]
    return lax.ppermute(block, axes, route)


def spread(value, axis):
    count = lax.axis_size(axis)
    return lax.all_to_all(jnp.broadcast_to(value[None], (count,) + value.shape), axis, 0, 0)


def local(right_side, start_guess, block_diag, face_lift, face_scale, neighbors, ghost_send, axes):
    send = ghost_send.reshape(2 * GHOST)
    near = neighbors.reshape(ELEMS * FACES)
    scale = face_scale.reshape(ELEMS * FACES)
    sent = [tiles(GHOST), tiles(GHOST)]
    guess, to_prev, to_next = call(pack_kernel, [tiles(ELEMS)] + sent, [], [SMEM, VMEM])(send, start_guess)

    def exchange(to_prev, to_next):
        return shifted(to_next, axes, 1), shifted(to_prev, axes, -1)

    from_prev, from_next = exchange(to_prev, to_next)
    matrices = block_diag.reshape(ELEMS * NODES, NODES)
    matrices = jnp.concatenate([matrices, matrices], 1)
    lift = jnp.concatenate(
        [jnp.pad(face_lift, ((0, 0), (0, 0), (0, 64))), jnp.pad(face_lift, ((0, 0), (0, 0), (64, 0)))], 1
    ).reshape(FACES * 128, 128)
    block_parts, lift_parts, right = call(
        prep_kernel,
        [
            jax.ShapeDtypeStruct((ELEMS * NODES, 256), BF16),
            jax.ShapeDtypeStruct((FACES * 128, 384), BF16),
            tiles(ELEMS),
        ],
        [],
        [VMEM] * 3,
    )(matrices, lift, right_side)
    own_scratch = [pltpu.VMEM((FACES, ELEMS + 1, 8, 128), F32)]
    ghost_scratch = [pltpu.VMEM((FACES, 2 * GHOST + 1, 8, 128), F32)]
    own = call(first_own_kernel, [tiles(ELEMS)], own_scratch, [SMEM] * 2 + [VMEM] * 3)(
        near, scale, guess, block_parts, lift_parts
    )[0]
    first, to_prev, to_next = call(
        first_ghost_kernel, [tiles(ELEMS)] + sent, ghost_scratch, [SMEM] * 3 + [VMEM] * 6
    )(near, scale, send, own, from_prev, from_next, lift_parts, right, guess)
    vector = first
    grams, stacks = [], []
    for index in range(STEPS):
        from_prev, from_next = exchange(to_prev, to_next)
        rows = 16 * (index + 1)
        stack_shape = jax.ShapeDtypeStruct((rows, ELEMS * NODES), BF16)
        own, gram, *stacks = call(
            functools.partial(own_kernel, index),
            [tiles(ELEMS), jax.ShapeDtypeStruct((16, rows), F32), stack_shape, stack_shape],
            own_scratch,
            [SMEM] * 2 + [VMEM] * (3 + len(stacks)),
        )(near, scale, vector, block_parts, lift_parts, *stacks)
        grams.append(gram)
        if index < STEPS - 1:
            vector, to_prev, to_next = call(
                ghost_kernel, [tiles(ELEMS)] + sent, ghost_scratch, [SMEM] * 3 + [VMEM] * 4
            )(near, scale, send, own, from_prev, from_next, lift_parts)
    rows = 16 * (STEPS + 1)
    stack_shape = jax.ShapeDtypeStruct((rows, ELEMS * NODES), BF16)
    high, low, packed = call(
        last_kernel,
        [stack_shape, stack_shape, jax.ShapeDtypeStruct((32, 128), F32)],
        ghost_scratch + [pltpu.VMEM((ELEMS, 8, 128), F32), pltpu.VMEM((16, rows), F32)],
        [SMEM] * 2 + [VMEM] * 10,
    )(near, scale, own, from_prev, from_next, lift_parts, *stacks, *grams)
    packed = spread(packed, axes[2]).sum(0)
    packed = spread(packed, axes[0]).sum(0)
    packed = spread(packed, axes[1])
    result = jax.ShapeDtypeStruct((ELEMS, RHS * NODES), F32)
    return tuple(
        call(
            solve_kernel,
            [result, result],
            [pltpu.VMEM((128, 128), F32), pltpu.VMEM((2, ELEMS, 8, 128), F32)],
            [VMEM] * 5,
        )(packed, high, low, first, start_guess)
    )


def solution(mesh):
    wide, narrow = mesh.devices.shape
    inner = 16 if wide % 16 == 0 else 2
    axes = ("outer", "inner", "narrow")
    split_mesh = Mesh(mesh.devices.reshape(wide // inner, inner, narrow), axes)
    rows = P(axes, None)
    return jax.shard_map(
        functools.partial(local, axes=axes),
        mesh=split_mesh,
        in_specs=(rows, rows, rows, P(), rows, rows, rows),
        out_specs=(rows, rows),
        check_vma=False,
    )
```

```python
import functools

import jax
import jax.numpy as jnp
from jax import lax
from jax.experimental import pallas as pl
from jax.experimental.pallas import tpu as pltpu
from jax.sharding import Mesh, PartitionSpec as P

STEPS = 4
GAIN = 1.5
RHS = 16
NODES = 64
FACES = 6
ELEMS = 32
GHOST = 4
F32 = jnp.float32
BF16 = jnp.bfloat16


VMEM = pl.BlockSpec(memory_space=pltpu.VMEM)
SMEM = pl.BlockSpec(memory_space=pltpu.SMEM)
HBM = pl.BlockSpec(memory_space=pltpu.HBM)
PARAMS = pltpu.CompilerParams(vmem_limit_bytes=32 * 1024 * 1024)


def tiles(count):
    return jax.ShapeDtypeStruct((count, 8, 128), F32)


def dot_nt(left, right):
    return lax.dot_general(left, right, (((1,), (1,)), ((), ())), preferred_element_type=F32)


def split(value):
    high = value.astype(BF16)
    low = (value - high.astype(F32)).astype(BF16)
    return high, low


def swap(value):
    return pltpu.roll(value, 64, 1)


def left_half(shape):
    return lax.broadcasted_iota(jnp.int32, shape, len(shape) - 1) < 64


def to_tiles(ref, out):
    for t in range(8):
        out[:, t, :] = ref[:, t * 128 : (t + 1) * 128]


def sides():
    odd = lax.rem(lax.axis_index("narrow"), 2)
    return GHOST * (1 - odd), GHOST * odd


def send_rows(send, source, to_other, to_pair):
    pair, other = sides()
    for k in range(GHOST):
        to_other[k] = source[send[0, other + k]]
        to_pair[k] = source[send[0, pair + k]]


def pack_kernel(
    send_in, guess_in, near_in, scale_in, tiled, to_other, to_pair, send_out, near_out, scale_out,
    send, guess, done,
):
    pairs = [
        (guess_in, guess),
        (send_in, send),
        (send_in, send_out),
        (near_in, near_out),
        (scale_in, scale_out),
    ]
    copies = [pltpu.make_async_copy(a, b, done.at[i]) for i, (a, b) in enumerate(pairs)]
    for copy in copies:
        copy.start()
    copies[0].wait()
    to_tiles(guess, tiled)
    copies[1].wait()
    send_rows(send, tiled, to_other, to_pair)
    for copy in copies[2:]:
        copy.wait()


def prep_kernel(
    blocks_in, lift_in, right_in, block_parts, lift_parts, right_tiled,
    blocks, lift, right, spread_blocks, done,
):
    pairs = [(lift_in, lift), (right_in, right), (blocks_in, blocks)]
    copies = [pltpu.make_async_copy(a, b, done.at[i]) for i, (a, b) in enumerate(pairs)]
    for copy in copies:
        copy.start()
    copies[0].wait()
    for f in range(FACES):
        upper = jnp.concatenate([lift[f], jnp.zeros((NODES, NODES), F32)], 1)
        high, low = split(jnp.concatenate([upper, swap(upper)], 0))
        rows = slice(f * 128, f * 128 + 128)
        lift_parts[rows, :128] = high
        lift_parts[rows, 128:256] = high
        lift_parts[rows, 256:] = low
    copies[1].wait()
    to_tiles(right, right_tiled)
    copies[2].wait()
    mask = left_half((ELEMS, 128))
    for pair in range(NODES // 2):
        two = blocks[:, pair * 128 : pair * 128 + 128]
        turned = swap(two)
        spread_blocks[:, 2 * pair, :] = jnp.where(mask, two, turned)
        spread_blocks[:, 2 * pair + 1, :] = jnp.where(mask, turned, two)
    for element in range(ELEMS):
        high, low = split(spread_blocks[element])
        rows = slice(element * NODES, (element + 1) * NODES)
        block_parts[rows, :128] = high
        block_parts[rows, 128:] = low


def lifted(vector, lift_parts):
    high, low = split(vector)
    return dot_nt(jnp.concatenate([high, low, high], 1), lift_parts[...])


def gather_faces(total, element, neighbors, scale, source, place):
    for f in range(FACES):
        total = total + scale[f, element] * source[f, place(neighbors[f, element])]
    return total


def dense(vector):
    upper, lower = [], []
    mask = left_half((8, 128))
    for pair in range(ELEMS // 2):
        first, second = vector[2 * pair], vector[2 * pair + 1]
        upper.append(jnp.where(mask, first, swap(second)))
        lower.append(jnp.where(mask, swap(first), second))
    return jnp.concatenate([jnp.concatenate(upper, 1), jnp.concatenate(lower, 1)], 0)


def own_part(vector, block_parts, lift_parts, neighbors, scale, out, own_lifted):
    value = vector[...].reshape(ELEMS * 8, 128)
    product = lifted(value, lift_parts)
    for f in range(FACES):
        own_lifted[f, :ELEMS] = product[:, f * 128 : (f + 1) * 128].reshape(ELEMS, 8, 128)
        own_lifted[f, ELEMS] = jnp.zeros((8, 128), F32)
    mask = left_half((ELEMS * 8, 128))
    high, low = split(value)
    high, low = high.astype(F32), low.astype(F32)
    turned_high, turned_low = swap(high), swap(low)
    first = jnp.where(mask, low, turned_high).astype(BF16)
    second = jnp.where(mask, turned_low, high).astype(BF16)
    first_rest = jnp.where(mask, high, 0.0).astype(BF16)
    second_rest = jnp.where(mask, 0.0, high).astype(BF16)
    first = jnp.concatenate([first, first_rest], 1)
    second = jnp.concatenate([second, second_rest], 1)
    mask = left_half((8, 128))
    for group in range(ELEMS // 4):
        rows = slice(group * 32, (group + 1) * 32)
        both = jnp.concatenate([first[rows], second[rows]], 0)
        result = dot_nt(both, block_parts[group * 256 : (group + 1) * 256, :])
        for part in range(4):
            lanes = slice((part // 2) * 128, (part // 2) * 128 + 128)
            top = result[part * 8 : part * 8 + 8, lanes]
            bottom = result[32 + part * 8 : 40 + part * 8, lanes]
            if part % 2 == 0:
                total = jnp.where(mask, top, swap(bottom))
            else:
                total = jnp.where(mask, swap(top), bottom)
            element = group * 4 + part
            out[element] = gather_faces(
                total, element, neighbors, scale, own_lifted, lambda n: jnp.minimum(n, ELEMS)
            )


def gram_rows(stack_high, stack_low, newest, count):
    high, low = split(newest)
    left = jnp.concatenate([high, high, low], 1)
    right = jnp.concatenate([stack_high, stack_low, stack_high], 1)
    return dot_nt(left, right)


def first_own_kernel(neighbors, scale, vector, block_parts, lift_parts, out, own_lifted):
    own_part(vector, block_parts, lift_parts, neighbors, scale, out, own_lifted)


def own_kernel(index, neighbors, scale, vector, block_parts, lift_parts, *rest):
    if index:
        old_high, old_low, out, gram, high_out, low_out, own_lifted = rest
    else:
        out, gram, high_out, low_out, own_lifted = rest
    own_part(vector, block_parts, lift_parts, neighbors, scale, out, own_lifted)
    new_gram(index, vector, old_high if index else None, old_low if index else None, gram, high_out, low_out)


def new_gram(index, vector, old_high, old_low, gram, high_out, low_out):
    newest = dense(vector)
    high, low = split(newest)
    if index:
        high_out[: 16 * index] = old_high[...]
        low_out[: 16 * index] = old_low[...]
    high_out[16 * index :] = high
    low_out[16 * index :] = low
    gram[...] = gram_rows(high_out[...], low_out[...], newest, index + 1)


def ghost_total(own, from_other, from_pair, lift_parts, neighbors, scale, ghost_lifted):
    ghosts = jnp.concatenate([from_other[...], from_pair[...]], 0).reshape(2 * GHOST * 8, 128)
    product = lifted(ghosts, lift_parts)
    pair, other = sides()
    for f in range(FACES):
        both = product[:, f * 128 : (f + 1) * 128].reshape(2 * GHOST, 8, 128)
        ghost_lifted[f, pl.ds(other, GHOST)] = both[:GHOST]
        ghost_lifted[f, pl.ds(pair, GHOST)] = both[GHOST:]
        ghost_lifted[f, 2 * GHOST] = jnp.zeros((8, 128), F32)
    place = lambda n: jnp.where(n >= ELEMS, n - ELEMS, 2 * GHOST)
    for element in range(ELEMS):
        yield element, gather_faces(own[element], element, neighbors, scale, ghost_lifted, place)


def first_ghost_kernel(
    neighbors, scale, send, own, from_other, from_pair, lift_parts, right, guess,
    out, to_other, to_pair, ghost_lifted,
):
    for element, total in ghost_total(own, from_other, from_pair, lift_parts, neighbors, scale, ghost_lifted):
        out[element] = right[element] - (guess[element] + total)
    send_rows(send, out, to_other, to_pair)


def ghost_kernel(
    neighbors, scale, send, own, from_other, from_pair, lift_parts,
    out, to_other, to_pair, ghost_lifted,
):
    for element, total in ghost_total(own, from_other, from_pair, lift_parts, neighbors, scale, ghost_lifted):
        out[element] = GAIN * total
    send_rows(send, out, to_other, to_pair)


def last_kernel(
    neighbors, scale, own, from_other, from_pair, lift_parts, old_high, old_low,
    gram0, gram1, gram2, gram3, high_out, low_out, packed, ghost_lifted, newest, gram4,
):
    for element, total in ghost_total(own, from_other, from_pair, lift_parts, neighbors, scale, ghost_lifted):
        newest[element] = GAIN * total
    new_gram(STEPS, newest, old_high, old_low, gram4, high_out, low_out)
    packed[0:16] = jnp.concatenate([gram4[...], gram1[...], gram0[...]], 1)
    packed[16:32] = jnp.concatenate([gram3[...], gram2[...], jnp.zeros((16, 16), F32)], 1)


def solve_spd(system):
    size, block = 64, 8
    row_id = lax.broadcasted_iota(jnp.int32, (size, 128), 0)
    for start in range(0, size, block):
        columns = [jnp.broadcast_to(system[:, start + j : start + j + 1], (size, 128)) for j in range(block)]
        rows = [system[start + i : start + i + 1, :] for i in range(block)]
        pivots = [[columns[j][start + i : start + i + 1, :] for j in range(block)] for i in range(block)]
        for j in range(block):
            inverse = 1.0 / pivots[j][j]
            rows[j] = rows[j] * inverse
            for l in range(j + 1, block):
                pivots[j][l] = pivots[j][l] * inverse
            for i in range(block):
                if i != j:
                    factor = pivots[i][j]
                    rows[i] = rows[i] - factor * rows[j]
                    for l in range(j + 1, block):
                        pivots[i][l] = pivots[i][l] - factor * pivots[j][l]
        update = system
        for j in range(block):
            update = update - columns[j] * rows[j]
        for j in range(block):
            update = jnp.where(row_id == start + j, rows[j], update)
        system = update
    return system


def solve_kernel(packed, high, low, first, guess, solution, residual, gram_low, tiled):
    total = jnp.sum(packed[...], 0)
    upper, lower = total[:16], total[16:]
    lane = lax.broadcasted_iota(jnp.int32, (16, 128), 1)
    pieces = [
        (pltpu.roll(upper, 16, 1), 16),
        (pltpu.roll(upper, 48, 1), 32),
        (pltpu.roll(lower, 64, 1), 48),
        (lower, 64),
        (upper, 80),
    ]
    for a, (piece, width) in enumerate(pieces):
        gram_low[16 * a : 16 * a + 16, :] = jnp.where(lane < width, piece, 0.0)
    gram_low[80:, :] = jnp.zeros((48, 128), F32)
    lower_part = gram_low[...]
    row = lax.broadcasted_iota(jnp.int32, (128, 128), 0) // 16
    column = lax.broadcasted_iota(jnp.int32, (128, 128), 1) // 16
    gram = jnp.where(row >= column, lower_part, lower_part.T)
    weighted = gram[:64] + gram[16:80] * (1.0 / GAIN)
    lane = lax.broadcasted_iota(jnp.int32, (64, 128), 1)
    normal = weighted + pltpu.roll(weighted, 112, 1) * (1.0 / GAIN)
    system = jnp.where(lane < 64, normal, pltpu.roll(weighted, 64, 1))
    system = jnp.where(lane < 80, system, 0.0)
    coeffs = pltpu.roll(solve_spd(system), 64, 1)
    empty = jnp.zeros((16, 128), F32)
    padded = jnp.concatenate([coeffs, empty], 0)
    mixed = padded + jnp.concatenate([empty, coeffs], 0) * (1.0 / GAIN)
    lane = lax.broadcasted_iota(jnp.int32, (80, 128), 1)
    both = jnp.where(lane < 16, padded, pltpu.roll(mixed, 16, 1))
    both = jnp.where(lane < 32, both, 0.0)
    both = jnp.concatenate([both, jnp.zeros((48, 128), F32)], 0).T[:32]
    mask_high, mask_low = split(both)
    change = jnp.dot(mask_high[:, :80], high[...], preferred_element_type=F32)
    change = change + jnp.dot(mask_high[:, :80], low[...], preferred_element_type=F32)
    change = change + jnp.dot(mask_low[:, :80], high[...], preferred_element_type=F32)
    mask = left_half((8, 128))
    for pair in range(ELEMS // 2):
        lanes = slice(pair * 128, pair * 128 + 128)
        top, bottom = change[0:8, lanes], change[8:16, lanes]
        tiled[0, 2 * pair] = jnp.where(mask, top, swap(bottom))
        tiled[0, 2 * pair + 1] = jnp.where(mask, swap(top), bottom)
        top, bottom = change[16:24, lanes], change[24:32, lanes]
        tiled[1, 2 * pair] = first[2 * pair] - jnp.where(mask, top, swap(bottom))
        tiled[1, 2 * pair + 1] = first[2 * pair + 1] - jnp.where(mask, swap(top), bottom)
    for t in range(8):
        lanes = slice(t * 128, t * 128 + 128)
        solution[:, lanes] = guess[:, lanes] + tiled[0, :, t, :]
        residual[:, lanes] = tiled[1, :, t, :]


def call(kernel, outs, scratch, specs, limit=32 * 1024, cost=None):
    return pl.pallas_call(
        kernel,
        out_shape=outs,
        in_specs=specs,
        out_specs=[VMEM] * len(outs),
        scratch_shapes=scratch,
        compiler_params=pltpu.CompilerParams(vmem_limit_bytes=limit * 1024),
        cost_estimate=cost,
    )


def swapped(block, axes, first):
    lower = range(first, lax.axis_size(axes) - 1, 2)
    return lax.ppermute(block, axes, [(i, i + 1) for i in lower] + [(i + 1, i) for i in lower])


def spread(value, axis):
    count = lax.axis_size(axis)
    return lax.all_to_all(jnp.broadcast_to(value[None], (count,) + value.shape), axis, 0, 0)


def local(right_side, start_guess, block_diag, face_lift, face_scale, neighbors, ghost_send, axes):
    sent = [tiles(GHOST), tiles(GHOST)]
    guess, to_other, to_pair, send, near, scale = call(
        pack_kernel,
        [tiles(ELEMS)]
        + sent
        + [
            jax.ShapeDtypeStruct((1, 2 * GHOST), jnp.int32),
            jax.ShapeDtypeStruct((FACES, ELEMS), jnp.int32),
            jax.ShapeDtypeStruct((FACES, ELEMS), F32),
        ],
        [
            pltpu.SMEM((1, 2 * GHOST), jnp.int32),
            pltpu.VMEM((ELEMS, RHS * NODES), F32),
            pltpu.SemaphoreType.DMA((5,)),
        ],
        [HBM] * 4,
        64512,
        pl.CostEstimate(flops=0, bytes_accessed=16_000_000, transcendentals=0),
    )(ghost_send, start_guess, neighbors.T, face_scale.T)

    def exchange(to_other, to_pair):
        from_other = swapped(to_other, axes, 1)
        return from_other, swapped(to_pair, axes, 0)

    from_other, from_pair = exchange(to_other, to_pair)
    block_parts, lift_parts, right = call(
        prep_kernel,
        [
            jax.ShapeDtypeStruct((ELEMS * NODES, 256), BF16),
            jax.ShapeDtypeStruct((FACES * 128, 384), BF16),
            tiles(ELEMS),
        ],
        [
            pltpu.VMEM((ELEMS, NODES * NODES), F32),
            pltpu.VMEM((FACES, NODES, NODES), F32),
            pltpu.VMEM((ELEMS, RHS * NODES), F32),
            pltpu.VMEM((ELEMS, NODES, 128), F32),
            pltpu.SemaphoreType.DMA((3,)),
        ],
        [HBM] * 3,
    )(block_diag, face_lift, right_side)
    own_scratch = [pltpu.VMEM((FACES, ELEMS + 1, 8, 128), F32)]
    ghost_scratch = [pltpu.VMEM((FACES, 2 * GHOST + 1, 8, 128), F32)]
    own = call(first_own_kernel, [tiles(ELEMS)], own_scratch, [SMEM] * 2 + [VMEM] * 3)(
        near, scale, guess, block_parts, lift_parts
    )[0]
    first, to_other, to_pair = call(
        first_ghost_kernel, [tiles(ELEMS)] + sent, ghost_scratch, [SMEM] * 3 + [VMEM] * 6
    )(near, scale, send, own, from_other, from_pair, lift_parts, right, guess)
    vector = first
    grams, stacks = [], []
    for index in range(STEPS):
        from_other, from_pair = exchange(to_other, to_pair)
        rows = 16 * (index + 1)
        stack_shape = jax.ShapeDtypeStruct((rows, ELEMS * NODES), BF16)
        own, gram, *stacks = call(
            functools.partial(own_kernel, index),
            [tiles(ELEMS), jax.ShapeDtypeStruct((16, rows), F32), stack_shape, stack_shape],
            own_scratch,
            [SMEM] * 2 + [VMEM] * (3 + len(stacks)),
        )(near, scale, vector, block_parts, lift_parts, *stacks)
        grams.append(gram)
        if index < STEPS - 1:
            vector, to_other, to_pair = call(
                ghost_kernel, [tiles(ELEMS)] + sent, ghost_scratch, [SMEM] * 3 + [VMEM] * 4
            )(near, scale, send, own, from_other, from_pair, lift_parts)
    rows = 16 * (STEPS + 1)
    stack_shape = jax.ShapeDtypeStruct((rows, ELEMS * NODES), BF16)
    high, low, packed = call(
        last_kernel,
        [stack_shape, stack_shape, jax.ShapeDtypeStruct((32, 128), F32)],
        ghost_scratch + [pltpu.VMEM((ELEMS, 8, 128), F32), pltpu.VMEM((16, rows), F32)],
        [SMEM] * 2 + [VMEM] * 10,
    )(near, scale, own, from_other, from_pair, lift_parts, *stacks, *grams)
    packed = spread(packed, (axes[0], axes[2])).sum(0)
    packed = spread(packed, axes[1])
    result = jax.ShapeDtypeStruct((ELEMS, RHS * NODES), F32)
    return tuple(
        call(
            solve_kernel,
            [result, result],
            [pltpu.VMEM((128, 128), F32), pltpu.VMEM((2, ELEMS, 8, 128), F32)],
            [VMEM] * 5,
        )(packed, high, low, first, start_guess)
    )


def solution(mesh):
    wide, narrow = mesh.devices.shape
    inner = 16 if wide % 16 == 0 else 2
    axes = ("outer", "inner", "narrow")
    split_mesh = Mesh(mesh.devices.reshape(wide // inner, inner, narrow), axes)
    rows = P(axes, None)
    return jax.shard_map(
        functools.partial(local, axes=axes),
        mesh=split_mesh,
        in_specs=(rows, rows, rows, P(), rows, rows, rows),
        out_specs=(rows, rows),
        check_vma=False,
    )
```

```python
import functools

import jax
import jax.numpy as jnp
from jax import lax
from jax.experimental import pallas as pl
from jax.experimental.pallas import tpu as pltpu
from jax.sharding import Mesh, PartitionSpec as P

STEPS = 4
GAIN = 1.5
RHS = 16
NODES = 64
FACES = 6
ELEMS = 32
GHOST = 4
F32 = jnp.float32
BF16 = jnp.bfloat16

OWN, FROM, SEND = (0, 576), (640, 784), (896, 992)

VMEM = pl.BlockSpec(memory_space=pltpu.VMEM)
HBM = pl.BlockSpec(memory_space=pltpu.HBM)


WIDTH = RHS * NODES
FIELD = jax.ShapeDtypeStruct((ELEMS, WIDTH), F32)


def dot_nt(left, right):
    return lax.dot_general(left, right, (((1,), (1,)), ((), ())), preferred_element_type=F32)


def split(value):
    high = value.astype(BF16)
    low = (value - high.astype(F32)).astype(BF16)
    return high, low


def swap(value):
    return pltpu.roll(value, 64, 1)


def left_half(shape):
    return lax.broadcasted_iota(jnp.int32, shape, len(shape) - 1) < 64


def slab(t):
    return slice(t * 128, t * 128 + 128)


def to_tiles(ref, out):
    for t in range(8):
        out[:, t, :] = ref[:, slab(t)]


def selection(near, scale, first, count):
    columns = []
    for f in range(FACES):
        place = first(lax.broadcasted_iota(jnp.int32, (count, ELEMS), 0))
        columns.append(jnp.where(place == near[f : f + 1, :], scale[f : f + 1, :], 0.0))
    chosen = jnp.concatenate(columns, 0)
    high = chosen.astype(BF16).astype(F32)
    return jnp.concatenate([high, high, chosen - high], 0).T


def pack_kernel(
    send_in, guess_in, near_in, scale_in, to_other, to_pair, choose,
    guess, near, scale, send_row, send, done,
):
    pairs = [(send_in, send), (guess_in, guess), (near_in, near), (scale_in, scale), (send_in, send_row)]
    copies = [pltpu.make_async_copy(a, b, done.at[i]) for i, (a, b) in enumerate(pairs)]
    for copy in copies:
        copy.start()
    for copy in copies:
        copy.wait()
    odd = lax.rem(lax.axis_index("narrow"), 2)
    for k in range(GHOST):
        to_other[k : k + 1, :] = guess[pl.ds(send[0, GHOST * odd + k], 1), :]
        to_pair[k : k + 1, :] = guess[pl.ds(send[0, GHOST * (1 - odd) + k], 1), :]
    choose[...] = jnp.zeros((ELEMS, 1024), BF16)
    choose[:, OWN[0] : OWN[1]] = selection(near, scale, lambda n: n, ELEMS).astype(BF16)
    ghosts = lambda m: ELEMS + lax.rem(m + GHOST * odd, 2 * GHOST)
    choose[:, FROM[0] : FROM[1]] = selection(near, scale, ghosts, 2 * GHOST).astype(BF16)
    row = send_row[...]
    row = jnp.where(odd == 1, jnp.concatenate([row[:, GHOST:], row[:, :GHOST]], 1), row)
    rows = (lax.broadcasted_iota(jnp.int32, (ELEMS, 2 * GHOST), 0) == row).astype(F32)
    rows = jnp.concatenate([rows, jnp.zeros((ELEMS, ELEMS - 2 * GHOST), F32)], 1)
    choose[:, SEND[0] : SEND[1]] = jnp.concatenate([rows, rows, rows], 0).T.astype(BF16)


def prep_kernel(blocks, lift, block_parts, lift_parts, spread_blocks):
    for f in range(FACES):
        upper = jnp.concatenate([lift[f], jnp.zeros((NODES, NODES), F32)], 1)
        high, low = split(jnp.concatenate([upper, swap(upper)], 0))
        rows = slice(f * 128, f * 128 + 128)
        lift_parts[rows, :128] = high
        lift_parts[rows, 128:256] = high
        lift_parts[rows, 256:] = low
    mask = left_half((ELEMS, 128))
    for pair in range(NODES // 2):
        two = blocks[:, pair * 128 : pair * 128 + 128]
        turned = swap(two)
        spread_blocks[:, 2 * pair, :] = jnp.where(mask, two, turned)
        spread_blocks[:, 2 * pair + 1, :] = jnp.where(mask, turned, two)
    for element in range(ELEMS):
        high, low = split(spread_blocks[element])
        rows = slice(element * NODES, (element + 1) * NODES)
        block_parts[rows, :128] = high
        block_parts[rows, 128:] = low


def face_sum(vector, lift_parts, choose, lanes):
    count = vector.shape[0]
    rows = jnp.concatenate([vector[:, slab(t)] for t in range(8)], 0)
    high, low = split(rows)
    moved = dot_nt(jnp.concatenate([high, low, high], 1), lift_parts[...])
    moved = jnp.concatenate(
        [
            jnp.concatenate([moved[t * count : (t + 1) * count, slab(f)] for t in range(8)], 1)
            for f in range(FACES)
        ],
        0,
    )
    high, low = split(moved)
    parts = jnp.concatenate([high, low, high], 0)
    return jnp.dot(choose[:, lanes[0] : lanes[1]], parts, preferred_element_type=F32)


def send_rows(vector, choose, to_other, to_pair):
    high = vector.astype(BF16)
    rest = vector - high.astype(F32)
    middle, low = split(rest)
    parts = jnp.concatenate([high, middle, low], 0)
    rows = jnp.dot(choose[:16, SEND[0] : SEND[1]], parts, preferred_element_type=F32)
    to_other[...] = rows[:GHOST]
    to_pair[...] = rows[GHOST : 2 * GHOST]


def dense(vector):
    upper, lower = [], []
    mask = left_half((8, 128))
    for pair in range(ELEMS // 2):
        first, second = vector[2 * pair], vector[2 * pair + 1]
        upper.append(jnp.where(mask, first, swap(second)))
        lower.append(jnp.where(mask, swap(first), second))
    return jnp.concatenate([jnp.concatenate(upper, 1), jnp.concatenate(lower, 1)], 0)


def own_part(vector, block_parts, lift_parts, choose, out, tiled, product):
    to_tiles(vector, tiled)
    value = tiled[...].reshape(ELEMS * 8, 128)
    mask = left_half((ELEMS * 8, 128))
    high, low = split(value)
    high, low = high.astype(F32), low.astype(F32)
    turned_high, turned_low = swap(high), swap(low)
    first = jnp.where(mask, low, turned_high).astype(BF16)
    second = jnp.where(mask, turned_low, high).astype(BF16)
    first_rest = jnp.where(mask, high, 0.0).astype(BF16)
    second_rest = jnp.where(mask, 0.0, high).astype(BF16)
    first = jnp.concatenate([first, first_rest], 1)
    second = jnp.concatenate([second, second_rest], 1)
    mask = left_half((8, 128))
    for group in range(ELEMS // 4):
        rows = slice(group * 32, (group + 1) * 32)
        both = jnp.concatenate([first[rows], second[rows]], 0)
        result = dot_nt(both, block_parts[group * 256 : (group + 1) * 256, :])
        for part in range(4):
            lanes = slab(part // 2)
            top = result[part * 8 : part * 8 + 8, lanes]
            bottom = result[32 + part * 8 : 40 + part * 8, lanes]
            if part % 2 == 0:
                product[group * 4 + part] = jnp.where(mask, top, swap(bottom))
            else:
                product[group * 4 + part] = jnp.where(mask, swap(top), bottom)
    faces = face_sum(vector[...], lift_parts, choose, OWN)
    for t in range(8):
        out[:, slab(t)] = faces[:, slab(t)] + product[:, t, :]


def gram_rows(stack_high, stack_low, newest, count):
    high, low = split(newest)
    left = jnp.concatenate([high, high, low], 1)
    right = jnp.concatenate([stack_high, stack_low, stack_high], 1)
    return dot_nt(left, right)


def first_own_kernel(choose, vector, block_parts, lift_parts, out, tiled, product):
    own_part(vector, block_parts, lift_parts, choose, out, tiled, product)


def own_kernel(index, choose, vector, block_parts, lift_parts, *rest):
    old_high, old_low = rest[:2] if index else (None, None)
    out, gram, high_out, low_out, tiled, product = rest[-6:]
    own_part(vector, block_parts, lift_parts, choose, out, tiled, product)
    new_gram(index, tiled, old_high, old_low, gram, high_out, low_out)


def new_gram(index, tiled, old_high, old_low, gram, high_out, low_out):
    newest = dense(tiled)
    high, low = split(newest)
    if index:
        high_out[: 16 * index] = old_high[...]
        low_out[: 16 * index] = old_low[...]
    high_out[16 * index :] = high
    low_out[16 * index :] = low
    gram[...] = gram_rows(high_out[...], low_out[...], newest, index + 1)


def ghost_part(from_other, from_pair, lift_parts, choose):
    ghosts = jnp.concatenate([from_other[...], from_pair[...]], 0)
    return face_sum(ghosts, lift_parts, choose, FROM)


def first_ghost_kernel(choose, own, from_other, from_pair, lift_parts, right, guess, out, to_other, to_pair):
    total = own[...] + ghost_part(from_other, from_pair, lift_parts, choose)
    vector = right[...] - (guess[...] + total)
    out[...] = vector
    send_rows(vector, choose, to_other, to_pair)


def ghost_kernel(choose, own, from_other, from_pair, lift_parts, out, to_other, to_pair):
    vector = GAIN * (own[...] + ghost_part(from_other, from_pair, lift_parts, choose))
    out[...] = vector
    send_rows(vector, choose, to_other, to_pair)


def last_kernel(
    choose, own, from_other, from_pair, lift_parts, old_high, old_low,
    gram0, gram1, gram2, gram3, high_out, low_out, packed, newest, tiled, gram4,
):
    newest[...] = GAIN * (own[...] + ghost_part(from_other, from_pair, lift_parts, choose))
    to_tiles(newest, tiled)
    new_gram(STEPS, tiled, old_high, old_low, gram4, high_out, low_out)
    packed[0:16] = jnp.concatenate([gram4[...], gram1[...], gram0[...]], 1)
    packed[16:32] = jnp.concatenate([gram3[...], gram2[...], jnp.zeros((16, 16), F32)], 1)


def solve_spd(system):
    size, block = 64, 8
    row_id = lax.broadcasted_iota(jnp.int32, (size, 128), 0)
    for start in range(0, size, block):
        columns = [jnp.broadcast_to(system[:, start + j : start + j + 1], (size, 128)) for j in range(block)]
        rows = [system[start + i : start + i + 1, :] for i in range(block)]
        pivots = [[columns[j][start + i : start + i + 1, :] for j in range(block)] for i in range(block)]
        for j in range(block):
            inverse = 1.0 / pivots[j][j]
            rows[j] = rows[j] * inverse
            for l in range(j + 1, block):
                pivots[j][l] = pivots[j][l] * inverse
            for i in range(block):
                if i != j:
                    factor = pivots[i][j]
                    rows[i] = rows[i] - factor * rows[j]
                    for l in range(j + 1, block):
                        pivots[i][l] = pivots[i][l] - factor * pivots[j][l]
        update = system
        for j in range(block):
            update = update - columns[j] * rows[j]
        for j in range(block):
            update = jnp.where(row_id == start + j, rows[j], update)
        system = update
    return system


def solve_kernel(packed, high, low, first, guess, solution, residual, gram_low, tiled):
    total = jnp.sum(packed[...], 0)
    upper, lower = total[:16], total[16:]
    lane = lax.broadcasted_iota(jnp.int32, (16, 128), 1)
    pieces = [
        (pltpu.roll(upper, 16, 1), 16),
        (pltpu.roll(upper, 48, 1), 32),
        (pltpu.roll(lower, 64, 1), 48),
        (lower, 64),
        (upper, 80),
    ]
    for a, (piece, width) in enumerate(pieces):
        gram_low[16 * a : 16 * a + 16, :] = jnp.where(lane < width, piece, 0.0)
    gram_low[80:, :] = jnp.zeros((48, 128), F32)
    lower_part = gram_low[...]
    row = lax.broadcasted_iota(jnp.int32, (128, 128), 0) // 16
    column = lax.broadcasted_iota(jnp.int32, (128, 128), 1) // 16
    gram = jnp.where(row >= column, lower_part, lower_part.T)
    weighted = gram[:64] + gram[16:80] * (1.0 / GAIN)
    lane = lax.broadcasted_iota(jnp.int32, (64, 128), 1)
    normal = weighted + pltpu.roll(weighted, 112, 1) * (1.0 / GAIN)
    system = jnp.where(lane < 64, normal, pltpu.roll(weighted, 64, 1))
    system = jnp.where(lane < 80, system, 0.0)
    coeffs = pltpu.roll(solve_spd(system), 64, 1)
    empty = jnp.zeros((16, 128), F32)
    padded = jnp.concatenate([coeffs, empty], 0)
    mixed = padded + jnp.concatenate([empty, coeffs], 0) * (1.0 / GAIN)
    lane = lax.broadcasted_iota(jnp.int32, (80, 128), 1)
    both = jnp.where(lane < 16, padded, pltpu.roll(mixed, 16, 1))
    both = jnp.where(lane < 32, both, 0.0)
    both = jnp.concatenate([both, jnp.zeros((48, 128), F32)], 0).T[:32]
    mask_high, mask_low = split(both)
    change = jnp.dot(mask_high[:, :80], high[...], preferred_element_type=F32)
    change = change + jnp.dot(mask_high[:, :80], low[...], preferred_element_type=F32)
    change = change + jnp.dot(mask_low[:, :80], high[...], preferred_element_type=F32)
    mask = left_half((8, 128))
    for pair in range(ELEMS // 2):
        lanes = slice(pair * 128, pair * 128 + 128)
        top, bottom = change[0:8, lanes], change[8:16, lanes]
        tiled[0, 2 * pair] = jnp.where(mask, top, swap(bottom))
        tiled[0, 2 * pair + 1] = jnp.where(mask, swap(top), bottom)
        top, bottom = change[16:24, lanes], change[24:32, lanes]
        tiled[1, 2 * pair] = jnp.where(mask, top, swap(bottom))
        tiled[1, 2 * pair + 1] = jnp.where(mask, swap(top), bottom)
    for t in range(8):
        lanes = slice(t * 128, t * 128 + 128)
        solution[:, lanes] = guess[:, lanes] + tiled[0, :, t, :]
        residual[:, lanes] = first[:, lanes] - tiled[1, :, t, :]


def call(kernel, outs, scratch, specs, limit=32 * 1024):
    return pl.pallas_call(
        kernel,
        out_shape=outs,
        in_specs=specs,
        out_specs=[VMEM] * len(outs),
        scratch_shapes=scratch,
        compiler_params=pltpu.CompilerParams(vmem_limit_bytes=limit * 1024),
    )


def swapped(block, axes, first):
    lower = range(first, lax.axis_size(axes) - 1, 2)
    return lax.ppermute(block, axes, [(i, i + 1) for i in lower] + [(i + 1, i) for i in lower])


def spread(value, axis):
    count = lax.axis_size(axis)
    return lax.all_to_all(jnp.broadcast_to(value[None], (count,) + value.shape), axis, 0, 0)


def local(right_side, start_guess, block_diag, face_lift, face_scale, neighbors, ghost_send, axes):
    sent = [jax.ShapeDtypeStruct((GHOST, WIDTH), F32)] * 2
    to_other, to_pair, choose = call(
        pack_kernel,
        sent + [jax.ShapeDtypeStruct((ELEMS, 1024), BF16)],
        [
            pltpu.VMEM((ELEMS, WIDTH), F32),
            pltpu.VMEM((FACES, ELEMS), jnp.int32),
            pltpu.VMEM((FACES, ELEMS), F32),
            pltpu.VMEM((1, 2 * GHOST), jnp.int32),
            pltpu.SMEM((1, 2 * GHOST), jnp.int32),
            pltpu.SemaphoreType.DMA((5,)),
        ],
        [HBM] * 4,
        60 * 1024,
    )(ghost_send, start_guess, neighbors.T, face_scale.T)

    def exchange(to_other, to_pair):
        from_other = swapped(to_other, axes, 1)
        return from_other, swapped(to_pair, axes, 0)

    from_other, from_pair = exchange(to_other, to_pair)
    block_parts, lift_parts = call(
        prep_kernel,
        [
            jax.ShapeDtypeStruct((ELEMS * NODES, 256), BF16),
            jax.ShapeDtypeStruct((FACES * 128, 384), BF16),
        ],
        [pltpu.VMEM((ELEMS, NODES, 128), F32)],
        [VMEM] * 2,
    )(block_diag, face_lift)
    tile_scratch = pltpu.VMEM((ELEMS, 8, 128), F32)
    own = call(first_own_kernel, [FIELD], [tile_scratch] * 2, [VMEM] * 4)(
        choose, start_guess, block_parts, lift_parts
    )[0]
    first, to_other, to_pair = call(first_ghost_kernel, [FIELD] + sent, [], [VMEM] * 7)(
        choose, own, from_other, from_pair, lift_parts, right_side, start_guess
    )
    vector = first
    grams, stacks = [], []
    for index in range(STEPS):
        from_other, from_pair = exchange(to_other, to_pair)
        rows = 16 * (index + 1)
        stack_shape = jax.ShapeDtypeStruct((rows, ELEMS * NODES), BF16)
        own, gram, *stacks = call(
            functools.partial(own_kernel, index),
            [FIELD, jax.ShapeDtypeStruct((16, rows), F32), stack_shape, stack_shape],
            [tile_scratch] * 2,
            [VMEM] * (4 + len(stacks)),
        )(choose, vector, block_parts, lift_parts, *stacks)
        grams.append(gram)
        if index < STEPS - 1:
            vector, to_other, to_pair = call(ghost_kernel, [FIELD] + sent, [], [VMEM] * 5)(
                choose, own, from_other, from_pair, lift_parts
            )
    rows = 16 * (STEPS + 1)
    stack_shape = jax.ShapeDtypeStruct((rows, ELEMS * NODES), BF16)
    high, low, packed = call(
        last_kernel,
        [stack_shape, stack_shape, jax.ShapeDtypeStruct((32, 128), F32)],
        [pltpu.VMEM((ELEMS, WIDTH), F32), tile_scratch, pltpu.VMEM((16, rows), F32)],
        [VMEM] * 11,
    )(choose, own, from_other, from_pair, lift_parts, *stacks, *grams)
    packed = spread(packed, (axes[0], axes[2])).sum(0)
    packed = spread(packed, axes[1])
    return tuple(
        call(
            solve_kernel,
            [FIELD, FIELD],
            [pltpu.VMEM((128, 128), F32), pltpu.VMEM((2, ELEMS, 8, 128), F32)],
            [VMEM] * 5,
        )(packed, high, low, first, start_guess)
    )


def solution(mesh):
    wide, narrow = mesh.devices.shape
    inner = 16 if wide % 16 == 0 else 2
    axes = ("outer", "inner", "narrow")
    split_mesh = Mesh(mesh.devices.reshape(wide // inner, inner, narrow), axes)
    rows = P(axes, None)
    return jax.shard_map(
        functools.partial(local, axes=axes),
        mesh=split_mesh,
        in_specs=(rows, rows, rows, P(), rows, rows, rows),
        out_specs=(rows, rows),
        check_vma=False,
    )
```

```python
import functools

import jax
import jax.numpy as jnp
from jax import lax
from jax.experimental import pallas as pl
from jax.experimental.pallas import tpu as pltpu
from jax.sharding import Mesh, PartitionSpec as P

STEPS = 4
GAIN = 1.5
RHS = 16
NODES = 64
FACES = 6
ELEMS = 32
GHOST = 4
F32 = jnp.float32
BF16 = jnp.bfloat16

OWN, FROM, SEND = (0, 576), (640, 784), (896, 992)

VMEM = pl.BlockSpec(memory_space=pltpu.VMEM)
HBM = pl.BlockSpec(memory_space=pltpu.HBM)


WIDTH = RHS * NODES
FIELD = jax.ShapeDtypeStruct((ELEMS, WIDTH), F32)


def dot_nt(left, right):
    return lax.dot_general(left, right, (((1,), (1,)), ((), ())), preferred_element_type=F32)


def split(value):
    high = value.astype(BF16)
    low = (value - high.astype(F32)).astype(BF16)
    return high, low


def swap(value):
    return pltpu.roll(value, 64, 1)


def left_half(shape):
    return lax.broadcasted_iota(jnp.int32, shape, len(shape) - 1) < 64


def slab(t):
    return slice(t * 128, t * 128 + 128)


def to_tiles(ref, out):
    for t in range(8):
        out[:, t, :] = ref[:, slab(t)]


def selection(near, scale, first, count):
    columns = []
    for f in range(FACES):
        place = first(lax.broadcasted_iota(jnp.int32, (count, ELEMS), 0))
        columns.append(jnp.where(place == near[f : f + 1, :], scale[f : f + 1, :], 0.0))
    return jnp.concatenate(columns, 0)


def three_parts(chosen, axis):
    high = chosen.astype(BF16).astype(F32)
    return jnp.concatenate([high, high, chosen - high], axis)


def pack_kernel(
    send_in, guess_in, near_in, scale_in, to_other, to_pair, choose,
    guess, near, scale, send_row, terms, send, done,
):
    pairs = [(send_in, send), (guess_in, guess), (near_in, near), (scale_in, scale), (send_in, send_row)]
    copies = [pltpu.make_async_copy(a, b, done.at[i]) for i, (a, b) in enumerate(pairs)]
    for copy in copies:
        copy.start()
    for copy in copies:
        copy.wait()
    odd = lax.rem(lax.axis_index("narrow"), 2)
    choose[...] = jnp.zeros((ELEMS, 1024), BF16)
    own = selection(near, scale, lambda n: n, ELEMS)
    choose[:, OWN[0] : OWN[1]] = three_parts(own, 0).T.astype(BF16)
    ghosts = selection(near, scale, lambda m: ELEMS + lax.rem(m + GHOST * odd, 2 * GHOST), 2 * GHOST)
    choose[:, FROM[0] : FROM[1]] = three_parts(ghosts, 0).T.astype(BF16)
    terms[...] = jnp.zeros((ELEMS, 128), F32)
    terms[:, : FACES * 2 * GHOST] = ghosts.T
    to_other[GHOST:, :] = jnp.zeros((GHOST, WIDTH), F32)
    for k in range(GHOST):
        row = send[0, GHOST * odd + k]
        to_other[k : k + 1, :] = guess[pl.ds(row, 1), :]
        to_other[GHOST + k : GHOST + k + 1, :128] = terms[pl.ds(row, 1), :]
        to_pair[k : k + 1, :] = guess[pl.ds(send[0, GHOST * (1 - odd) + k], 1), :]
    row = send_row[...]
    row = jnp.where(odd == 1, jnp.concatenate([row[:, GHOST:], row[:, :GHOST]], 1), row)
    rows = (lax.broadcasted_iota(jnp.int32, (ELEMS, 2 * GHOST), 0) == row).astype(F32)
    rows = jnp.concatenate([rows, jnp.zeros((ELEMS, ELEMS - 2 * GHOST), F32)], 1)
    choose[:, SEND[0] : SEND[1]] = jnp.concatenate([rows, rows, rows], 0).T.astype(BF16)


def prep_kernel(blocks, lift, block_parts, lift_parts, spread_blocks):
    for f in range(FACES):
        upper = jnp.concatenate([lift[f], jnp.zeros((NODES, NODES), F32)], 1)
        high, low = split(jnp.concatenate([upper, swap(upper)], 0))
        rows = slice(f * 128, f * 128 + 128)
        lift_parts[rows, :128] = high
        lift_parts[rows, 128:256] = high
        lift_parts[rows, 256:] = low
    mask = left_half((ELEMS, 128))
    for pair in range(NODES // 2):
        two = blocks[:, pair * 128 : pair * 128 + 128]
        turned = swap(two)
        spread_blocks[:, 2 * pair, :] = jnp.where(mask, two, turned)
        spread_blocks[:, 2 * pair + 1, :] = jnp.where(mask, turned, two)
    for element in range(ELEMS):
        high, low = split(spread_blocks[element])
        rows = slice(element * NODES, (element + 1) * NODES)
        block_parts[rows, :128] = high
        block_parts[rows, 128:] = low


def face_sum(vector, lift_parts, chosen):
    count = vector.shape[0]
    rows = jnp.concatenate([vector[:, slab(t)] for t in range(8)], 0)
    high, low = split(rows)
    moved = dot_nt(jnp.concatenate([high, low, high], 1), lift_parts[...])
    moved = jnp.concatenate(
        [
            jnp.concatenate([moved[t * count : (t + 1) * count, slab(f)] for t in range(8)], 1)
            for f in range(FACES)
        ],
        0,
    )
    high, low = split(moved)
    parts = jnp.concatenate([high, low, high], 0)
    return jnp.dot(chosen, parts, preferred_element_type=F32)


def from_sides(choose, lift_parts, other=None, pair=None):
    empty = jnp.zeros((GHOST, WIDTH), F32)
    ghosts = jnp.concatenate([empty if other is None else other, empty if pair is None else pair], 0)
    return face_sum(ghosts, lift_parts, choose[:, FROM[0] : FROM[1]])


def sent_rows(vector, choose):
    high = vector.astype(BF16)
    rest = vector - high.astype(F32)
    middle, low = split(rest)
    parts = jnp.concatenate([high, middle, low], 0)
    rows = jnp.dot(choose[:16, SEND[0] : SEND[1]], parts, preferred_element_type=F32)
    return rows[:GHOST], rows[GHOST : 2 * GHOST]


def dense(vector):
    upper, lower = [], []
    mask = left_half((8, 128))
    for pair in range(ELEMS // 2):
        first, second = vector[2 * pair], vector[2 * pair + 1]
        upper.append(jnp.where(mask, first, swap(second)))
        lower.append(jnp.where(mask, swap(first), second))
    return jnp.concatenate([jnp.concatenate(upper, 1), jnp.concatenate(lower, 1)], 0)


def own_part(vector, block_parts, lift_parts, choose, out, tiled, product, other=None):
    to_tiles(vector, tiled)
    value = tiled[...].reshape(ELEMS * 8, 128)
    mask = left_half((ELEMS * 8, 128))
    high, low = split(value)
    high, low = high.astype(F32), low.astype(F32)
    turned_high, turned_low = swap(high), swap(low)
    first = jnp.where(mask, low, turned_high).astype(BF16)
    second = jnp.where(mask, turned_low, high).astype(BF16)
    first_rest = jnp.where(mask, high, 0.0).astype(BF16)
    second_rest = jnp.where(mask, 0.0, high).astype(BF16)
    first = jnp.concatenate([first, first_rest], 1)
    second = jnp.concatenate([second, second_rest], 1)
    mask = left_half((8, 128))
    for group in range(ELEMS // 4):
        rows = slice(group * 32, (group + 1) * 32)
        both = jnp.concatenate([first[rows], second[rows]], 0)
        result = dot_nt(both, block_parts[group * 256 : (group + 1) * 256, :])
        for part in range(4):
            lanes = slab(part // 2)
            top = result[part * 8 : part * 8 + 8, lanes]
            bottom = result[32 + part * 8 : 40 + part * 8, lanes]
            if part % 2 == 0:
                product[group * 4 + part] = jnp.where(mask, top, swap(bottom))
            else:
                product[group * 4 + part] = jnp.where(mask, swap(top), bottom)
    faces = face_sum(vector[...], lift_parts, choose[:, OWN[0] : OWN[1]])
    if other is not None:
        faces = faces + from_sides(choose, lift_parts, other=other[...])
    for t in range(8):
        out[:, slab(t)] = faces[:, slab(t)] + product[:, t, :]


def gram_of(left_high, left_low, high, low):
    left = jnp.concatenate([left_high, left_high, left_low], 1)
    return dot_nt(left, jnp.concatenate([high, low, high], 1))


def first_own_kernel(choose, vector, block_parts, lift_parts, out, tiled, product):
    own_part(vector, block_parts, lift_parts, choose, out, tiled, product)


def second_own_kernel(choose, vector, block_parts, lift_parts, other, out, tiled, product):
    own_part(vector, block_parts, lift_parts, choose, out, tiled, product, other)


def dense_own_kernel(
    choose, vector, block_parts, lift_parts, other, out, high_out, low_out, tiled, product
):
    own_part(vector, block_parts, lift_parts, choose, out, tiled, product, other)
    high_out[...], low_out[...] = split(dense(tiled))


def first_ghost_kernel(
    choose, own, from_other, from_pair, lift_parts, right, guess, out, to_other, to_pair, terms
):
    faces = from_sides(choose, lift_parts, from_other[:GHOST], from_pair[...])
    vector = right[...] - (guess[...] + (own[...] + faces))
    out[...] = vector
    to_other[...], to_pair[...] = sent_rows(vector, choose)
    partner = three_parts(from_other[GHOST:, : FACES * 2 * GHOST], 1)
    terms[...] = jnp.concatenate([partner, jnp.zeros((16 - GHOST, partner.shape[1]), F32)], 0).astype(BF16)


def pair_kernel(choose, own, from_pair, lift_parts, to_other, partial, message):
    total = own[...] + from_sides(choose, lift_parts, pair=from_pair[...])
    partial[...] = total
    message[:GHOST] = to_other[...]
    message[GHOST:] = sent_rows(GAIN * total, choose)[0]


def missing_terms(terms, lift_parts, to_other, missing):
    rows = jnp.concatenate([to_other[...], jnp.zeros((GHOST, WIDTH), F32)], 0)
    missing[...] = GAIN * face_sum(rows, lift_parts, terms[...])[:GHOST]


def flight_kernel(terms, lift_parts, to_other, missing):
    missing_terms(terms, lift_parts, to_other, missing)


def gram_flight_kernel(
    terms, lift_parts, to_other, first, second, third, missing, high, low, gram, tiled
):
    missing_terms(terms, lift_parts, to_other, missing)
    for a, vector in enumerate((first, second, third)):
        to_tiles(vector, tiled)
        high[16 * a : 16 * a + 16], low[16 * a : 16 * a + 16] = split(dense(tiled))
    gram[...] = gram_of(high[...], low[...], high[...], low[...])


def other_kernel(choose, partial, message, missing, lift_parts, out, to_pair, next_other):
    faces = from_sides(choose, lift_parts, other=message[:GHOST])
    vector = GAIN * (partial[...] + faces)
    out[...] = vector
    to_pair[...] = sent_rows(vector, choose)[1]
    next_other[...] = message[GHOST:] + missing[...]


def second_pair_kernel(choose, own, from_pair, lift_parts, out, to_other, to_pair):
    vector = GAIN * (own[...] + from_sides(choose, lift_parts, pair=from_pair[...]))
    out[...] = vector
    to_other[...], to_pair[...] = sent_rows(vector, choose)


def last_kernel(
    choose, own, from_pair, lift_parts, high, low, high3, low3, gram, high4, low4, packed, newest, tiled,
):
    newest[...] = GAIN * (own[...] + from_sides(choose, lift_parts, pair=from_pair[...]))
    to_tiles(newest, tiled)
    high4[...], low4[...] = split(dense(tiled))
    left_high = jnp.concatenate([high3[...], high4[...]], 0)
    left_low = jnp.concatenate([low3[...], low4[...]], 0)
    rows = gram_of(
        left_high,
        left_low,
        jnp.concatenate([high[...], left_high], 0),
        jnp.concatenate([low[...], left_low], 0),
    )
    packed[0:16] = jnp.concatenate([rows[16:], gram[16:32, :32], gram[:16, :16]], 1)
    packed[16:32] = jnp.concatenate([rows[:16, :64], gram[32:, :], jnp.zeros((16, 16), F32)], 1)


def solve_spd(system):
    size, block = 64, 8
    row_id = lax.broadcasted_iota(jnp.int32, (size, 128), 0)
    for start in range(0, size, block):
        columns = [jnp.broadcast_to(system[:, start + j : start + j + 1], (size, 128)) for j in range(block)]
        rows = [system[start + i : start + i + 1, :] for i in range(block)]
        pivots = [[columns[j][start + i : start + i + 1, :] for j in range(block)] for i in range(block)]
        for j in range(block):
            inverse = 1.0 / pivots[j][j]
            rows[j] = rows[j] * inverse
            for l in range(j + 1, block):
                pivots[j][l] = pivots[j][l] * inverse
            for i in range(block):
                if i != j:
                    factor = pivots[i][j]
                    rows[i] = rows[i] - factor * rows[j]
                    for l in range(j + 1, block):
                        pivots[i][l] = pivots[i][l] - factor * pivots[j][l]
        update = system
        for j in range(block):
            update = update - columns[j] * rows[j]
        for j in range(block):
            update = jnp.where(row_id == start + j, rows[j], update)
        system = update
    return system


def solve_kernel(
    mine, theirs, high, low, high3, low3, high4, low4, first, guess,
    solution, residual, gram_low, tiled,
):
    high = jnp.concatenate([high[...], high3[...], high4[...]], 0)
    low = jnp.concatenate([low[...], low3[...], low4[...]], 0)
    odd = lax.rem(lax.axis_index("narrow"), 2) == 1
    upper = jnp.where(odd, theirs[...], mine[...])
    lower = jnp.where(odd, mine[...], theirs[...])
    lane = lax.broadcasted_iota(jnp.int32, (16, 128), 1)
    pieces = [
        (pltpu.roll(upper, 16, 1), 16),
        (pltpu.roll(upper, 48, 1), 32),
        (pltpu.roll(lower, 64, 1), 48),
        (lower, 64),
        (upper, 80),
    ]
    for a, (piece, width) in enumerate(pieces):
        gram_low[16 * a : 16 * a + 16, :] = jnp.where(lane < width, piece, 0.0)
    gram_low[80:, :] = jnp.zeros((48, 128), F32)
    lower_part = gram_low[...]
    row = lax.broadcasted_iota(jnp.int32, (128, 128), 0) // 16
    column = lax.broadcasted_iota(jnp.int32, (128, 128), 1) // 16
    gram = jnp.where(row >= column, lower_part, lower_part.T)
    weighted = gram[:64] + gram[16:80] * (1.0 / GAIN)
    lane = lax.broadcasted_iota(jnp.int32, (64, 128), 1)
    normal = weighted + pltpu.roll(weighted, 112, 1) * (1.0 / GAIN)
    system = jnp.where(lane < 64, normal, pltpu.roll(weighted, 64, 1))
    system = jnp.where(lane < 80, system, 0.0)
    coeffs = pltpu.roll(solve_spd(system), 64, 1)
    empty = jnp.zeros((16, 128), F32)
    padded = jnp.concatenate([coeffs, empty], 0)
    mixed = padded + jnp.concatenate([empty, coeffs], 0) * (1.0 / GAIN)
    lane = lax.broadcasted_iota(jnp.int32, (80, 128), 1)
    both = jnp.where(lane < 16, padded, pltpu.roll(mixed, 16, 1))
    both = jnp.where(lane < 32, both, 0.0)
    both = jnp.concatenate([both, jnp.zeros((48, 128), F32)], 0).T[:32]
    mask_high, mask_low = split(both)
    change = jnp.dot(mask_high[:, :80], high, preferred_element_type=F32)
    change = change + jnp.dot(mask_high[:, :80], low, preferred_element_type=F32)
    change = change + jnp.dot(mask_low[:, :80], high, preferred_element_type=F32)
    mask = left_half((8, 128))
    for pair in range(ELEMS // 2):
        lanes = slice(pair * 128, pair * 128 + 128)
        top, bottom = change[0:8, lanes], change[8:16, lanes]
        tiled[0, 2 * pair] = jnp.where(mask, top, swap(bottom))
        tiled[0, 2 * pair + 1] = jnp.where(mask, swap(top), bottom)
        top, bottom = change[16:24, lanes], change[24:32, lanes]
        tiled[1, 2 * pair] = jnp.where(mask, top, swap(bottom))
        tiled[1, 2 * pair + 1] = jnp.where(mask, swap(top), bottom)
    for t in range(8):
        lanes = slice(t * 128, t * 128 + 128)
        solution[:, lanes] = guess[:, lanes] + tiled[0, :, t, :]
        residual[:, lanes] = first[:, lanes] - tiled[1, :, t, :]


def call(kernel, outs, scratch, specs, limit=32 * 1024):
    return pl.pallas_call(
        kernel,
        out_shape=outs,
        in_specs=specs,
        out_specs=[VMEM] * len(outs),
        scratch_shapes=scratch,
        compiler_params=pltpu.CompilerParams(vmem_limit_bytes=limit * 1024),
    )


def swapped(block, axes, first):
    lower = range(first, lax.axis_size(axes) - 1, 2)
    return lax.ppermute(block, axes, [(i, i + 1) for i in lower] + [(i + 1, i) for i in lower])


def local(right_side, start_guess, block_diag, face_lift, face_scale, neighbors, ghost_send, axes):
    sent = jax.ShapeDtypeStruct((GHOST, WIDTH), F32)
    message = jax.ShapeDtypeStruct((2 * GHOST, WIDTH), F32)
    to_other, to_pair, choose = call(
        pack_kernel,
        [message, sent, jax.ShapeDtypeStruct((ELEMS, 1024), BF16)],
        [
            pltpu.VMEM((ELEMS, WIDTH), F32),
            pltpu.VMEM((FACES, ELEMS), jnp.int32),
            pltpu.VMEM((FACES, ELEMS), F32),
            pltpu.VMEM((1, 2 * GHOST), jnp.int32),
            pltpu.VMEM((ELEMS, 128), F32),
            pltpu.SMEM((1, 2 * GHOST), jnp.int32),
            pltpu.SemaphoreType.DMA((5,)),
        ],
        [HBM] * 4,
        60 * 1024,
    )(ghost_send, start_guess, neighbors.T, face_scale.T)
    from_other = swapped(to_other, axes, 1)
    from_pair = swapped(to_pair, axes, 0)
    block_parts, lift_parts = call(
        prep_kernel,
        [
            jax.ShapeDtypeStruct((ELEMS * NODES, 256), BF16),
            jax.ShapeDtypeStruct((FACES * 128, 384), BF16),
        ],
        [pltpu.VMEM((ELEMS, NODES, 128), F32)],
        [VMEM] * 2,
    )(block_diag, face_lift)
    tile_scratch = pltpu.VMEM((ELEMS, 8, 128), F32)
    own_call = lambda *args: call(
        first_own_kernel, [FIELD], [tile_scratch] * 2, [VMEM] * 4
    )(*args)[0]
    own = own_call(choose, start_guess, block_parts, lift_parts)
    basis = []
    vector, to_other, to_pair, terms = call(
        first_ghost_kernel,
        [FIELD, sent, sent, jax.ShapeDtypeStruct((16, 3 * FACES * 2 * GHOST), BF16)],
        [],
        [VMEM] * 7,
    )(choose, own, from_other, from_pair, lift_parts, right_side, start_guess)
    basis.append(vector)
    stack = lambda rows: jax.ShapeDtypeStruct((rows, ELEMS * NODES), BF16)
    for half in range(2):
        from_pair = swapped(to_pair, axes, 0)
        own = own_call(choose, vector, block_parts, lift_parts)
        partial, outgoing = call(pair_kernel, [FIELD, message], [], [VMEM] * 5)(
            choose, own, from_pair, lift_parts, to_other
        )
        incoming = swapped(outgoing, axes, 1)
        if half == 0:
            missing = call(flight_kernel, [sent], [], [VMEM] * 3)(terms, lift_parts, to_other)[0]
        else:
            missing, high, low, gram = call(
                gram_flight_kernel,
                [sent, stack(48), stack(48), jax.ShapeDtypeStruct((48, 48), F32)],
                [tile_scratch],
                [VMEM] * 6,
            )(terms, lift_parts, to_other, *basis)
        vector, to_pair, next_other = call(other_kernel, [FIELD, sent, sent], [], [VMEM] * 5)(
            choose, partial, incoming, missing, lift_parts
        )
        basis.append(vector)
        from_pair = swapped(to_pair, axes, 0)
        if half == 0:
            own = call(second_own_kernel, [FIELD], [tile_scratch] * 2, [VMEM] * 5)(
                choose, vector, block_parts, lift_parts, next_other
            )[0]
            vector, to_other, to_pair = call(second_pair_kernel, [FIELD, sent, sent], [], [VMEM] * 4)(
                choose, own, from_pair, lift_parts
            )
            basis.append(vector)
        else:
            own, high3, low3 = call(
                dense_own_kernel, [FIELD, stack(16), stack(16)], [tile_scratch] * 2, [VMEM] * 5
            )(choose, vector, block_parts, lift_parts, next_other)
    high4, low4, packed = call(
        last_kernel,
        [stack(16), stack(16), jax.ShapeDtypeStruct((32, 128), F32)],
        [pltpu.VMEM((ELEMS, WIDTH), F32), tile_scratch],
        [VMEM] * 9,
    )(choose, own, from_pair, lift_parts, high, low, high3, low3, gram)
    outer, inner, narrow = (lax.axis_size(axis) for axis in axes)
    halves = jnp.broadcast_to(packed.reshape(1, 2, 16, 128), (outer * narrow // 2, 2, 16, 128))
    halves = halves.reshape(outer * narrow, 16, 128)
    mine = lax.all_to_all(halves, (axes[0], axes[2]), 0, 0).sum(0)
    mine = jnp.broadcast_to(mine[None], (inner, 16, 128))
    mine = lax.all_to_all(mine, axes[1], 0, 0).sum(0)
    theirs = swapped(mine, axes, 0)
    return tuple(
        call(
            solve_kernel,
            [FIELD, FIELD],
            [pltpu.VMEM((128, 128), F32), pltpu.VMEM((2, ELEMS, 8, 128), F32)],
            [VMEM] * 10,
        )(mine, theirs, high, low, high3, low3, high4, low4, basis[0], start_guess)
    )


def solution(mesh):
    wide, narrow = mesh.devices.shape
    inner = 16 if wide % 16 == 0 else 2
    axes = ("outer", "inner", "narrow")
    split_mesh = Mesh(mesh.devices.reshape(wide // inner, inner, narrow), axes)
    rows = P(axes, None)
    return jax.shard_map(
        functools.partial(local, axes=axes),
        mesh=split_mesh,
        in_specs=(rows, rows, rows, P(), rows, rows, rows),
        out_specs=(rows, rows),
        check_vma=False,
    )
```

```python
import functools

import jax
import jax.numpy as jnp
from jax import lax
from jax.experimental import pallas as pl
from jax.experimental.pallas import tpu as pltpu
from jax.sharding import Mesh, PartitionSpec as P

STEPS = 4
GAIN = 1.5
RHS = 16
NODES = 64
FACES = 6
ELEMS = 32
GHOST = 4
F32 = jnp.float32
BF16 = jnp.bfloat16

OWN, FROM, SEND = (0, 576), (640, 784), (896, 992)

VMEM = pl.BlockSpec(memory_space=pltpu.VMEM)
HBM = pl.BlockSpec(memory_space=pltpu.HBM)


WIDTH = RHS * NODES
FIELD = jax.ShapeDtypeStruct((ELEMS, WIDTH), F32)


def dot_nt(left, right):
    return lax.dot_general(left, right, (((1,), (1,)), ((), ())), preferred_element_type=F32)


def split(value):
    high = value.astype(BF16)
    low = (value - high.astype(F32)).astype(BF16)
    return high, low


def swap(value):
    return pltpu.roll(value, 64, 1)


def left_half(shape):
    return lax.broadcasted_iota(jnp.int32, shape, len(shape) - 1) < 64


def slab(t):
    return slice(t * 128, t * 128 + 128)


def to_tiles(ref, out):
    for t in range(8):
        out[:, t, :] = ref[:, slab(t)]


def selection(near, scale, first, count):
    columns = []
    for f in range(FACES):
        place = first(lax.broadcasted_iota(jnp.int32, (count, ELEMS), 0))
        columns.append(jnp.where(place == near[f : f + 1, :], scale[f : f + 1, :], 0.0))
    return jnp.concatenate(columns, 0)


def three_parts(chosen, axis):
    high = chosen.astype(BF16).astype(F32)
    return jnp.concatenate([high, high, chosen - high], axis)


def pack_kernel(
    send_in, guess_in, near_in, scale_in, to_other, to_pair, choose,
    guess, near, scale, send_row, terms, send, done,
):
    pairs = [(send_in, send), (guess_in, guess), (near_in, near), (scale_in, scale), (send_in, send_row)]
    copies = [pltpu.make_async_copy(a, b, done.at[i]) for i, (a, b) in enumerate(pairs)]
    for copy in copies:
        copy.start()
    for copy in copies:
        copy.wait()
    odd = lax.rem(lax.axis_index("narrow"), 2)
    choose[...] = jnp.zeros((ELEMS, 1024), BF16)
    own = selection(near, scale, lambda n: n, ELEMS)
    choose[:, OWN[0] : OWN[1]] = three_parts(own, 0).T.astype(BF16)
    ghosts = selection(near, scale, lambda m: ELEMS + lax.rem(m + GHOST * odd, 2 * GHOST), 2 * GHOST)
    choose[:, FROM[0] : FROM[1]] = three_parts(ghosts, 0).T.astype(BF16)
    terms[...] = jnp.zeros((ELEMS, 128), F32)
    terms[:, : FACES * 2 * GHOST] = ghosts.T
    to_other[GHOST:, :] = jnp.zeros((GHOST, WIDTH), F32)
    for k in range(GHOST):
        row = send[0, GHOST * odd + k]
        to_other[k : k + 1, :] = guess[pl.ds(row, 1), :]
        to_other[GHOST + k : GHOST + k + 1, :128] = terms[pl.ds(row, 1), :]
        to_pair[k : k + 1, :] = guess[pl.ds(send[0, GHOST * (1 - odd) + k], 1), :]
    row = send_row[...]
    row = jnp.where(odd == 1, jnp.concatenate([row[:, GHOST:], row[:, :GHOST]], 1), row)
    rows = (lax.broadcasted_iota(jnp.int32, (ELEMS, 2 * GHOST), 0) == row).astype(F32)
    rows = jnp.concatenate([rows, jnp.zeros((ELEMS, ELEMS - 2 * GHOST), F32)], 1)
    choose[:, SEND[0] : SEND[1]] = jnp.concatenate([rows, rows, rows], 0).T.astype(BF16)


def prep_kernel(blocks, lift, block_parts, lift_parts, spread_blocks):
    for f in range(FACES):
        upper = jnp.concatenate([lift[f], jnp.zeros((NODES, NODES), F32)], 1)
        high, low = split(jnp.concatenate([upper, swap(upper)], 0).T)
        lift_parts[:128, slab(f)] = high
        lift_parts[128:256, slab(f)] = high
        lift_parts[256:, slab(f)] = low
    mask = left_half((ELEMS, 128))
    for pair in range(NODES // 2):
        two = blocks[:, pair * 128 : pair * 128 + 128]
        turned = swap(two)
        spread_blocks[:, 2 * pair, :] = jnp.where(mask, two, turned)
        spread_blocks[:, 2 * pair + 1, :] = jnp.where(mask, turned, two)
    for element in range(ELEMS):
        high, low = split(spread_blocks[element])
        rows = slice(element * NODES, (element + 1) * NODES)
        block_parts[rows, :128] = high
        block_parts[rows, 128:] = low


def face_sum(vector, lift_parts, chosen):
    count = vector.shape[0]
    rows = jnp.concatenate([vector[:, slab(t)] for t in range(8)], 0)
    high, low = split(rows)
    both = jnp.concatenate([high, low, high], 1)
    moved = jnp.dot(both, lift_parts[...], preferred_element_type=F32)
    moved = jnp.concatenate(
        [
            jnp.concatenate([moved[t * count : (t + 1) * count, slab(f)] for t in range(8)], 1)
            for f in range(FACES)
        ],
        0,
    )
    high, low = split(moved)
    parts = jnp.concatenate([high, low, high], 0)
    return jnp.dot(chosen, parts, preferred_element_type=F32)


def from_sides(choose, lift_parts, other=None, pair=None):
    empty = jnp.zeros((GHOST, WIDTH), F32)
    ghosts = jnp.concatenate([empty if other is None else other, empty if pair is None else pair], 0)
    return face_sum(ghosts, lift_parts, choose[:, FROM[0] : FROM[1]])


def sent_rows(vector, choose):
    high = vector.astype(BF16)
    rest = vector - high.astype(F32)
    middle, low = split(rest)
    parts = jnp.concatenate([high, middle, low], 0)
    rows = jnp.dot(choose[:16, SEND[0] : SEND[1]], parts, preferred_element_type=F32)
    return rows[:GHOST], rows[GHOST : 2 * GHOST]


def dense(vector):
    upper, lower = [], []
    mask = left_half((8, 128))
    for pair in range(ELEMS // 2):
        first, second = vector[2 * pair], vector[2 * pair + 1]
        upper.append(jnp.where(mask, first, swap(second)))
        lower.append(jnp.where(mask, swap(first), second))
    return jnp.concatenate([jnp.concatenate(upper, 1), jnp.concatenate(lower, 1)], 0)


def own_part(vector, block_parts, lift_parts, choose, out, tiled, product):
    to_tiles(vector, tiled)
    value = tiled[...].reshape(ELEMS * 8, 128)
    mask = left_half((ELEMS * 8, 128))
    high, low = split(value)
    high, low = high.astype(F32), low.astype(F32)
    turned_high, turned_low = swap(high), swap(low)
    first = jnp.where(mask, low, turned_high).astype(BF16)
    second = jnp.where(mask, turned_low, high).astype(BF16)
    first_rest = jnp.where(mask, high, 0.0).astype(BF16)
    second_rest = jnp.where(mask, 0.0, high).astype(BF16)
    first = jnp.concatenate([first, first_rest], 1)
    second = jnp.concatenate([second, second_rest], 1)
    mask = left_half((8, 128))
    for group in range(ELEMS // 4):
        rows = slice(group * 32, (group + 1) * 32)
        both = jnp.concatenate([first[rows], second[rows]], 0)
        result = dot_nt(both, block_parts[group * 256 : (group + 1) * 256, :])
        for part in range(4):
            lanes = slab(part // 2)
            top = result[part * 8 : part * 8 + 8, lanes]
            bottom = result[32 + part * 8 : 40 + part * 8, lanes]
            if part % 2 == 0:
                product[group * 4 + part] = jnp.where(mask, top, swap(bottom))
            else:
                product[group * 4 + part] = jnp.where(mask, swap(top), bottom)
    faces = face_sum(vector[...], lift_parts, choose[:, OWN[0] : OWN[1]])
    for t in range(8):
        out[:, slab(t)] = faces[:, slab(t)] + product[:, t, :]


def gram_of(left_high, left_low, high, low):
    left = jnp.concatenate([left_high, left_high, left_low], 1)
    return dot_nt(left, jnp.concatenate([high, low, high], 1))


def first_own_kernel(choose, vector, block_parts, lift_parts, out, tiled, product):
    own_part(vector, block_parts, lift_parts, choose, out, tiled, product)


def dense_own_kernel(
    choose, vector, block_parts, lift_parts, out, high_out, low_out, tiled, product
):
    own_part(vector, block_parts, lift_parts, choose, out, tiled, product)
    high_out[...], low_out[...] = split(dense(tiled))


def first_ghost_kernel(
    choose, own, from_other, from_pair, lift_parts, right, guess, out, to_other, to_pair, terms
):
    faces = from_sides(choose, lift_parts, from_other[:GHOST], from_pair[...])
    vector = right[...] - (guess[...] + (own[...] + faces))
    out[...] = vector
    to_other[...], to_pair[...] = sent_rows(vector, choose)
    partner = three_parts(from_other[GHOST:, : FACES * 2 * GHOST], 1)
    terms[...] = jnp.concatenate([partner, jnp.zeros((16 - GHOST, partner.shape[1]), F32)], 0).astype(BF16)


def pair_kernel(choose, own, from_pair, lift_parts, to_other, partial, message):
    total = own[...] + from_sides(choose, lift_parts, pair=from_pair[...])
    partial[...] = total
    message[:GHOST] = to_other[...]
    message[GHOST:] = sent_rows(GAIN * total, choose)[0]


def missing_terms(terms, lift_parts, to_other, missing):
    rows = jnp.concatenate([to_other[...], jnp.zeros((GHOST, WIDTH), F32)], 0)
    missing[...] = GAIN * face_sum(rows, lift_parts, terms[...])[:GHOST]


def flight_kernel(terms, lift_parts, to_other, missing):
    missing_terms(terms, lift_parts, to_other, missing)


def gram_flight_kernel(
    terms, lift_parts, to_other, first, second, third, missing, high, low, gram, tiled
):
    missing_terms(terms, lift_parts, to_other, missing)
    for a, vector in enumerate((first, second, third)):
        to_tiles(vector, tiled)
        high[16 * a : 16 * a + 16], low[16 * a : 16 * a + 16] = split(dense(tiled))
    gram[...] = gram_of(high[...], low[...], high[...], low[...])


def other_kernel(choose, partial, message, missing, lift_parts, out, to_pair, next_other):
    faces = from_sides(choose, lift_parts, other=message[:GHOST])
    vector = GAIN * (partial[...] + faces)
    out[...] = vector
    to_pair[...] = sent_rows(vector, choose)[1]
    next_other[...] = message[GHOST:] + missing[...]


def both_kernel(choose, own, from_other, from_pair, lift_parts, out, to_other, to_pair):
    vector = GAIN * (own[...] + from_sides(choose, lift_parts, from_other[...], from_pair[...]))
    out[...] = vector
    to_other[...], to_pair[...] = sent_rows(vector, choose)


def last_kernel(
    choose, own, from_other, from_pair, lift_parts, high, low, high3, low3, gram, high4, low4, packed, newest, tiled,
):
    newest[...] = GAIN * (own[...] + from_sides(choose, lift_parts, from_other[...], from_pair[...]))
    to_tiles(newest, tiled)
    high4[...], low4[...] = split(dense(tiled))
    left_high = jnp.concatenate([high3[...], high4[...]], 0)
    left_low = jnp.concatenate([low3[...], low4[...]], 0)
    rows = gram_of(
        left_high,
        left_low,
        jnp.concatenate([high[...], left_high], 0),
        jnp.concatenate([low[...], left_low], 0),
    )
    packed[0:16] = jnp.concatenate([rows[16:], gram[16:32, :32], gram[:16, :16]], 1)
    packed[16:32] = jnp.concatenate([rows[:16, :64], gram[32:, :], jnp.zeros((16, 16), F32)], 1)


def solve_spd(system):
    size, block = 64, 16
    row_id = lax.broadcasted_iota(jnp.int32, (block, 128), 0)
    for start in range(0, size, block):
        stop = start + block
        columns = [jnp.broadcast_to(system[:, start + j : start + j + 1], (size, 128)) for j in range(block)]
        pivots = [column[start:stop, :] for column in columns]
        rows = system[start:stop, :]
        for j in range(block):
            here = row_id == j
            inverse = 1.0 / pivots[j][j : j + 1, :]
            factor = pivots[j]
            for l in range(j + 1, block):
                scaled = pivots[l][j : j + 1, :] * inverse
                pivots[l] = jnp.where(here, scaled, pivots[l] - factor * scaled)
            scaled = rows[j : j + 1, :] * inverse
            rows = jnp.where(here, scaled, rows - factor * scaled)
        terms = [columns[j] * rows[j : j + 1, :] for j in range(block)]
        while len(terms) > 1:
            terms = [a + b for a, b in zip(terms[::2], terms[1::2])]
        update = system - terms[0]
        parts = [update[:start], rows, update[stop:]]
        system = jnp.concatenate([part for part in parts if part.shape[0]], 0)
    return system


def solve_kernel(
    mine, theirs, high, low, high3, low3, high4, low4, first, guess,
    solution, residual, gram_low, tiled,
):
    high = jnp.concatenate([high[...], high3[...], high4[...]], 0)
    low = jnp.concatenate([low[...], low3[...], low4[...]], 0)
    odd = lax.rem(lax.axis_index("narrow"), 2) == 1
    upper = jnp.where(odd, theirs[...], mine[...])
    lower = jnp.where(odd, mine[...], theirs[...])
    lane = lax.broadcasted_iota(jnp.int32, (16, 128), 1)
    pieces = [
        (pltpu.roll(upper, 16, 1), 16),
        (pltpu.roll(upper, 48, 1), 32),
        (pltpu.roll(lower, 64, 1), 48),
        (lower, 64),
        (upper, 80),
    ]
    for a, (piece, width) in enumerate(pieces):
        gram_low[16 * a : 16 * a + 16, :] = jnp.where(lane < width, piece, 0.0)
    gram_low[80:, :] = jnp.zeros((48, 128), F32)
    lower_part = gram_low[...]
    row = lax.broadcasted_iota(jnp.int32, (128, 128), 0) // 16
    column = lax.broadcasted_iota(jnp.int32, (128, 128), 1) // 16
    gram = jnp.where(row >= column, lower_part, lower_part.T)
    weighted = gram[:64] + gram[16:80] * (1.0 / GAIN)
    lane = lax.broadcasted_iota(jnp.int32, (64, 128), 1)
    normal = weighted + pltpu.roll(weighted, 112, 1) * (1.0 / GAIN)
    system = jnp.where(lane < 64, normal, pltpu.roll(weighted, 64, 1))
    system = jnp.where(lane < 80, system, 0.0)
    coeffs = pltpu.roll(solve_spd(system), 64, 1)
    empty = jnp.zeros((16, 128), F32)
    padded = jnp.concatenate([coeffs, empty], 0)
    mixed = padded + jnp.concatenate([empty, coeffs], 0) * (1.0 / GAIN)
    lane = lax.broadcasted_iota(jnp.int32, (80, 128), 1)
    both = jnp.where(lane < 16, padded, pltpu.roll(mixed, 16, 1))
    both = jnp.where(lane < 32, both, 0.0)
    both = jnp.concatenate([both, jnp.zeros((48, 128), F32)], 0).T[:32]
    mask_high, mask_low = split(both)
    change = jnp.dot(mask_high[:, :80], high, preferred_element_type=F32)
    change = change + jnp.dot(mask_high[:, :80], low, preferred_element_type=F32)
    change = change + jnp.dot(mask_low[:, :80], high, preferred_element_type=F32)
    mask = left_half((8, 128))
    for pair in range(ELEMS // 2):
        lanes = slice(pair * 128, pair * 128 + 128)
        top, bottom = change[0:8, lanes], change[8:16, lanes]
        tiled[0, 2 * pair] = jnp.where(mask, top, swap(bottom))
        tiled[0, 2 * pair + 1] = jnp.where(mask, swap(top), bottom)
        top, bottom = change[16:24, lanes], change[24:32, lanes]
        tiled[1, 2 * pair] = jnp.where(mask, top, swap(bottom))
        tiled[1, 2 * pair + 1] = jnp.where(mask, swap(top), bottom)
    for t in range(8):
        lanes = slice(t * 128, t * 128 + 128)
        solution[:, lanes] = guess[:, lanes] + tiled[0, :, t, :]
        residual[:, lanes] = first[:, lanes] - tiled[1, :, t, :]


def call(kernel, outs, scratch, specs, limit=32 * 1024):
    return pl.pallas_call(
        kernel,
        out_shape=outs,
        in_specs=specs,
        out_specs=[VMEM] * len(outs),
        scratch_shapes=scratch,
        compiler_params=pltpu.CompilerParams(vmem_limit_bytes=limit * 1024),
    )


def swapped(block, axes, first):
    lower = range(first, lax.axis_size(axes) - 1, 2)
    return lax.ppermute(block, axes, [(i, i + 1) for i in lower] + [(i + 1, i) for i in lower])


def local(right_side, start_guess, block_diag, face_lift, face_scale, neighbors, ghost_send, axes):
    sent = jax.ShapeDtypeStruct((GHOST, WIDTH), F32)
    message = jax.ShapeDtypeStruct((2 * GHOST, WIDTH), F32)
    to_other, to_pair, choose = call(
        pack_kernel,
        [message, sent, jax.ShapeDtypeStruct((ELEMS, 1024), BF16)],
        [
            pltpu.VMEM((ELEMS, WIDTH), F32),
            pltpu.VMEM((FACES, ELEMS), jnp.int32),
            pltpu.VMEM((FACES, ELEMS), F32),
            pltpu.VMEM((1, 2 * GHOST), jnp.int32),
            pltpu.VMEM((ELEMS, 128), F32),
            pltpu.SMEM((1, 2 * GHOST), jnp.int32),
            pltpu.SemaphoreType.DMA((5,)),
        ],
        [HBM] * 4,
        60 * 1024,
    )(ghost_send, start_guess, neighbors.T, face_scale.T)
    from_other = swapped(to_other, axes, 1)
    from_pair = swapped(to_pair, axes, 0)
    block_parts, lift_parts = call(
        prep_kernel,
        [
            jax.ShapeDtypeStruct((ELEMS * NODES, 256), BF16),
            jax.ShapeDtypeStruct((384, FACES * 128), BF16),
        ],
        [pltpu.VMEM((ELEMS, NODES, 128), F32)],
        [VMEM] * 2,
    )(block_diag, face_lift)
    tile_scratch = pltpu.VMEM((ELEMS, 8, 128), F32)
    own_call = lambda *args: call(
        first_own_kernel, [FIELD], [tile_scratch] * 2, [VMEM] * 4
    )(*args)[0]
    own = own_call(choose, start_guess, block_parts, lift_parts)
    basis = []
    vector, to_other, to_pair, terms = call(
        first_ghost_kernel,
        [FIELD, sent, sent, jax.ShapeDtypeStruct((16, 3 * FACES * 2 * GHOST), BF16)],
        [],
        [VMEM] * 7,
    )(choose, own, from_other, from_pair, lift_parts, right_side, start_guess)
    basis.append(vector)
    stack = lambda rows: jax.ShapeDtypeStruct((rows, ELEMS * NODES), BF16)
    for half in range(2):
        from_pair = swapped(to_pair, axes, 0)
        own = own_call(choose, vector, block_parts, lift_parts)
        partial, outgoing = call(pair_kernel, [FIELD, message], [], [VMEM] * 5)(
            choose, own, from_pair, lift_parts, to_other
        )
        incoming = swapped(outgoing, axes, 1)
        if half == 0:
            missing = call(flight_kernel, [sent], [], [VMEM] * 3)(terms, lift_parts, to_other)[0]
        else:
            missing, high, low, gram = call(
                gram_flight_kernel,
                [sent, stack(48), stack(48), jax.ShapeDtypeStruct((48, 48), F32)],
                [tile_scratch],
                [VMEM] * 6,
            )(terms, lift_parts, to_other, *basis)
        vector, to_pair, next_other = call(other_kernel, [FIELD, sent, sent], [], [VMEM] * 5)(
            choose, partial, incoming, missing, lift_parts
        )
        basis.append(vector)
        from_pair = swapped(to_pair, axes, 0)
        if half == 0:
            own = own_call(choose, vector, block_parts, lift_parts)
            vector, to_other, to_pair = call(both_kernel, [FIELD, sent, sent], [], [VMEM] * 5)(
                choose, own, next_other, from_pair, lift_parts
            )
            basis.append(vector)
        else:
            own, high3, low3 = call(
                dense_own_kernel, [FIELD, stack(16), stack(16)], [tile_scratch] * 2, [VMEM] * 4
            )(choose, vector, block_parts, lift_parts)
    high4, low4, packed = call(
        last_kernel,
        [stack(16), stack(16), jax.ShapeDtypeStruct((32, 128), F32)],
        [pltpu.VMEM((ELEMS, WIDTH), F32), tile_scratch],
        [VMEM] * 10,
    )(choose, own, next_other, from_pair, lift_parts, high, low, high3, low3, gram)
    outer, inner, narrow = (lax.axis_size(axis) for axis in axes)
    halves = jnp.broadcast_to(packed.reshape(1, 2, 16, 128), (outer * narrow // 2, 2, 16, 128))
    halves = halves.reshape(outer * narrow, 16, 128)
    mine = lax.all_to_all(halves, (axes[0], axes[2]), 0, 0).sum(0)
    mine = jnp.broadcast_to(mine[None], (inner, 16, 128))
    mine = lax.all_to_all(mine, axes[1], 0, 0).sum(0)
    theirs = swapped(mine, axes, 0)
    return tuple(
        call(
            solve_kernel,
            [FIELD, FIELD],
            [pltpu.VMEM((128, 128), F32), pltpu.VMEM((2, ELEMS, 8, 128), F32)],
            [VMEM] * 10,
        )(mine, theirs, high, low, high3, low3, high4, low4, basis[0], start_guess)
    )


def solution(mesh):
    wide, narrow = mesh.devices.shape
    inner = 16 if wide % 16 == 0 else 2
    axes = ("outer", "inner", "narrow")
    split_mesh = Mesh(mesh.devices.reshape(wide // inner, inner, narrow), axes)
    rows = P(axes, None)
    return jax.shard_map(
        functools.partial(local, axes=axes),
        mesh=split_mesh,
        in_specs=(rows, rows, rows, P(), rows, rows, rows),
        out_specs=(rows, rows),
        check_vma=False,
    )
```

```python
import functools

import jax
import jax.numpy as jnp
from jax import lax
from jax.experimental import pallas as pl
from jax.experimental.pallas import tpu as pltpu
from jax.sharding import Mesh, PartitionSpec as P

STEPS = 4
GAIN = 1.5
RHS = 16
NODES = 64
FACES = 6
ELEMS = 32
GHOST = 4
F32 = jnp.float32
BF16 = jnp.bfloat16

OWN, FROM, SEND = (0, 576), (640, 784), (896, 992)

VMEM = pl.BlockSpec(memory_space=pltpu.VMEM)
HBM = pl.BlockSpec(memory_space=pltpu.HBM)


WIDTH = RHS * NODES
FIELD = jax.ShapeDtypeStruct((ELEMS, WIDTH), F32)


def dot_nt(left, right):
    return lax.dot_general(left, right, (((1,), (1,)), ((), ())), preferred_element_type=F32)


def split(value):
    high = value.astype(BF16)
    low = (value - high.astype(F32)).astype(BF16)
    return high, low


def swap(value):
    return pltpu.roll(value, 64, 1)


def left_half(shape):
    return lax.broadcasted_iota(jnp.int32, shape, len(shape) - 1) < 64


def slab(t):
    return slice(t * 128, t * 128 + 128)


def to_tiles(ref, out):
    for t in range(8):
        out[:, t, :] = ref[:, slab(t)]


def selection(near, scale, first, count):
    columns = []
    for f in range(FACES):
        place = first(lax.broadcasted_iota(jnp.int32, (count, ELEMS), 0))
        columns.append(jnp.where(place == near[f : f + 1, :], scale[f : f + 1, :], 0.0))
    return jnp.concatenate(columns, 0)


def three_parts(chosen, axis):
    high = chosen.astype(BF16).astype(F32)
    return jnp.concatenate([high, high, chosen - high], axis)


def pack_kernel(
    send_in, guess_in, near_in, scale_in, to_other, to_pair, choose,
    guess, near, scale, send_row, terms, send, done,
):
    pairs = [(send_in, send), (guess_in, guess), (near_in, near), (scale_in, scale), (send_in, send_row)]
    copies = [pltpu.make_async_copy(a, b, done.at[i]) for i, (a, b) in enumerate(pairs)]
    for copy in copies:
        copy.start()
    for copy in copies:
        copy.wait()
    odd = lax.rem(lax.axis_index("narrow"), 2)
    choose[...] = jnp.zeros((ELEMS, 1024), BF16)
    own = selection(near, scale, lambda n: n, ELEMS)
    choose[:, OWN[0] : OWN[1]] = three_parts(own, 0).T.astype(BF16)
    ghosts = selection(near, scale, lambda m: ELEMS + lax.rem(m + GHOST * odd, 2 * GHOST), 2 * GHOST)
    choose[:, FROM[0] : FROM[1]] = three_parts(ghosts, 0).T.astype(BF16)
    terms[...] = jnp.zeros((ELEMS, 128), F32)
    terms[:, : FACES * 2 * GHOST] = ghosts.T
    for out, first in ((to_other, GHOST * odd), (to_pair, GHOST * (1 - odd))):
        out[GHOST:, :] = jnp.zeros((GHOST, WIDTH), F32)
        for k in range(GHOST):
            row = send[0, first + k]
            out[k : k + 1, :] = guess[pl.ds(row, 1), :]
            out[GHOST + k : GHOST + k + 1, :128] = terms[pl.ds(row, 1), :]
    row = send_row[...]
    row = jnp.where(odd == 1, jnp.concatenate([row[:, GHOST:], row[:, :GHOST]], 1), row)
    rows = (lax.broadcasted_iota(jnp.int32, (ELEMS, 2 * GHOST), 0) == row).astype(F32)
    rows = jnp.concatenate([rows, jnp.zeros((ELEMS, ELEMS - 2 * GHOST), F32)], 1)
    choose[:, SEND[0] : SEND[1]] = jnp.concatenate([rows, rows, rows], 0).T.astype(BF16)


def prep_kernel(blocks, lift, block_parts, lift_parts, spread_blocks):
    for f in range(FACES):
        upper = jnp.concatenate([lift[f], jnp.zeros((NODES, NODES), F32)], 1)
        high, low = split(jnp.concatenate([upper, swap(upper)], 0).T)
        lift_parts[:128, slab(f)] = high
        lift_parts[128:256, slab(f)] = high
        lift_parts[256:, slab(f)] = low
    mask = left_half((ELEMS, 128))
    for pair in range(NODES // 2):
        two = blocks[:, pair * 128 : pair * 128 + 128]
        turned = swap(two)
        spread_blocks[:, 2 * pair, :] = jnp.where(mask, two, turned)
        spread_blocks[:, 2 * pair + 1, :] = jnp.where(mask, turned, two)
    for element in range(ELEMS):
        high, low = split(spread_blocks[element])
        rows = slice(element * NODES, (element + 1) * NODES)
        block_parts[rows, :128] = high
        block_parts[rows, 128:] = low


def face_sum(vector, lift_parts, chosen):
    count = vector.shape[0]
    rows = jnp.concatenate([vector[:, slab(t)] for t in range(8)], 0)
    high, low = split(rows)
    both = jnp.concatenate([high, low, high], 1)
    moved = jnp.dot(both, lift_parts[...], preferred_element_type=F32)
    moved = jnp.concatenate(
        [
            jnp.concatenate([moved[t * count : (t + 1) * count, slab(f)] for t in range(8)], 1)
            for f in range(FACES)
        ],
        0,
    )
    high, low = split(moved)
    parts = jnp.concatenate([high, low, high], 0)
    return jnp.dot(chosen, parts, preferred_element_type=F32)


def from_sides(choose, lift_parts, other=None, pair=None):
    empty = jnp.zeros((GHOST, WIDTH), F32)
    ghosts = jnp.concatenate([empty if other is None else other, empty if pair is None else pair], 0)
    return face_sum(ghosts, lift_parts, choose[:, FROM[0] : FROM[1]])


def sent_rows(vector, choose):
    high = vector.astype(BF16)
    rest = vector - high.astype(F32)
    middle, low = split(rest)
    parts = jnp.concatenate([high, middle, low], 0)
    rows = jnp.dot(choose[:16, SEND[0] : SEND[1]], parts, preferred_element_type=F32)
    return rows[:GHOST], rows[GHOST : 2 * GHOST]


def dense(vector):
    upper, lower = [], []
    mask = left_half((8, 128))
    for pair in range(ELEMS // 2):
        first, second = vector[2 * pair], vector[2 * pair + 1]
        upper.append(jnp.where(mask, first, swap(second)))
        lower.append(jnp.where(mask, swap(first), second))
    return jnp.concatenate([jnp.concatenate(upper, 1), jnp.concatenate(lower, 1)], 0)


def own_part(vector, block_parts, lift_parts, choose, out, tiled, product):
    to_tiles(vector, tiled)
    value = tiled[...].reshape(ELEMS * 8, 128)
    mask = left_half((ELEMS * 8, 128))
    high, low = split(value)
    high, low = high.astype(F32), low.astype(F32)
    turned_high, turned_low = swap(high), swap(low)
    first = jnp.where(mask, low, turned_high).astype(BF16)
    second = jnp.where(mask, turned_low, high).astype(BF16)
    first_rest = jnp.where(mask, high, 0.0).astype(BF16)
    second_rest = jnp.where(mask, 0.0, high).astype(BF16)
    first = jnp.concatenate([first, first_rest], 1)
    second = jnp.concatenate([second, second_rest], 1)
    mask = left_half((8, 128))
    for group in range(ELEMS // 4):
        rows = slice(group * 32, (group + 1) * 32)
        both = jnp.concatenate([first[rows], second[rows]], 0)
        result = dot_nt(both, block_parts[group * 256 : (group + 1) * 256, :])
        for part in range(4):
            lanes = slab(part // 2)
            top = result[part * 8 : part * 8 + 8, lanes]
            bottom = result[32 + part * 8 : 40 + part * 8, lanes]
            if part % 2 == 0:
                product[group * 4 + part] = jnp.where(mask, top, swap(bottom))
            else:
                product[group * 4 + part] = jnp.where(mask, swap(top), bottom)
    faces = face_sum(vector[...], lift_parts, choose[:, OWN[0] : OWN[1]])
    for t in range(8):
        out[:, slab(t)] = faces[:, slab(t)] + product[:, t, :]


def gram_of(left_high, left_low, high, low):
    left = jnp.concatenate([left_high, left_high, left_low], 1)
    return dot_nt(left, jnp.concatenate([high, low, high], 1))


def first_own_kernel(choose, vector, block_parts, lift_parts, out, tiled, product):
    own_part(vector, block_parts, lift_parts, choose, out, tiled, product)


def dense_own_kernel(
    choose, vector, block_parts, lift_parts, out, high_out, low_out, tiled, product
):
    own_part(vector, block_parts, lift_parts, choose, out, tiled, product)
    high_out[...], low_out[...] = split(dense(tiled))


def first_ghost_kernel(
    choose, own, from_other, from_pair, lift_parts, right, guess,
    out, to_other, to_pair, terms, pair_terms,
):
    faces = from_sides(choose, lift_parts, from_other[:GHOST], from_pair[:GHOST])
    vector = right[...] - (guess[...] + (own[...] + faces))
    out[...] = vector
    to_other[...], to_pair[...] = sent_rows(vector, choose)
    for sent, out in ((from_other, terms), (from_pair, pair_terms)):
        theirs = three_parts(sent[GHOST:, : FACES * 2 * GHOST], 1)
        empty = jnp.zeros((16 - GHOST, theirs.shape[1]), F32)
        out[...] = jnp.concatenate([theirs, empty], 0).astype(BF16)


def pair_kernel(choose, own, from_pair, lift_parts, to_other, partial, message):
    total = own[...] + from_sides(choose, lift_parts, pair=from_pair[...])
    partial[...] = total
    message[:GHOST] = to_other[...]
    message[GHOST:] = sent_rows(GAIN * total, choose)[0]


def missing_terms(terms, lift_parts, to_other, missing):
    rows = jnp.concatenate([to_other[...], jnp.zeros((GHOST, WIDTH), F32)], 0)
    missing[...] = GAIN * face_sum(rows, lift_parts, terms[...])[:GHOST]


def flight_kernel(terms, lift_parts, to_other, missing):
    missing_terms(terms, lift_parts, to_other, missing)


def gram_flight_kernel(
    terms, lift_parts, to_other, first, second, third, missing, high, low, gram, tiled
):
    missing_terms(terms, lift_parts, to_other, missing)
    for a, vector in enumerate((first, second, third)):
        to_tiles(vector, tiled)
        high[16 * a : 16 * a + 16], low[16 * a : 16 * a + 16] = split(dense(tiled))
    gram[...] = gram_of(high[...], low[...], high[...], low[...])


def other_own_kernel(
    choose, partial, message, missing, block_parts, lift_parts, out, own, to_pair, outgoing, tiled, product
):
    vector = GAIN * (partial[...] + from_sides(choose, lift_parts, other=message[:GHOST]))
    out[...] = vector
    own_part(out, block_parts, lift_parts, choose, own, tiled, product)
    total = own[...] + from_sides(choose, lift_parts, other=message[GHOST:] + missing[...])
    own[...] = total
    rows = sent_rows(vector, choose)[1]
    to_pair[...] = rows
    outgoing[:GHOST] = rows
    outgoing[GHOST:] = sent_rows(GAIN * total, choose)[1]


def pair_flight_kernel(terms, lift_parts, to_pair, missing):
    rows = jnp.concatenate([jnp.zeros((GHOST, WIDTH), F32), to_pair[...]], 0)
    missing[...] = GAIN * face_sum(rows, lift_parts, terms[...])[:GHOST]


def pair_own_kernel(
    choose, own, message, missing, block_parts, lift_parts, out, partial, to_other, outgoing, tiled, product
):
    vector = GAIN * (own[...] + from_sides(choose, lift_parts, pair=message[:GHOST]))
    out[...] = vector
    own_part(out, block_parts, lift_parts, choose, partial, tiled, product)
    total = partial[...] + from_sides(choose, lift_parts, pair=message[GHOST:] + missing[...])
    partial[...] = total
    rows = sent_rows(vector, choose)[0]
    to_other[...] = rows
    outgoing[:GHOST] = rows
    outgoing[GHOST:] = sent_rows(GAIN * total, choose)[0]


def other_kernel(choose, partial, message, missing, lift_parts, out, to_pair, next_other):
    faces = from_sides(choose, lift_parts, other=message[:GHOST])
    vector = GAIN * (partial[...] + faces)
    out[...] = vector
    to_pair[...] = sent_rows(vector, choose)[1]
    next_other[...] = message[GHOST:] + missing[...]


def last_kernel(
    choose, own, from_other, from_pair, lift_parts, high, low, high3, low3, gram, high4, low4, packed, newest, tiled,
):
    newest[...] = GAIN * (own[...] + from_sides(choose, lift_parts, from_other[...], from_pair[...]))
    to_tiles(newest, tiled)
    high4[...], low4[...] = split(dense(tiled))
    left_high = jnp.concatenate([high3[...], high4[...]], 0)
    left_low = jnp.concatenate([low3[...], low4[...]], 0)
    rows = gram_of(
        left_high,
        left_low,
        jnp.concatenate([high[...], left_high], 0),
        jnp.concatenate([low[...], left_low], 0),
    )
    packed[0:16] = jnp.concatenate([rows[16:], gram[16:32, :32], gram[:16, :16]], 1)
    packed[16:32] = jnp.concatenate([rows[:16, :64], gram[32:, :], jnp.zeros((16, 16), F32)], 1)


def solve_spd(system):
    size, block = 64, 16
    row_id = lax.broadcasted_iota(jnp.int32, (block, 128), 0)
    for start in range(0, size, block):
        stop = start + block
        columns = [jnp.broadcast_to(system[:, start + j : start + j + 1], (size, 128)) for j in range(block)]
        pivots = [column[start:stop, :] for column in columns]
        rows = system[start:stop, :]
        for j in range(block):
            here = row_id == j
            inverse = 1.0 / pivots[j][j : j + 1, :]
            factor = pivots[j]
            for l in range(j + 1, block):
                scaled = pivots[l][j : j + 1, :] * inverse
                pivots[l] = jnp.where(here, scaled, pivots[l] - factor * scaled)
            scaled = rows[j : j + 1, :] * inverse
            rows = jnp.where(here, scaled, rows - factor * scaled)
        terms = [columns[j] * rows[j : j + 1, :] for j in range(block)]
        while len(terms) > 1:
            terms = [a + b for a, b in zip(terms[::2], terms[1::2])]
        update = system - terms[0]
        parts = [update[:start], rows, update[stop:]]
        system = jnp.concatenate([part for part in parts if part.shape[0]], 0)
    return system


def solve_kernel(
    mine, theirs, high, low, high3, low3, high4, low4, first, guess,
    solution, residual, gram_low, tiled,
):
    high = jnp.concatenate([high[...], high3[...], high4[...]], 0)
    low = jnp.concatenate([low[...], low3[...], low4[...]], 0)
    odd = lax.rem(lax.axis_index("narrow"), 2) == 1
    upper = jnp.where(odd, theirs[...], mine[...])
    lower = jnp.where(odd, mine[...], theirs[...])
    lane = lax.broadcasted_iota(jnp.int32, (16, 128), 1)
    pieces = [
        (pltpu.roll(upper, 16, 1), 16),
        (pltpu.roll(upper, 48, 1), 32),
        (pltpu.roll(lower, 64, 1), 48),
        (lower, 64),
        (upper, 80),
    ]
    for a, (piece, width) in enumerate(pieces):
        gram_low[16 * a : 16 * a + 16, :] = jnp.where(lane < width, piece, 0.0)
    gram_low[80:, :] = jnp.zeros((48, 128), F32)
    lower_part = gram_low[...]
    row = lax.broadcasted_iota(jnp.int32, (128, 128), 0) // 16
    column = lax.broadcasted_iota(jnp.int32, (128, 128), 1) // 16
    gram = jnp.where(row >= column, lower_part, lower_part.T)
    weighted = gram[:64] + gram[16:80] * (1.0 / GAIN)
    lane = lax.broadcasted_iota(jnp.int32, (64, 128), 1)
    normal = weighted + pltpu.roll(weighted, 112, 1) * (1.0 / GAIN)
    system = jnp.where(lane < 64, normal, pltpu.roll(weighted, 64, 1))
    system = jnp.where(lane < 80, system, 0.0)
    coeffs = pltpu.roll(solve_spd(system), 64, 1)
    empty = jnp.zeros((16, 128), F32)
    padded = jnp.concatenate([coeffs, empty], 0)
    mixed = padded + jnp.concatenate([empty, coeffs], 0) * (1.0 / GAIN)
    lane = lax.broadcasted_iota(jnp.int32, (80, 128), 1)
    both = jnp.where(lane < 16, padded, pltpu.roll(mixed, 16, 1))
    both = jnp.where(lane < 32, both, 0.0)
    both = jnp.concatenate([both, jnp.zeros((48, 128), F32)], 0).T[:32]
    mask_high, mask_low = split(both)
    change = jnp.dot(mask_high[:, :80], high, preferred_element_type=F32)
    change = change + jnp.dot(mask_high[:, :80], low, preferred_element_type=F32)
    change = change + jnp.dot(mask_low[:, :80], high, preferred_element_type=F32)
    mask = left_half((8, 128))
    for pair in range(ELEMS // 2):
        lanes = slice(pair * 128, pair * 128 + 128)
        top, bottom = change[0:8, lanes], change[8:16, lanes]
        tiled[0, 2 * pair] = jnp.where(mask, top, swap(bottom))
        tiled[0, 2 * pair + 1] = jnp.where(mask, swap(top), bottom)
        top, bottom = change[16:24, lanes], change[24:32, lanes]
        tiled[1, 2 * pair] = jnp.where(mask, top, swap(bottom))
        tiled[1, 2 * pair + 1] = jnp.where(mask, swap(top), bottom)
    for t in range(8):
        lanes = slice(t * 128, t * 128 + 128)
        solution[:, lanes] = guess[:, lanes] + tiled[0, :, t, :]
        residual[:, lanes] = first[:, lanes] - tiled[1, :, t, :]


def call(kernel, outs, scratch, specs, limit=32 * 1024):
    return pl.pallas_call(
        kernel,
        out_shape=outs,
        in_specs=specs,
        out_specs=[VMEM] * len(outs),
        scratch_shapes=scratch,
        compiler_params=pltpu.CompilerParams(vmem_limit_bytes=limit * 1024),
    )


def swapped(block, axes, first):
    lower = range(first, lax.axis_size(axes) - 1, 2)
    return lax.ppermute(block, axes, [(i, i + 1) for i in lower] + [(i + 1, i) for i in lower])


def local(right_side, start_guess, block_diag, face_lift, face_scale, neighbors, ghost_send, axes):
    sent = jax.ShapeDtypeStruct((GHOST, WIDTH), F32)
    message = jax.ShapeDtypeStruct((2 * GHOST, WIDTH), F32)
    to_other, to_pair, choose = call(
        pack_kernel,
        [message, message, jax.ShapeDtypeStruct((ELEMS, 1024), BF16)],
        [
            pltpu.VMEM((ELEMS, WIDTH), F32),
            pltpu.VMEM((FACES, ELEMS), jnp.int32),
            pltpu.VMEM((FACES, ELEMS), F32),
            pltpu.VMEM((1, 2 * GHOST), jnp.int32),
            pltpu.VMEM((ELEMS, 128), F32),
            pltpu.SMEM((1, 2 * GHOST), jnp.int32),
            pltpu.SemaphoreType.DMA((5,)),
        ],
        [HBM] * 4,
        60 * 1024,
    )(ghost_send, start_guess, neighbors.T, face_scale.T)
    from_other = swapped(to_other, axes, 1)
    from_pair = swapped(to_pair, axes, 0)
    block_parts, lift_parts = call(
        prep_kernel,
        [
            jax.ShapeDtypeStruct((ELEMS * NODES, 256), BF16),
            jax.ShapeDtypeStruct((384, FACES * 128), BF16),
        ],
        [pltpu.VMEM((ELEMS, NODES, 128), F32)],
        [VMEM] * 2,
    )(block_diag, face_lift)
    tile_scratch = pltpu.VMEM((ELEMS, 8, 128), F32)
    own_call = lambda *args: call(
        first_own_kernel, [FIELD], [tile_scratch] * 2, [VMEM] * 4
    )(*args)[0]
    own = own_call(choose, start_guess, block_parts, lift_parts)
    vector, to_other, to_pair, terms, pair_terms = call(
        first_ghost_kernel,
        [FIELD, sent, sent] + [jax.ShapeDtypeStruct((16, 3 * FACES * 2 * GHOST), BF16)] * 2,
        [],
        [VMEM] * 7,
    )(choose, own, from_other, from_pair, lift_parts, right_side, start_guess)
    basis = [vector]
    stack = lambda rows: jax.ShapeDtypeStruct((rows, ELEMS * NODES), BF16)
    from_pair = swapped(to_pair, axes, 0)
    own = own_call(choose, vector, block_parts, lift_parts)
    partial, outgoing = call(pair_kernel, [FIELD, message], [], [VMEM] * 5)(
        choose, own, from_pair, lift_parts, to_other
    )
    incoming = swapped(outgoing, axes, 1)
    missing = call(flight_kernel, [sent], [], [VMEM] * 3)(terms, lift_parts, to_other)[0]
    joint = [FIELD, FIELD, sent, message], [tile_scratch] * 2, [VMEM] * 6
    vector, own, to_pair, outgoing = call(other_own_kernel, *joint)(
        choose, partial, incoming, missing, block_parts, lift_parts
    )
    basis.append(vector)
    incoming = swapped(outgoing, axes, 0)
    missing = call(pair_flight_kernel, [sent], [], [VMEM] * 3)(pair_terms, lift_parts, to_pair)[0]
    vector, partial, to_other, outgoing = call(pair_own_kernel, *joint)(
        choose, own, incoming, missing, block_parts, lift_parts
    )
    basis.append(vector)
    incoming = swapped(outgoing, axes, 1)
    missing, high, low, gram = call(
        gram_flight_kernel,
        [sent, stack(48), stack(48), jax.ShapeDtypeStruct((48, 48), F32)],
        [tile_scratch],
        [VMEM] * 6,
    )(terms, lift_parts, to_other, *basis)
    vector, to_pair, next_other = call(other_kernel, [FIELD, sent, sent], [], [VMEM] * 5)(
        choose, partial, incoming, missing, lift_parts
    )
    from_pair = swapped(to_pair, axes, 0)
    own, high3, low3 = call(
        dense_own_kernel, [FIELD, stack(16), stack(16)], [tile_scratch] * 2, [VMEM] * 4
    )(choose, vector, block_parts, lift_parts)
    high4, low4, packed = call(
        last_kernel,
        [stack(16), stack(16), jax.ShapeDtypeStruct((32, 128), F32)],
        [pltpu.VMEM((ELEMS, WIDTH), F32), tile_scratch],
        [VMEM] * 10,
    )(choose, own, next_other, from_pair, lift_parts, high, low, high3, low3, gram)
    outer, inner, narrow = (lax.axis_size(axis) for axis in axes)
    halves = jnp.broadcast_to(packed.reshape(1, 2, 16, 128), (outer * narrow // 2, 2, 16, 128))
    halves = halves.reshape(outer * narrow, 16, 128)
    mine = lax.all_to_all(halves, (axes[0], axes[2]), 0, 0).sum(0)
    mine = jnp.broadcast_to(mine[None], (inner, 16, 128))
    mine = lax.all_to_all(mine, axes[1], 0, 0).sum(0)
    theirs = swapped(mine, axes, 0)
    return tuple(
        call(
            solve_kernel,
            [FIELD, FIELD],
            [pltpu.VMEM((128, 128), F32), pltpu.VMEM((2, ELEMS, 8, 128), F32)],
            [VMEM] * 10,
        )(mine, theirs, high, low, high3, low3, high4, low4, basis[0], start_guess)
    )


def solution(mesh):
    wide, narrow = mesh.devices.shape
    inner = 16 if wide % 16 == 0 else 2
    axes = ("outer", "inner", "narrow")
    split_mesh = Mesh(mesh.devices.reshape(wide // inner, inner, narrow), axes)
    rows = P(axes, None)
    return jax.shard_map(
        functools.partial(local, axes=axes),
        mesh=split_mesh,
        in_specs=(rows, rows, rows, P(), rows, rows, rows),
        out_specs=(rows, rows),
        check_vma=False,
    )
```

```python
import functools

import jax
import jax.numpy as jnp
from jax import lax
from jax.experimental import pallas as pl
from jax.experimental.pallas import tpu as pltpu
from jax.sharding import Mesh, PartitionSpec as P

STEPS = 4
GAIN = 1.5
RHS = 16
NODES = 64
FACES = 6
ELEMS = 32
GHOST = 4
F32 = jnp.float32
BF16 = jnp.bfloat16

OWN, FROM, SEND = (0, 576), (640, 784), (896, 992)

VMEM = pl.BlockSpec(memory_space=pltpu.VMEM)
HBM = pl.BlockSpec(memory_space=pltpu.HBM)


WIDTH = RHS * NODES
FIELD = jax.ShapeDtypeStruct((ELEMS, WIDTH), F32)


def dot_nt(left, right):
    return lax.dot_general(left, right, (((1,), (1,)), ((), ())), preferred_element_type=F32)


def split(value):
    high = value.astype(BF16)
    low = (value - high.astype(F32)).astype(BF16)
    return high, low


def swap(value):
    return pltpu.roll(value, 64, 1)


def left_half(shape):
    return lax.broadcasted_iota(jnp.int32, shape, len(shape) - 1) < 64


def slab(t):
    return slice(t * 128, t * 128 + 128)


def to_tiles(ref, out):
    for t in range(8):
        out[:, t, :] = ref[:, slab(t)]


def selection(near, scale, first, count):
    columns = []
    for f in range(FACES):
        place = first(lax.broadcasted_iota(jnp.int32, (count, ELEMS), 0))
        columns.append(jnp.where(place == near[f : f + 1, :], scale[f : f + 1, :], 0.0))
    return jnp.concatenate(columns, 0)


def three_parts(chosen, axis):
    high = chosen.astype(BF16).astype(F32)
    return jnp.concatenate([high, high, chosen - high], axis)


def pack_kernel(
    send_in, guess_in, near_in, scale_in, to_other, to_pair, choose,
    guess, near, scale, send_row, terms, send, done,
):
    pairs = [(send_in, send), (guess_in, guess), (near_in, near), (scale_in, scale), (send_in, send_row)]
    copies = [pltpu.make_async_copy(a, b, done.at[i]) for i, (a, b) in enumerate(pairs)]
    for copy in copies:
        copy.start()
    for copy in copies:
        copy.wait()
    odd = lax.rem(lax.axis_index("narrow"), 2)
    choose[...] = jnp.zeros((ELEMS, 1024), BF16)
    own = selection(near, scale, lambda n: n, ELEMS)
    choose[:, OWN[0] : OWN[1]] = three_parts(own, 0).T.astype(BF16)
    ghosts = selection(near, scale, lambda m: ELEMS + lax.rem(m + GHOST * odd, 2 * GHOST), 2 * GHOST)
    choose[:, FROM[0] : FROM[1]] = three_parts(ghosts, 0).T.astype(BF16)
    terms[...] = jnp.zeros((ELEMS, 128), F32)
    terms[:, : FACES * 2 * GHOST] = ghosts.T
    for out, first in ((to_other, GHOST * odd), (to_pair, GHOST * (1 - odd))):
        out[GHOST:, :] = jnp.zeros((GHOST, WIDTH), F32)
        for k in range(GHOST):
            row = send[0, first + k]
            out[k : k + 1, :] = guess[pl.ds(row, 1), :]
            out[GHOST + k : GHOST + k + 1, :128] = terms[pl.ds(row, 1), :]
    row = send_row[...]
    row = jnp.where(odd == 1, jnp.concatenate([row[:, GHOST:], row[:, :GHOST]], 1), row)
    rows = (lax.broadcasted_iota(jnp.int32, (ELEMS, 2 * GHOST), 0) == row).astype(F32)
    rows = jnp.concatenate([rows, jnp.zeros((ELEMS, ELEMS - 2 * GHOST), F32)], 1)
    choose[:, SEND[0] : SEND[1]] = jnp.concatenate([rows, rows, rows], 0).T.astype(BF16)


def prep_kernel(blocks_in, lift_in, block_parts, lift_parts, blocks, lift, spread_blocks, done):
    copies = [
        pltpu.make_async_copy(lift_in, lift, done.at[0]),
        pltpu.make_async_copy(blocks_in, blocks, done.at[1]),
    ]
    for copy in copies:
        copy.start()
    copies[0].wait()
    for f in range(FACES):
        upper = jnp.concatenate([lift[f], jnp.zeros((NODES, NODES), F32)], 1)
        high, low = split(jnp.concatenate([upper, swap(upper)], 0).T)
        lift_parts[:128, slab(f)] = high
        lift_parts[128:256, slab(f)] = high
        lift_parts[256:, slab(f)] = low
    copies[1].wait()
    mask = left_half((ELEMS, 128))
    for pair in range(NODES // 2):
        two = blocks[:, pair * 128 : pair * 128 + 128]
        turned = swap(two)
        spread_blocks[:, 2 * pair, :] = jnp.where(mask, two, turned)
        spread_blocks[:, 2 * pair + 1, :] = jnp.where(mask, turned, two)
    for element in range(ELEMS):
        high, low = split(spread_blocks[element])
        rows = slice(element * NODES, (element + 1) * NODES)
        block_parts[rows, :128] = high
        block_parts[rows, 128:] = low


def face_sum(vector, lift_parts, chosen):
    count = vector.shape[0]
    rows = jnp.concatenate([vector[:, slab(t)] for t in range(8)], 0)
    high, low = split(rows)
    both = jnp.concatenate([high, low, high], 1)
    moved = jnp.dot(both, lift_parts[...], preferred_element_type=F32)
    moved = jnp.concatenate(
        [
            jnp.concatenate([moved[t * count : (t + 1) * count, slab(f)] for t in range(8)], 1)
            for f in range(FACES)
        ],
        0,
    )
    high, low = split(moved)
    parts = jnp.concatenate([high, low, high], 0)
    return jnp.dot(chosen, parts, preferred_element_type=F32)


def from_sides(choose, lift_parts, other=None, pair=None):
    empty = jnp.zeros((GHOST, WIDTH), F32)
    ghosts = jnp.concatenate([empty if other is None else other, empty if pair is None else pair], 0)
    return face_sum(ghosts, lift_parts, choose[:, FROM[0] : FROM[1]])


def sent_rows(vector, choose):
    high = vector.astype(BF16)
    rest = vector - high.astype(F32)
    middle, low = split(rest)
    parts = jnp.concatenate([high, middle, low], 0)
    rows = jnp.dot(choose[:16, SEND[0] : SEND[1]], parts, preferred_element_type=F32)
    return rows[:GHOST], rows[GHOST : 2 * GHOST]


def dense(vector):
    upper, lower = [], []
    mask = left_half((8, 128))
    for pair in range(ELEMS // 2):
        first, second = vector[2 * pair], vector[2 * pair + 1]
        upper.append(jnp.where(mask, first, swap(second)))
        lower.append(jnp.where(mask, swap(first), second))
    return jnp.concatenate([jnp.concatenate(upper, 1), jnp.concatenate(lower, 1)], 0)


def own_part(vector, block_parts, lift_parts, choose, out, tiled, product):
    to_tiles(vector, tiled)
    value = tiled[...].reshape(ELEMS * 8, 128)
    mask = left_half((ELEMS * 8, 128))
    high, low = split(value)
    high, low = high.astype(F32), low.astype(F32)
    turned_high, turned_low = swap(high), swap(low)
    first = jnp.where(mask, low, turned_high).astype(BF16)
    second = jnp.where(mask, turned_low, high).astype(BF16)
    first_rest = jnp.where(mask, high, 0.0).astype(BF16)
    second_rest = jnp.where(mask, 0.0, high).astype(BF16)
    first = jnp.concatenate([first, first_rest], 1)
    second = jnp.concatenate([second, second_rest], 1)
    mask = left_half((8, 128))
    for group in range(ELEMS // 4):
        rows = slice(group * 32, (group + 1) * 32)
        both = jnp.concatenate([first[rows], second[rows]], 0)
        result = dot_nt(both, block_parts[group * 256 : (group + 1) * 256, :])
        for part in range(4):
            lanes = slab(part // 2)
            top = result[part * 8 : part * 8 + 8, lanes]
            bottom = result[32 + part * 8 : 40 + part * 8, lanes]
            if part % 2 == 0:
                product[group * 4 + part] = jnp.where(mask, top, swap(bottom))
            else:
                product[group * 4 + part] = jnp.where(mask, swap(top), bottom)
    faces = face_sum(vector[...], lift_parts, choose[:, OWN[0] : OWN[1]])
    for t in range(8):
        out[:, slab(t)] = faces[:, slab(t)] + product[:, t, :]


def gram_of(left_high, left_low, high, low):
    left = jnp.concatenate([left_high, left_high, left_low], 1)
    return dot_nt(left, jnp.concatenate([high, low, high], 1))


def first_own_kernel(choose, vector, block_parts, lift_parts, out, tiled, product):
    own_part(vector, block_parts, lift_parts, choose, out, tiled, product)


def dense_own_kernel(
    choose, vector, block_parts, lift_parts, out, high_out, low_out, tiled, product
):
    own_part(vector, block_parts, lift_parts, choose, out, tiled, product)
    high_out[...], low_out[...] = split(dense(tiled))


def first_ghost_kernel(
    choose, own, from_other, from_pair, lift_parts, right, guess,
    out, to_other, to_pair, terms, pair_terms,
):
    faces = from_sides(choose, lift_parts, from_other[:GHOST], from_pair[:GHOST])
    vector = right[...] - (guess[...] + (own[...] + faces))
    out[...] = vector
    to_other[...], to_pair[...] = sent_rows(vector, choose)
    for sent, out in ((from_other, terms), (from_pair, pair_terms)):
        theirs = three_parts(sent[GHOST:, : FACES * 2 * GHOST], 1)
        empty = jnp.zeros((16 - GHOST, theirs.shape[1]), F32)
        out[...] = jnp.concatenate([theirs, empty], 0).astype(BF16)


def pair_kernel(choose, own, from_pair, lift_parts, to_other, partial, message):
    total = own[...] + from_sides(choose, lift_parts, pair=from_pair[...])
    partial[...] = total
    message[:GHOST] = to_other[...]
    message[GHOST:] = sent_rows(GAIN * total, choose)[0]


def missing_terms(terms, lift_parts, to_other, missing):
    rows = jnp.concatenate([to_other[...], jnp.zeros((GHOST, WIDTH), F32)], 0)
    missing[...] = GAIN * face_sum(rows, lift_parts, terms[...])[:GHOST]


def flight_kernel(terms, lift_parts, to_other, missing):
    missing_terms(terms, lift_parts, to_other, missing)


def gram_flight_kernel(
    terms, lift_parts, to_other, first, second, third, missing, high, low, gram, tiled
):
    missing_terms(terms, lift_parts, to_other, missing)
    for a, vector in enumerate((first, second, third)):
        to_tiles(vector, tiled)
        high[16 * a : 16 * a + 16], low[16 * a : 16 * a + 16] = split(dense(tiled))
    gram[...] = gram_of(high[...], low[...], high[...], low[...])


def other_own_kernel(
    choose, partial, message, missing, block_parts, lift_parts, out, own, to_pair, outgoing, tiled, product
):
    vector = GAIN * (partial[...] + from_sides(choose, lift_parts, other=message[:GHOST]))
    out[...] = vector
    own_part(out, block_parts, lift_parts, choose, own, tiled, product)
    total = own[...] + from_sides(choose, lift_parts, other=message[GHOST:] + missing[...])
    own[...] = total
    rows = sent_rows(vector, choose)[1]
    to_pair[...] = rows
    outgoing[:GHOST] = rows
    outgoing[GHOST:] = sent_rows(GAIN * total, choose)[1]


def pair_flight_kernel(terms, lift_parts, to_pair, missing):
    rows = jnp.concatenate([jnp.zeros((GHOST, WIDTH), F32), to_pair[...]], 0)
    missing[...] = GAIN * face_sum(rows, lift_parts, terms[...])[:GHOST]


def pair_own_kernel(
    choose, own, message, missing, block_parts, lift_parts, out, partial, to_other, outgoing, tiled, product
):
    vector = GAIN * (own[...] + from_sides(choose, lift_parts, pair=message[:GHOST]))
    out[...] = vector
    own_part(out, block_parts, lift_parts, choose, partial, tiled, product)
    total = partial[...] + from_sides(choose, lift_parts, pair=message[GHOST:] + missing[...])
    partial[...] = total
    rows = sent_rows(vector, choose)[0]
    to_other[...] = rows
    outgoing[:GHOST] = rows
    outgoing[GHOST:] = sent_rows(GAIN * total, choose)[0]


def other_kernel(choose, partial, message, missing, lift_parts, out, to_pair, next_other):
    faces = from_sides(choose, lift_parts, other=message[:GHOST])
    vector = GAIN * (partial[...] + faces)
    out[...] = vector
    to_pair[...] = sent_rows(vector, choose)[1]
    next_other[...] = message[GHOST:] + missing[...]


def last_kernel(
    choose, own, from_other, from_pair, lift_parts, high, low, high3, low3, gram, high4, low4, packed, newest, tiled,
):
    newest[...] = GAIN * (own[...] + from_sides(choose, lift_parts, from_other[...], from_pair[...]))
    to_tiles(newest, tiled)
    high4[...], low4[...] = split(dense(tiled))
    left_high = jnp.concatenate([high3[...], high4[...]], 0)
    left_low = jnp.concatenate([low3[...], low4[...]], 0)
    rows = gram_of(
        left_high,
        left_low,
        jnp.concatenate([high[...], left_high], 0),
        jnp.concatenate([low[...], left_low], 0),
    )
    packed[0:16] = jnp.concatenate([rows[16:], gram[16:32, :32], gram[:16, :16]], 1)
    packed[16:32] = jnp.concatenate([rows[:16, :64], gram[32:, :], jnp.zeros((16, 16), F32)], 1)


def solve_spd(system):
    size, block = 64, 16
    row_id = lax.broadcasted_iota(jnp.int32, (block, 128), 0)
    for start in range(0, size, block):
        stop = start + block
        columns = [jnp.broadcast_to(system[:, start + j : start + j + 1], (size, 128)) for j in range(block)]
        pivots = [column[start:stop, :] for column in columns]
        rows = system[start:stop, :]
        for j in range(block):
            here = row_id == j
            inverse = 1.0 / pivots[j][j : j + 1, :]
            factor = pivots[j]
            for l in range(j + 1, block):
                scaled = pivots[l][j : j + 1, :] * inverse
                pivots[l] = jnp.where(here, scaled, pivots[l] - factor * scaled)
            scaled = rows[j : j + 1, :] * inverse
            rows = jnp.where(here, scaled, rows - factor * scaled)
        terms = [columns[j] * rows[j : j + 1, :] for j in range(block)]
        while len(terms) > 1:
            terms = [a + b for a, b in zip(terms[::2], terms[1::2])]
        update = system - terms[0]
        parts = [update[:start], rows, update[stop:]]
        system = jnp.concatenate([part for part in parts if part.shape[0]], 0)
    return system


def solve_kernel(
    mine, theirs, high, low, high3, low3, high4, low4, first, guess,
    solution, residual, gram_low, tiled,
):
    high = jnp.concatenate([high[...], high3[...], high4[...]], 0)
    low = jnp.concatenate([low[...], low3[...], low4[...]], 0)
    odd = lax.rem(lax.axis_index("narrow"), 2) == 1
    upper = jnp.where(odd, theirs[...], mine[...])
    lower = jnp.where(odd, mine[...], theirs[...])
    lane = lax.broadcasted_iota(jnp.int32, (16, 128), 1)
    pieces = [
        (pltpu.roll(upper, 16, 1), 16),
        (pltpu.roll(upper, 48, 1), 32),
        (pltpu.roll(lower, 64, 1), 48),
        (lower, 64),
        (upper, 80),
    ]
    for a, (piece, width) in enumerate(pieces):
        gram_low[16 * a : 16 * a + 16, :] = jnp.where(lane < width, piece, 0.0)
    gram_low[80:, :] = jnp.zeros((48, 128), F32)
    lower_part = gram_low[...]
    row = lax.broadcasted_iota(jnp.int32, (128, 128), 0) // 16
    column = lax.broadcasted_iota(jnp.int32, (128, 128), 1) // 16
    gram = jnp.where(row >= column, lower_part, lower_part.T)
    weighted = gram[:64] + gram[16:80] * (1.0 / GAIN)
    lane = lax.broadcasted_iota(jnp.int32, (64, 128), 1)
    normal = weighted + pltpu.roll(weighted, 112, 1) * (1.0 / GAIN)
    system = jnp.where(lane < 64, normal, pltpu.roll(weighted, 64, 1))
    system = jnp.where(lane < 80, system, 0.0)
    coeffs = pltpu.roll(solve_spd(system), 64, 1)
    empty = jnp.zeros((16, 128), F32)
    padded = jnp.concatenate([coeffs, empty], 0)
    mixed = padded + jnp.concatenate([empty, coeffs], 0) * (1.0 / GAIN)
    lane = lax.broadcasted_iota(jnp.int32, (80, 128), 1)
    both = jnp.where(lane < 16, padded, pltpu.roll(mixed, 16, 1))
    both = jnp.where(lane < 32, both, 0.0)
    both = jnp.concatenate([both, jnp.zeros((48, 128), F32)], 0).T[:32]
    mask_high, mask_low = split(both)
    change = jnp.dot(mask_high[:, :80], high, preferred_element_type=F32)
    change = change + jnp.dot(mask_high[:, :80], low, preferred_element_type=F32)
    change = change + jnp.dot(mask_low[:, :80], high, preferred_element_type=F32)
    mask = left_half((8, 128))
    for pair in range(ELEMS // 2):
        lanes = slice(pair * 128, pair * 128 + 128)
        top, bottom = change[0:8, lanes], change[8:16, lanes]
        tiled[0, 2 * pair] = jnp.where(mask, top, swap(bottom))
        tiled[0, 2 * pair + 1] = jnp.where(mask, swap(top), bottom)
        top, bottom = change[16:24, lanes], change[24:32, lanes]
        tiled[1, 2 * pair] = jnp.where(mask, top, swap(bottom))
        tiled[1, 2 * pair + 1] = jnp.where(mask, swap(top), bottom)
    for t in range(8):
        lanes = slice(t * 128, t * 128 + 128)
        solution[:, lanes] = guess[:, lanes] + tiled[0, :, t, :]
        residual[:, lanes] = first[:, lanes] - tiled[1, :, t, :]


def call(kernel, outs, scratch, specs, limit=32 * 1024):
    return pl.pallas_call(
        kernel,
        out_shape=outs,
        in_specs=specs,
        out_specs=[VMEM] * len(outs),
        scratch_shapes=scratch,
        compiler_params=pltpu.CompilerParams(vmem_limit_bytes=limit * 1024),
    )


def in_hbm(array):
    return pltpu.with_memory_space_constraint(array, pltpu.HBM)


def swapped(block, axes, first):
    lower = range(first, lax.axis_size(axes) - 1, 2)
    return lax.ppermute(block, axes, [(i, i + 1) for i in lower] + [(i + 1, i) for i in lower])


def local(right_side, start_guess, block_diag, face_lift, face_scale, neighbors, ghost_send, axes):
    sent = jax.ShapeDtypeStruct((GHOST, WIDTH), F32)
    message = jax.ShapeDtypeStruct((2 * GHOST, WIDTH), F32)
    to_other, to_pair, choose = call(
        pack_kernel,
        [message, message, jax.ShapeDtypeStruct((ELEMS, 1024), BF16)],
        [
            pltpu.VMEM((ELEMS, WIDTH), F32),
            pltpu.VMEM((FACES, ELEMS), jnp.int32),
            pltpu.VMEM((FACES, ELEMS), F32),
            pltpu.VMEM((1, 2 * GHOST), jnp.int32),
            pltpu.VMEM((ELEMS, 128), F32),
            pltpu.SMEM((1, 2 * GHOST), jnp.int32),
            pltpu.SemaphoreType.DMA((5,)),
        ],
        [HBM] * 4,
    )(*map(in_hbm, (ghost_send, start_guess, neighbors.T, face_scale.T)))
    from_other = swapped(to_other, axes, 1)
    from_pair = swapped(to_pair, axes, 0)
    block_parts, lift_parts = call(
        prep_kernel,
        [
            jax.ShapeDtypeStruct((ELEMS * NODES, 256), BF16),
            jax.ShapeDtypeStruct((384, FACES * 128), BF16),
        ],
        [
            pltpu.VMEM((ELEMS, NODES * NODES), F32),
            pltpu.VMEM((FACES, NODES, NODES), F32),
            pltpu.VMEM((ELEMS, NODES, 128), F32),
            pltpu.SemaphoreType.DMA((2,)),
        ],
        [HBM] * 2,
    )(in_hbm(block_diag), in_hbm(face_lift))
    tile_scratch = pltpu.VMEM((ELEMS, 8, 128), F32)
    own_call = lambda *args: call(
        first_own_kernel, [FIELD], [tile_scratch] * 2, [VMEM] * 4
    )(*args)[0]
    own = own_call(choose, start_guess, block_parts, lift_parts)
    vector, to_other, to_pair, terms, pair_terms = call(
        first_ghost_kernel,
        [FIELD, sent, sent] + [jax.ShapeDtypeStruct((16, 3 * FACES * 2 * GHOST), BF16)] * 2,
        [],
        [VMEM] * 7,
    )(choose, own, from_other, from_pair, lift_parts, right_side, start_guess)
    basis = [vector]
    stack = lambda rows: jax.ShapeDtypeStruct((rows, ELEMS * NODES), BF16)
    from_pair = swapped(to_pair, axes, 0)
    own = own_call(choose, vector, block_parts, lift_parts)
    partial, outgoing = call(pair_kernel, [FIELD, message], [], [VMEM] * 5)(
        choose, own, from_pair, lift_parts, to_other
    )
    incoming = swapped(outgoing, axes, 1)
    missing = call(flight_kernel, [sent], [], [VMEM] * 3)(terms, lift_parts, to_other)[0]
    joint = [FIELD, FIELD, sent, message], [tile_scratch] * 2, [VMEM] * 6
    vector, own, to_pair, outgoing = call(other_own_kernel, *joint)(
        choose, partial, incoming, missing, block_parts, lift_parts
    )
    basis.append(vector)
    incoming = swapped(outgoing, axes, 0)
    missing = call(pair_flight_kernel, [sent], [], [VMEM] * 3)(pair_terms, lift_parts, to_pair)[0]
    vector, partial, to_other, outgoing = call(pair_own_kernel, *joint)(
        choose, own, incoming, missing, block_parts, lift_parts
    )
    basis.append(vector)
    incoming = swapped(outgoing, axes, 1)
    missing, high, low, gram = call(
        gram_flight_kernel,
        [sent, stack(48), stack(48), jax.ShapeDtypeStruct((48, 48), F32)],
        [tile_scratch],
        [VMEM] * 6,
    )(terms, lift_parts, to_other, *basis)
    vector, to_pair, next_other = call(other_kernel, [FIELD, sent, sent], [], [VMEM] * 5)(
        choose, partial, incoming, missing, lift_parts
    )
    from_pair = swapped(to_pair, axes, 0)
    own, high3, low3 = call(
        dense_own_kernel, [FIELD, stack(16), stack(16)], [tile_scratch] * 2, [VMEM] * 4
    )(choose, vector, block_parts, lift_parts)
    high4, low4, packed = call(
        last_kernel,
        [stack(16), stack(16), jax.ShapeDtypeStruct((32, 128), F32)],
        [pltpu.VMEM((ELEMS, WIDTH), F32), tile_scratch],
        [VMEM] * 10,
    )(choose, own, next_other, from_pair, lift_parts, high, low, high3, low3, gram)
    outer, inner, narrow = (lax.axis_size(axis) for axis in axes)
    halves = jnp.broadcast_to(packed.reshape(1, 2, 16, 128), (outer * narrow // 2, 2, 16, 128))
    halves = halves.reshape(outer * narrow, 16, 128)
    mine = lax.all_to_all(halves, (axes[0], axes[2]), 0, 0).sum(0)
    mine = jnp.broadcast_to(mine[None], (inner, 16, 128))
    mine = lax.all_to_all(mine, axes[1], 0, 0).sum(0)
    theirs = swapped(mine, axes, 0)
    return tuple(
        call(
            solve_kernel,
            [FIELD, FIELD],
            [pltpu.VMEM((128, 128), F32), pltpu.VMEM((2, ELEMS, 8, 128), F32)],
            [VMEM] * 10,
        )(mine, theirs, high, low, high3, low3, high4, low4, basis[0], start_guess)
    )


def solution(mesh):
    wide, narrow = mesh.devices.shape
    inner = 16 if wide % 16 == 0 else 2
    axes = ("outer", "inner", "narrow")
    split_mesh = Mesh(mesh.devices.reshape(wide // inner, inner, narrow), axes)
    rows = P(axes, None)
    return jax.shard_map(
        functools.partial(local, axes=axes),
        mesh=split_mesh,
        in_specs=(rows, rows, rows, P(), rows, rows, rows),
        out_specs=(rows, rows),
        check_vma=False,
    )
```

```python
import functools

import jax
import jax.numpy as jnp
from jax import lax
from jax.experimental import pallas as pl
from jax.experimental.pallas import tpu as pltpu
from jax.sharding import Mesh, PartitionSpec as P

STEPS = 4
GAIN = 1.5
RHS = 16
NODES = 64
FACES = 6
ELEMS = 32
GHOST = 4
F32 = jnp.float32
BF16 = jnp.bfloat16

OWN, FROM, SEND = (0, 576), (640, 784), (896, 992)

VMEM = pl.BlockSpec(memory_space=pltpu.VMEM)
HBM = pl.BlockSpec(memory_space=pltpu.HBM)


WIDTH = RHS * NODES
FIELD = jax.ShapeDtypeStruct((ELEMS, WIDTH), F32)


def dot_nt(left, right):
    return lax.dot_general(left, right, (((1,), (1,)), ((), ())), preferred_element_type=F32)


def split(value):
    high = value.astype(BF16)
    low = (value - high.astype(F32)).astype(BF16)
    return high, low


def swap(value):
    return pltpu.roll(value, 64, 1)


def left_half(shape):
    return lax.broadcasted_iota(jnp.int32, shape, len(shape) - 1) < 64


def slab(t):
    return slice(t * 128, t * 128 + 128)


def to_tiles(ref, out):
    for t in range(8):
        out[:, t, :] = ref[:, slab(t)]


def selection(near, scale, first, count):
    columns = []
    for f in range(FACES):
        place = first(lax.broadcasted_iota(jnp.int32, (count, ELEMS), 0))
        columns.append(jnp.where(place == near[f : f + 1, :], scale[f : f + 1, :], 0.0))
    return jnp.concatenate(columns, 0)


def three_parts(chosen, axis):
    high = chosen.astype(BF16).astype(F32)
    return jnp.concatenate([high, high, chosen - high], axis)


def pack_kernel(
    send_in, guess_in, near_in, scale_in, to_other, to_pair, choose,
    guess, near, scale, send_row, terms, send, done,
):
    pairs = [(send_in, send), (guess_in, guess), (near_in, near), (scale_in, scale), (send_in, send_row)]
    copies = [pltpu.make_async_copy(a, b, done.at[i]) for i, (a, b) in enumerate(pairs)]
    for copy in copies:
        copy.start()
    for copy in copies:
        copy.wait()
    odd = lax.rem(lax.axis_index("narrow"), 2)
    choose[...] = jnp.zeros((ELEMS, 1024), BF16)
    own = selection(near, scale, lambda n: n, ELEMS)
    choose[:, OWN[0] : OWN[1]] = three_parts(own, 0).T.astype(BF16)
    ghosts = selection(near, scale, lambda m: ELEMS + lax.rem(m + GHOST * odd, 2 * GHOST), 2 * GHOST)
    choose[:, FROM[0] : FROM[1]] = three_parts(ghosts, 0).T.astype(BF16)
    terms[...] = jnp.zeros((ELEMS, 128), F32)
    terms[:, : FACES * 2 * GHOST] = ghosts.T
    for out, first in ((to_other, GHOST * odd), (to_pair, GHOST * (1 - odd))):
        out[GHOST:, :] = jnp.zeros((GHOST, WIDTH), F32)
        for k in range(GHOST):
            row = send[0, first + k]
            out[k : k + 1, :] = guess[pl.ds(row, 1), :]
            out[GHOST + k : GHOST + k + 1, :128] = terms[pl.ds(row, 1), :]
    row = send_row[...]
    row = jnp.where(odd == 1, jnp.concatenate([row[:, GHOST:], row[:, :GHOST]], 1), row)
    rows = (lax.broadcasted_iota(jnp.int32, (ELEMS, 2 * GHOST), 0) == row).astype(F32)
    rows = jnp.concatenate([rows, jnp.zeros((ELEMS, ELEMS - 2 * GHOST), F32)], 1)
    choose[:, SEND[0] : SEND[1]] = jnp.concatenate([rows, rows, rows], 0).T.astype(BF16)


def prep_kernel(blocks_in, lift_in, block_parts, lift_parts, blocks, lift, spread_blocks, done):
    copies = [
        pltpu.make_async_copy(lift_in, lift, done.at[0]),
        pltpu.make_async_copy(blocks_in, blocks, done.at[1]),
    ]
    for copy in copies:
        copy.start()
    copies[0].wait()
    for f in range(FACES):
        upper = jnp.concatenate([lift[f], jnp.zeros((NODES, NODES), F32)], 1)
        high, low = split(jnp.concatenate([upper, swap(upper)], 0).T)
        lift_parts[:128, slab(f)] = high
        lift_parts[128:256, slab(f)] = high
        lift_parts[256:, slab(f)] = low
    copies[1].wait()
    mask = left_half((ELEMS, 128))
    for pair in range(NODES // 2):
        two = blocks[:, pair * 128 : pair * 128 + 128]
        turned = swap(two)
        spread_blocks[:, 2 * pair, :] = jnp.where(mask, two, turned)
        spread_blocks[:, 2 * pair + 1, :] = jnp.where(mask, turned, two)
    for pair in range(ELEMS // 2):
        high, low = split(spread_blocks[2 * pair : 2 * pair + 2].reshape(128, 128).T)
        block_parts[:128, slab(pair)] = high
        block_parts[128:, slab(pair)] = low


def face_sum(vector, lift_parts, chosen):
    count = vector.shape[0]
    rows = jnp.concatenate([vector[:, slab(t)] for t in range(8)], 0)
    high, low = split(rows)
    both = jnp.concatenate([high, low, high], 1)
    moved = jnp.dot(both, lift_parts[...], preferred_element_type=F32)
    moved = jnp.concatenate(
        [
            jnp.concatenate([moved[t * count : (t + 1) * count, slab(f)] for t in range(8)], 1)
            for f in range(FACES)
        ],
        0,
    )
    high, low = split(moved)
    parts = jnp.concatenate([high, low, high], 0)
    return jnp.dot(chosen, parts, preferred_element_type=F32)


def from_sides(choose, lift_parts, other=None, pair=None):
    empty = jnp.zeros((GHOST, WIDTH), F32)
    ghosts = jnp.concatenate([empty if other is None else other, empty if pair is None else pair], 0)
    return face_sum(ghosts, lift_parts, choose[:, FROM[0] : FROM[1]])


def sent_rows(vector, choose):
    high = vector.astype(BF16)
    rest = vector - high.astype(F32)
    middle, low = split(rest)
    parts = jnp.concatenate([high, middle, low], 0)
    rows = jnp.dot(choose[:16, SEND[0] : SEND[1]], parts, preferred_element_type=F32)
    return rows[:GHOST], rows[GHOST : 2 * GHOST]


def dense(vector):
    upper, lower = [], []
    mask = left_half((8, 128))
    for pair in range(ELEMS // 2):
        first, second = vector[2 * pair], vector[2 * pair + 1]
        upper.append(jnp.where(mask, first, swap(second)))
        lower.append(jnp.where(mask, swap(first), second))
    return jnp.concatenate([jnp.concatenate(upper, 1), jnp.concatenate(lower, 1)], 0)


def own_part(vector, block_parts, lift_parts, choose, out, tiled, product):
    faces = face_sum(vector[...], lift_parts, choose[:, OWN[0] : OWN[1]])
    to_tiles(vector, tiled)
    value = tiled[...].reshape(ELEMS * 8, 128)
    mask = left_half((ELEMS * 8, 128))
    high, low = split(value)
    high, low = high.astype(F32), low.astype(F32)
    turned_high, turned_low = split(swap(value))
    turned_high, turned_low = turned_high.astype(F32), turned_low.astype(F32)
    first = jnp.where(mask, low, turned_high).astype(BF16)
    second = jnp.where(mask, turned_low, high).astype(BF16)
    first_rest = jnp.where(mask, high, 0.0).astype(BF16)
    second_rest = jnp.where(mask, 0.0, high).astype(BF16)
    first = jnp.concatenate([first, first_rest], 1)
    second = jnp.concatenate([second, second_rest], 1)
    mask = left_half((8, 128))
    for group in range(ELEMS // 4):
        rows = slice(group * 32, (group + 1) * 32)
        both = jnp.concatenate([first[rows], second[rows]], 0)
        columns = block_parts[:, group * 256 : (group + 1) * 256]
        result = jnp.dot(both, columns, preferred_element_type=F32)
        for part in range(4):
            lanes = slab(part // 2)
            top = result[part * 8 : part * 8 + 8, lanes]
            bottom = result[32 + part * 8 : 40 + part * 8, lanes]
            if part % 2 == 0:
                product[group * 4 + part] = jnp.where(mask, top, swap(bottom))
            else:
                product[group * 4 + part] = jnp.where(mask, swap(top), bottom)
    for t in range(8):
        out[:, slab(t)] = faces[:, slab(t)] + product[:, t, :]


def gram_of(left_high, left_low, high, low):
    count = left_high.shape[0]
    both = dot_nt(jnp.concatenate([left_high, left_low], 0), high)
    return both[:count] + both[count:] + dot_nt(left_high, low)


def first_own_kernel(choose, vector, block_parts, lift_parts, out, tiled, product):
    own_part(vector, block_parts, lift_parts, choose, out, tiled, product)


def dense_own_kernel(
    choose, vector, block_parts, lift_parts, out, high_out, low_out, tiled, product
):
    own_part(vector, block_parts, lift_parts, choose, out, tiled, product)
    high_out[...], low_out[...] = split(dense(tiled))


def first_ghost_kernel(
    choose, own, from_other, from_pair, lift_parts, right, guess,
    out, to_other, to_pair, terms, pair_terms,
):
    faces = from_sides(choose, lift_parts, from_other[:GHOST], from_pair[:GHOST])
    vector = right[...] - (guess[...] + (own[...] + faces))
    out[...] = vector
    to_other[...], to_pair[...] = sent_rows(vector, choose)
    for sent, out in ((from_other, terms), (from_pair, pair_terms)):
        theirs = three_parts(sent[GHOST:, : FACES * 2 * GHOST], 1)
        empty = jnp.zeros((16 - GHOST, theirs.shape[1]), F32)
        out[...] = jnp.concatenate([theirs, empty], 0).astype(BF16)


def pair_kernel(choose, own, from_pair, lift_parts, to_other, partial, message):
    total = own[...] + from_sides(choose, lift_parts, pair=from_pair[...])
    partial[...] = total
    message[:GHOST] = to_other[...]
    message[GHOST:] = sent_rows(GAIN * total, choose)[0]


def missing_terms(terms, lift_parts, to_other, missing):
    rows = jnp.concatenate([to_other[...], jnp.zeros((GHOST, WIDTH), F32)], 0)
    missing[...] = GAIN * face_sum(rows, lift_parts, terms[...])[:GHOST]


def flight_kernel(terms, lift_parts, to_other, missing):
    missing_terms(terms, lift_parts, to_other, missing)


def gram_flight_kernel(
    terms, lift_parts, to_other, first, second, third, missing, high, low, gram, tiled
):
    missing_terms(terms, lift_parts, to_other, missing)
    for a, vector in enumerate((first, second, third)):
        to_tiles(vector, tiled)
        high[16 * a : 16 * a + 16], low[16 * a : 16 * a + 16] = split(dense(tiled))
    gram[...] = gram_of(high[...], low[...], high[...], low[...])


def other_own_kernel(
    choose, partial, message, missing, block_parts, lift_parts, out, own, to_pair, outgoing, tiled, product
):
    vector = GAIN * (partial[...] + from_sides(choose, lift_parts, other=message[:GHOST]))
    out[...] = vector
    own_part(out, block_parts, lift_parts, choose, own, tiled, product)
    total = own[...] + from_sides(choose, lift_parts, other=message[GHOST:] + missing[...])
    own[...] = total
    rows = sent_rows(vector, choose)[1]
    to_pair[...] = rows
    outgoing[:GHOST] = rows
    outgoing[GHOST:] = sent_rows(GAIN * total, choose)[1]


def pair_flight_kernel(terms, lift_parts, to_pair, missing):
    rows = jnp.concatenate([jnp.zeros((GHOST, WIDTH), F32), to_pair[...]], 0)
    missing[...] = GAIN * face_sum(rows, lift_parts, terms[...])[:GHOST]


def pair_own_kernel(
    choose, own, message, missing, block_parts, lift_parts, out, partial, to_other, outgoing, tiled, product
):
    vector = GAIN * (own[...] + from_sides(choose, lift_parts, pair=message[:GHOST]))
    out[...] = vector
    own_part(out, block_parts, lift_parts, choose, partial, tiled, product)
    total = partial[...] + from_sides(choose, lift_parts, pair=message[GHOST:] + missing[...])
    partial[...] = total
    rows = sent_rows(vector, choose)[0]
    to_other[...] = rows
    outgoing[:GHOST] = rows
    outgoing[GHOST:] = sent_rows(GAIN * total, choose)[0]


def other_kernel(choose, partial, message, missing, lift_parts, out, to_pair, next_other):
    faces = from_sides(choose, lift_parts, other=message[:GHOST])
    vector = GAIN * (partial[...] + faces)
    out[...] = vector
    to_pair[...] = sent_rows(vector, choose)[1]
    next_other[...] = message[GHOST:] + missing[...]


def last_kernel(
    choose, own, from_other, from_pair, lift_parts, high, low, high3, low3, gram, high4, low4, packed, newest, tiled,
):
    newest[...] = GAIN * (own[...] + from_sides(choose, lift_parts, from_other[...], from_pair[...]))
    to_tiles(newest, tiled)
    high4[...], low4[...] = split(dense(tiled))
    left_high = jnp.concatenate([high3[...], high4[...]], 0)
    left_low = jnp.concatenate([low3[...], low4[...]], 0)
    rows = gram_of(
        left_high,
        left_low,
        jnp.concatenate([high[...], left_high], 0),
        jnp.concatenate([low[...], left_low], 0),
    )
    packed[0:16] = jnp.concatenate([rows[16:], gram[16:32, :32], gram[:16, :16]], 1)
    packed[16:32] = jnp.concatenate([rows[:16, :64], gram[32:, :], jnp.zeros((16, 16), F32)], 1)


def solve_spd(system):
    size, block = 64, 16
    row_id = lax.broadcasted_iota(jnp.int32, (block, 128), 0)
    for start in range(0, size, block):
        stop = start + block
        columns = [jnp.broadcast_to(system[:, start + j : start + j + 1], (size, 128)) for j in range(block)]
        pivots = [column[start:stop, :] for column in columns]
        rows = system[start:stop, :]
        for j in range(block):
            here = row_id == j
            inverse = 1.0 / pivots[j][j : j + 1, :]
            factor = pivots[j]
            for l in range(j + 1, block):
                scaled = pivots[l][j : j + 1, :] * inverse
                pivots[l] = jnp.where(here, scaled, pivots[l] - factor * scaled)
            scaled = rows[j : j + 1, :] * inverse
            rows = jnp.where(here, scaled, rows - factor * scaled)
        terms = [columns[j] * rows[j : j + 1, :] for j in range(block)]
        while len(terms) > 1:
            terms = [a + b for a, b in zip(terms[::2], terms[1::2])]
        update = system - terms[0]
        parts = [update[:start], rows, update[stop:]]
        system = jnp.concatenate([part for part in parts if part.shape[0]], 0)
    return system


def solve_kernel(
    mine, theirs, high, low, high3, low3, high4, low4, first, guess,
    solution, residual, gram_low, tiled,
):
    high = jnp.concatenate([high[...], high3[...], high4[...]], 0)
    low = jnp.concatenate([low[...], low3[...], low4[...]], 0)
    odd = lax.rem(lax.axis_index("narrow"), 2) == 1
    upper = jnp.where(odd, theirs[...], mine[...])
    lower = jnp.where(odd, mine[...], theirs[...])
    lane = lax.broadcasted_iota(jnp.int32, (16, 128), 1)
    pieces = [
        (pltpu.roll(upper, 16, 1), 16),
        (pltpu.roll(upper, 48, 1), 32),
        (pltpu.roll(lower, 64, 1), 48),
        (lower, 64),
        (upper, 80),
    ]
    for a, (piece, width) in enumerate(pieces):
        gram_low[16 * a : 16 * a + 16, :] = jnp.where(lane < width, piece, 0.0)
    gram_low[80:, :] = jnp.zeros((48, 128), F32)
    lower_part = gram_low[...]
    row = lax.broadcasted_iota(jnp.int32, (128, 128), 0) // 16
    column = lax.broadcasted_iota(jnp.int32, (128, 128), 1) // 16
    gram = jnp.where(row >= column, lower_part, lower_part.T)
    weighted = gram[:64] + gram[16:80] * (1.0 / GAIN)
    lane = lax.broadcasted_iota(jnp.int32, (64, 128), 1)
    normal = weighted + pltpu.roll(weighted, 112, 1) * (1.0 / GAIN)
    system = jnp.where(lane < 64, normal, pltpu.roll(weighted, 64, 1))
    system = jnp.where(lane < 80, system, 0.0)
    coeffs = pltpu.roll(solve_spd(system), 64, 1)
    empty = jnp.zeros((16, 128), F32)
    padded = jnp.concatenate([coeffs, empty], 0)
    mixed = padded + jnp.concatenate([empty, coeffs], 0) * (1.0 / GAIN)
    lane = lax.broadcasted_iota(jnp.int32, (80, 128), 1)
    both = jnp.where(lane < 16, padded, pltpu.roll(mixed, 16, 1))
    both = jnp.where(lane < 32, both, 0.0)
    both = jnp.concatenate([both, jnp.zeros((48, 128), F32)], 0).T[:32]
    mask_high, mask_low = split(both)
    change = jnp.dot(mask_high[:, :80], high, preferred_element_type=F32)
    change = change + jnp.dot(mask_high[:, :80], low, preferred_element_type=F32)
    change = change + jnp.dot(mask_low[:, :80], high, preferred_element_type=F32)
    mask = left_half((8, 128))
    for pair in range(ELEMS // 2):
        lanes = slice(pair * 128, pair * 128 + 128)
        top, bottom = change[0:8, lanes], change[8:16, lanes]
        tiled[0, 2 * pair] = jnp.where(mask, top, swap(bottom))
        tiled[0, 2 * pair + 1] = jnp.where(mask, swap(top), bottom)
        top, bottom = change[16:24, lanes], change[24:32, lanes]
        tiled[1, 2 * pair] = jnp.where(mask, top, swap(bottom))
        tiled[1, 2 * pair + 1] = jnp.where(mask, swap(top), bottom)
    for t in range(8):
        lanes = slice(t * 128, t * 128 + 128)
        solution[:, lanes] = guess[:, lanes] + tiled[0, :, t, :]
        residual[:, lanes] = first[:, lanes] - tiled[1, :, t, :]


def call(kernel, outs, scratch, specs, limit=32 * 1024):
    return pl.pallas_call(
        kernel,
        out_shape=outs,
        in_specs=specs,
        out_specs=[VMEM] * len(outs),
        scratch_shapes=scratch,
        compiler_params=pltpu.CompilerParams(vmem_limit_bytes=limit * 1024),
    )


def in_hbm(array):
    return pltpu.with_memory_space_constraint(array, pltpu.HBM)


def swapped(block, axes, first):
    lower = range(first, lax.axis_size(axes) - 1, 2)
    return lax.ppermute(block, axes, [(i, i + 1) for i in lower] + [(i + 1, i) for i in lower])


def local(right_side, start_guess, block_diag, face_lift, face_scale, neighbors, ghost_send, axes):
    sent = jax.ShapeDtypeStruct((GHOST, WIDTH), F32)
    message = jax.ShapeDtypeStruct((2 * GHOST, WIDTH), F32)
    to_other, to_pair, choose = call(
        pack_kernel,
        [message, message, jax.ShapeDtypeStruct((ELEMS, 1024), BF16)],
        [
            pltpu.VMEM((ELEMS, WIDTH), F32),
            pltpu.VMEM((FACES, ELEMS), jnp.int32),
            pltpu.VMEM((FACES, ELEMS), F32),
            pltpu.VMEM((1, 2 * GHOST), jnp.int32),
            pltpu.VMEM((ELEMS, 128), F32),
            pltpu.SMEM((1, 2 * GHOST), jnp.int32),
            pltpu.SemaphoreType.DMA((5,)),
        ],
        [HBM] * 4,
    )(*map(in_hbm, (ghost_send, start_guess, neighbors.T, face_scale.T)))
    from_other = swapped(to_other, axes, 1)
    from_pair = swapped(to_pair, axes, 0)
    block_parts, lift_parts = call(
        prep_kernel,
        [
            jax.ShapeDtypeStruct((256, ELEMS * NODES), BF16),
            jax.ShapeDtypeStruct((384, FACES * 128), BF16),
        ],
        [
            pltpu.VMEM((ELEMS, NODES * NODES), F32),
            pltpu.VMEM((FACES, NODES, NODES), F32),
            pltpu.VMEM((ELEMS, NODES, 128), F32),
            pltpu.SemaphoreType.DMA((2,)),
        ],
        [HBM] * 2,
    )(in_hbm(block_diag), in_hbm(face_lift))
    tile_scratch = pltpu.VMEM((ELEMS, 8, 128), F32)
    own_call = lambda *args: call(
        first_own_kernel, [FIELD], [tile_scratch] * 2, [VMEM] * 4
    )(*args)[0]
    own = own_call(choose, start_guess, block_parts, lift_parts)
    vector, to_other, to_pair, terms, pair_terms = call(
        first_ghost_kernel,
        [FIELD, sent, sent] + [jax.ShapeDtypeStruct((16, 3 * FACES * 2 * GHOST), BF16)] * 2,
        [],
        [VMEM] * 7,
    )(choose, own, from_other, from_pair, lift_parts, right_side, start_guess)
    basis = [vector]
    stack = lambda rows: jax.ShapeDtypeStruct((rows, ELEMS * NODES), BF16)
    from_pair = swapped(to_pair, axes, 0)
    own = own_call(choose, vector, block_parts, lift_parts)
    partial, outgoing = call(pair_kernel, [FIELD, message], [], [VMEM] * 5)(
        choose, own, from_pair, lift_parts, to_other
    )
    incoming = swapped(outgoing, axes, 1)
    missing = call(flight_kernel, [sent], [], [VMEM] * 3)(terms, lift_parts, to_other)[0]
    joint = [FIELD, FIELD, sent, message], [tile_scratch] * 2, [VMEM] * 6
    vector, own, to_pair, outgoing = call(other_own_kernel, *joint)(
        choose, partial, incoming, missing, block_parts, lift_parts
    )
    basis.append(vector)
    incoming = swapped(outgoing, axes, 0)
    missing = call(pair_flight_kernel, [sent], [], [VMEM] * 3)(pair_terms, lift_parts, to_pair)[0]
    vector, partial, to_other, outgoing = call(pair_own_kernel, *joint)(
        choose, own, incoming, missing, block_parts, lift_parts
    )
    basis.append(vector)
    incoming = swapped(outgoing, axes, 1)
    missing, high, low, gram = call(
        gram_flight_kernel,
        [sent, stack(48), stack(48), jax.ShapeDtypeStruct((48, 48), F32)],
        [tile_scratch],
        [VMEM] * 6,
    )(terms, lift_parts, to_other, *basis)
    vector, to_pair, next_other = call(other_kernel, [FIELD, sent, sent], [], [VMEM] * 5)(
        choose, partial, incoming, missing, lift_parts
    )
    from_pair = swapped(to_pair, axes, 0)
    own, high3, low3 = call(
        dense_own_kernel, [FIELD, stack(16), stack(16)], [tile_scratch] * 2, [VMEM] * 4
    )(choose, vector, block_parts, lift_parts)
    high4, low4, packed = call(
        last_kernel,
        [stack(16), stack(16), jax.ShapeDtypeStruct((32, 128), F32)],
        [pltpu.VMEM((ELEMS, WIDTH), F32), tile_scratch],
        [VMEM] * 10,
    )(choose, own, next_other, from_pair, lift_parts, high, low, high3, low3, gram)
    outer, inner, narrow = (lax.axis_size(axis) for axis in axes)
    halves = jnp.broadcast_to(packed.reshape(1, 2, 16, 128), (outer * narrow // 2, 2, 16, 128))
    halves = halves.reshape(outer * narrow, 16, 128)
    mine = lax.all_to_all(halves, (axes[0], axes[2]), 0, 0).sum(0)
    mine = jnp.broadcast_to(mine[None], (inner, 16, 128))
    mine = lax.all_to_all(mine, axes[1], 0, 0).sum(0)
    theirs = swapped(mine, axes, 0)
    return tuple(
        call(
            solve_kernel,
            [FIELD, FIELD],
            [pltpu.VMEM((128, 128), F32), pltpu.VMEM((2, ELEMS, 8, 128), F32)],
            [VMEM] * 10,
        )(mine, theirs, high, low, high3, low3, high4, low4, basis[0], start_guess)
    )


def solution(mesh):
    wide, narrow = mesh.devices.shape
    inner = 16 if wide % 16 == 0 else 2
    axes = ("outer", "inner", "narrow")
    split_mesh = Mesh(mesh.devices.reshape(wide // inner, inner, narrow), axes)
    rows = P(axes, None)
    return jax.shard_map(
        functools.partial(local, axes=axes),
        mesh=split_mesh,
        in_specs=(rows, rows, rows, P(), rows, rows, rows),
        out_specs=(rows, rows),
        check_vma=False,
    )
```

```python
import functools

import jax
import jax.numpy as jnp
from jax import lax
from jax.experimental import pallas as pl
from jax.experimental.pallas import tpu as pltpu
from jax.sharding import Mesh, PartitionSpec as P

STEPS = 4
GAIN = 1.5
RHS = 16
NODES = 64
FACES = 6
ELEMS = 32
GHOST = 4
F32 = jnp.float32
BF16 = jnp.bfloat16

OWN, FROM, SEND = (0, 576), (640, 784), (896, 992)

VMEM = pl.BlockSpec(memory_space=pltpu.VMEM)
HBM = pl.BlockSpec(memory_space=pltpu.HBM)


WIDTH = RHS * NODES
FIELD = jax.ShapeDtypeStruct((ELEMS, WIDTH), F32)


def dot_nt(left, right):
    return lax.dot_general(left, right, (((1,), (1,)), ((), ())), preferred_element_type=F32)


def split(value):
    high = value.astype(BF16)
    low = (value - high.astype(F32)).astype(BF16)
    return high, low


def swap(value):
    return pltpu.roll(value, 64, 1)


def left_half(shape):
    return lax.broadcasted_iota(jnp.int32, shape, len(shape) - 1) < 64


def slab(t):
    return slice(t * 128, t * 128 + 128)


def to_tiles(ref, out):
    for t in range(8):
        out[:, t, :] = ref[:, slab(t)]


def selection(near, scale, first, count):
    columns = []
    for f in range(FACES):
        place = first(lax.broadcasted_iota(jnp.int32, (count, ELEMS), 0))
        columns.append(jnp.where(place == near[f : f + 1, :], scale[f : f + 1, :], 0.0))
    return jnp.concatenate(columns, 0)


def three_parts(chosen, axis):
    high = chosen.astype(BF16).astype(F32)
    return jnp.concatenate([high, high, chosen - high], axis)


def pack_kernel(
    send_in, guess_in, near_in, scale_in, to_other, to_pair, choose,
    guess, near, scale, send_row, terms, send, done,
):
    pairs = [(send_in, send), (guess_in, guess), (near_in, near), (scale_in, scale), (send_in, send_row)]
    copies = [pltpu.make_async_copy(a, b, done.at[i]) for i, (a, b) in enumerate(pairs)]
    for copy in copies:
        copy.start()
    for copy in copies:
        copy.wait()
    odd = lax.rem(lax.axis_index("narrow"), 2)
    choose[...] = jnp.zeros((ELEMS, 1024), BF16)
    own = selection(near, scale, lambda n: n, ELEMS)
    choose[:, OWN[0] : OWN[1]] = three_parts(own, 0).T.astype(BF16)
    ghosts = selection(near, scale, lambda m: ELEMS + lax.rem(m + GHOST * odd, 2 * GHOST), 2 * GHOST)
    choose[:, FROM[0] : FROM[1]] = three_parts(ghosts, 0).T.astype(BF16)
    terms[...] = jnp.zeros((ELEMS, 128), F32)
    terms[:, : FACES * 2 * GHOST] = ghosts.T
    for out, first in ((to_other, GHOST * odd), (to_pair, GHOST * (1 - odd))):
        out[GHOST:, :] = jnp.zeros((GHOST, WIDTH), F32)
        for k in range(GHOST):
            row = send[0, first + k]
            out[k : k + 1, :] = guess[pl.ds(row, 1), :]
            out[GHOST + k : GHOST + k + 1, :128] = terms[pl.ds(row, 1), :]
    row = send_row[...]
    row = jnp.where(odd == 1, jnp.concatenate([row[:, GHOST:], row[:, :GHOST]], 1), row)
    rows = (lax.broadcasted_iota(jnp.int32, (ELEMS, 2 * GHOST), 0) == row).astype(F32)
    rows = jnp.concatenate([rows, jnp.zeros((ELEMS, ELEMS - 2 * GHOST), F32)], 1)
    choose[:, SEND[0] : SEND[1]] = jnp.concatenate([rows, rows, rows], 0).T.astype(BF16)


def prep_kernel(blocks_in, lift_in, block_parts, lift_parts, blocks, lift, spread_blocks, done):
    copies = [
        pltpu.make_async_copy(lift_in, lift, done.at[0]),
        pltpu.make_async_copy(blocks_in, blocks, done.at[1]),
    ]
    for copy in copies:
        copy.start()
    copies[0].wait()
    for f in range(FACES):
        upper = jnp.concatenate([lift[f], jnp.zeros((NODES, NODES), F32)], 1)
        high, low = split(jnp.concatenate([upper, swap(upper)], 0).T)
        lift_parts[:128, slab(f)] = high
        lift_parts[128:256, slab(f)] = high
        lift_parts[256:, slab(f)] = low
    copies[1].wait()
    mask = left_half((ELEMS, 128))
    for pair in range(NODES // 2):
        two = blocks[:, pair * 128 : pair * 128 + 128]
        turned = swap(two)
        spread_blocks[:, 2 * pair, :] = jnp.where(mask, two, turned)
        spread_blocks[:, 2 * pair + 1, :] = jnp.where(mask, turned, two)
    for pair in range(ELEMS // 2):
        high, low = split(spread_blocks[2 * pair : 2 * pair + 2].reshape(128, 128).T)
        block_parts[:128, slab(pair)] = high
        block_parts[128:, slab(pair)] = low


def face_sum(vector, lift_parts, chosen):
    count = vector.shape[0]
    rows = jnp.concatenate([vector[:, slab(t)] for t in range(8)], 0)
    high, low = split(rows)
    both = jnp.concatenate([high, low, high], 1)
    moved = jnp.dot(both, lift_parts[...], preferred_element_type=F32)
    moved = jnp.concatenate(
        [
            jnp.concatenate([moved[t * count : (t + 1) * count, slab(f)] for t in range(8)], 1)
            for f in range(FACES)
        ],
        0,
    )
    high, low = split(moved)
    parts = jnp.concatenate([high, low, high], 0)
    return jnp.dot(chosen, parts, preferred_element_type=F32)


def from_sides(choose, lift_parts, other=None, pair=None):
    empty = jnp.zeros((GHOST, WIDTH), F32)
    ghosts = jnp.concatenate([empty if other is None else other, empty if pair is None else pair], 0)
    return face_sum(ghosts, lift_parts, choose[:, FROM[0] : FROM[1]])


def sent_rows(vector, choose):
    high = vector.astype(BF16)
    rest = vector - high.astype(F32)
    middle, low = split(rest)
    parts = jnp.concatenate([high, middle, low], 0)
    rows = jnp.dot(choose[:16, SEND[0] : SEND[1]], parts, preferred_element_type=F32)
    return rows[:GHOST], rows[GHOST : 2 * GHOST]


def dense(vector):
    upper, lower = [], []
    mask = left_half((8, 128))
    for pair in range(ELEMS // 2):
        first, second = vector[2 * pair], vector[2 * pair + 1]
        upper.append(jnp.where(mask, first, swap(second)))
        lower.append(jnp.where(mask, swap(first), second))
    return jnp.concatenate([jnp.concatenate(upper, 1), jnp.concatenate(lower, 1)], 0)


def own_part(vector, block_parts, lift_parts, choose, out, tiled, product):
    faces = face_sum(vector[...], lift_parts, choose[:, OWN[0] : OWN[1]])
    to_tiles(vector, tiled)
    value = tiled[...].reshape(ELEMS * 8, 128)
    mask = left_half((ELEMS * 8, 128))
    high, low = split(value)
    high, low = high.astype(F32), low.astype(F32)
    turned_high, turned_low = split(swap(value))
    turned_high, turned_low = turned_high.astype(F32), turned_low.astype(F32)
    first = jnp.where(mask, low, turned_high).astype(BF16)
    second = jnp.where(mask, turned_low, high).astype(BF16)
    first_rest = jnp.where(mask, high, 0.0).astype(BF16)
    second_rest = jnp.where(mask, 0.0, high).astype(BF16)
    first = jnp.concatenate([first, first_rest], 1)
    second = jnp.concatenate([second, second_rest], 1)
    mask = left_half((8, 128))
    for group in range(ELEMS // 4):
        rows = slice(group * 32, (group + 1) * 32)
        both = jnp.concatenate([first[rows], second[rows]], 0)
        columns = block_parts[:, group * 256 : (group + 1) * 256]
        result = jnp.dot(both, columns, preferred_element_type=F32)
        for part in range(4):
            lanes = slab(part // 2)
            top = result[part * 8 : part * 8 + 8, lanes]
            bottom = result[32 + part * 8 : 40 + part * 8, lanes]
            if part % 2 == 0:
                product[group * 4 + part] = jnp.where(mask, top, swap(bottom))
            else:
                product[group * 4 + part] = jnp.where(mask, swap(top), bottom)
    for t in range(8):
        out[:, slab(t)] = faces[:, slab(t)] + product[:, t, :]


def gram_of(left_high, left_low, high, low):
    count = left_high.shape[0]
    both = dot_nt(jnp.concatenate([left_high, left_low], 0), high)
    return both[:count] + both[count:] + dot_nt(left_high, low)


def first_own_kernel(choose, vector, block_parts, lift_parts, out, tiled, product):
    own_part(vector, block_parts, lift_parts, choose, out, tiled, product)


def dense_own_kernel(
    choose, vector, block_parts, lift_parts, out, high_out, low_out, tiled, product
):
    own_part(vector, block_parts, lift_parts, choose, out, tiled, product)
    high_out[...], low_out[...] = split(dense(tiled))


def first_ghost_kernel(
    choose, own, from_other, from_pair, lift_parts, right, guess,
    out, to_other, to_pair, terms, pair_terms,
):
    faces = from_sides(choose, lift_parts, from_other[:GHOST], from_pair[:GHOST])
    vector = right[...] - (guess[...] + (own[...] + faces))
    out[...] = vector
    to_other[...], to_pair[...] = sent_rows(vector, choose)
    for sent, out in ((from_other, terms), (from_pair, pair_terms)):
        theirs = three_parts(sent[GHOST:, : FACES * 2 * GHOST], 1)
        empty = jnp.zeros((16 - GHOST, theirs.shape[1]), F32)
        out[...] = jnp.concatenate([theirs, empty], 0).astype(BF16)


def pair_kernel(choose, own, from_pair, lift_parts, to_other, partial, message):
    total = own[...] + from_sides(choose, lift_parts, pair=from_pair[...])
    partial[...] = total
    message[:GHOST] = to_other[...]
    message[GHOST:] = sent_rows(GAIN * total, choose)[0]


def missing_terms(terms, lift_parts, to_other, missing):
    rows = jnp.concatenate([to_other[...], jnp.zeros((GHOST, WIDTH), F32)], 0)
    missing[...] = GAIN * face_sum(rows, lift_parts, terms[...])[:GHOST]


def flight_kernel(terms, lift_parts, to_other, missing):
    missing_terms(terms, lift_parts, to_other, missing)


def gram_flight_kernel(
    terms, lift_parts, to_other, first, second, third, missing, high, low, gram, tiled
):
    missing_terms(terms, lift_parts, to_other, missing)
    for a, vector in enumerate((first, second, third)):
        to_tiles(vector, tiled)
        high[16 * a : 16 * a + 16], low[16 * a : 16 * a + 16] = split(dense(tiled))
    gram[...] = gram_of(high[...], low[...], high[...], low[...])


def other_own_kernel(
    choose, partial, message, missing, block_parts, lift_parts, out, own, to_pair, outgoing, tiled, product
):
    vector = GAIN * (partial[...] + from_sides(choose, lift_parts, other=message[:GHOST]))
    out[...] = vector
    own_part(out, block_parts, lift_parts, choose, own, tiled, product)
    total = own[...] + from_sides(choose, lift_parts, other=message[GHOST:] + missing[...])
    own[...] = total
    rows = sent_rows(vector, choose)[1]
    to_pair[...] = rows
    outgoing[:GHOST] = rows
    outgoing[GHOST:] = sent_rows(GAIN * total, choose)[1]


def pair_flight_kernel(terms, lift_parts, to_pair, missing):
    rows = jnp.concatenate([jnp.zeros((GHOST, WIDTH), F32), to_pair[...]], 0)
    missing[...] = GAIN * face_sum(rows, lift_parts, terms[...])[:GHOST]


def pair_own_kernel(
    choose, own, message, missing, block_parts, lift_parts, out, partial, to_other, outgoing, tiled, product
):
    vector = GAIN * (own[...] + from_sides(choose, lift_parts, pair=message[:GHOST]))
    out[...] = vector
    own_part(out, block_parts, lift_parts, choose, partial, tiled, product)
    total = partial[...] + from_sides(choose, lift_parts, pair=message[GHOST:] + missing[...])
    partial[...] = total
    rows = sent_rows(vector, choose)[0]
    to_other[...] = rows
    outgoing[:GHOST] = rows
    outgoing[GHOST:] = sent_rows(GAIN * total, choose)[0]


def other_kernel(choose, partial, message, missing, lift_parts, out, to_pair, next_other):
    faces = from_sides(choose, lift_parts, other=message[:GHOST])
    vector = GAIN * (partial[...] + faces)
    out[...] = vector
    to_pair[...] = sent_rows(vector, choose)[1]
    next_other[...] = message[GHOST:] + missing[...]


def fold(blocks):
    lane = lax.broadcasted_iota(jnp.int32, (1, 128), 1)
    rows = []
    for k in range(14):
        part = pltpu.roll(blocks[14 + k // 7 : 15 + k // 7, :], (112 - 16 * (k % 7)) % 128, 1)
        rows.append(jnp.where(lane < 112, blocks[k : k + 1, :], part))
    return rows


def unfold(rows):
    lane = lax.broadcasted_iota(jnp.int32, (1, 128), 1) // 16
    ends = []
    for half in range(2):
        total = jnp.zeros((1, 128), F32)
        for b in range(7):
            part = pltpu.roll(rows[7 * half + b], 16 * b + 16, 1)
            total = jnp.where(lane == b, part, total)
        ends.append(total)
    return jnp.concatenate(rows + ends, 0)


def last_kernel(
    choose, own, from_other, from_pair, lift_parts, high, low, high3, low3, gram, high4, low4, packed, newest, tiled, gram_low,
):
    newest[...] = GAIN * (own[...] + from_sides(choose, lift_parts, from_other[...], from_pair[...]))
    to_tiles(newest, tiled)
    high4[...], low4[...] = split(dense(tiled))
    left_high = jnp.concatenate([high3[...], high4[...]], 0)
    left_low = jnp.concatenate([low3[...], low4[...]], 0)
    rows = gram_of(
        left_high,
        left_low,
        jnp.concatenate([high[...], left_high], 0),
        jnp.concatenate([low[...], left_low], 0),
    )
    gram_low[...] = jnp.zeros((128, 128), F32)
    gram_low[0:48, 0:48] = gram[...]
    gram_low[48:80, 0:80] = rows
    known = gram_low[...]
    row = lax.broadcasted_iota(jnp.int32, (128, 128), 0) // 16
    column = lax.broadcasted_iota(jnp.int32, (128, 128), 1) // 16
    full = jnp.where(row >= column, known, known.T)
    weighted = full[:64] + full[16:80] * (1.0 / GAIN)
    normal = weighted + pltpu.roll(weighted, 112, 1) * (1.0 / GAIN)
    lane = lax.broadcasted_iota(jnp.int32, (16, 128), 1)
    joined = []
    for a in range(STEPS):
        part = slice(16 * a, 16 * a + 16)
        width = 16 * (a + 1)
        right = pltpu.roll(weighted[part], width, 1)
        joined.append(jnp.where(lane < width, normal[part], right))
    first = jnp.where(lane < 80, joined[3], pltpu.roll(joined[0], 80, 1))
    second = jnp.where(lane < 64, joined[2], pltpu.roll(joined[1], 64, 1))
    for half, blocks in enumerate((first, second)):
        folded = fold(blocks)
        for k in range(7):
            packed[half, k] = jnp.concatenate(folded[2 * k : 2 * k + 2], 0)


def solve_spd(system):
    size, block = 64, 16
    row_id = lax.broadcasted_iota(jnp.int32, (block, 128), 0)
    for start in range(0, size, block):
        stop = start + block
        columns = [jnp.broadcast_to(system[:, start + j : start + j + 1], (size, 128)) for j in range(block)]
        pivots = [column[start:stop, :] for column in columns]
        rows = system[start:stop, :]
        for j in range(block):
            here = row_id == j
            inverse = 1.0 / pivots[j][j : j + 1, :]
            factor = pivots[j]
            for l in range(j + 1, block):
                scaled = pivots[l][j : j + 1, :] * inverse
                pivots[l] = jnp.where(here, scaled, pivots[l] - factor * scaled)
            scaled = rows[j : j + 1, :] * inverse
            rows = jnp.where(here, scaled, rows - factor * scaled)
        terms = [columns[j] * rows[j : j + 1, :] for j in range(block)]
        while len(terms) > 1:
            terms = [a + b for a, b in zip(terms[::2], terms[1::2])]
        update = system - terms[0]
        parts = [update[:start], rows, update[stop:]]
        system = jnp.concatenate([part for part in parts if part.shape[0]], 0)
    return system


def solve_kernel(
    mine, theirs, high, low, high3, low3, high4, low4, first, guess,
    solution, residual, gram_low, tiled,
):
    high = jnp.concatenate([high[...], high3[...], high4[...]], 0)
    low = jnp.concatenate([low[...], low3[...], low4[...]], 0)
    odd = lax.rem(lax.axis_index("narrow"), 2) == 1
    halves = []
    for one, two in ((mine, theirs), (theirs, mine)):
        pairs = [jnp.where(odd, two[k], one[k]) for k in range(7)]
        halves.append(unfold([pair[i : i + 1, :] for pair in pairs for i in range(2)]))
    lane = lax.broadcasted_iota(jnp.int32, (16, 128), 1)
    joined = [pltpu.roll(halves[0], 48, 1), pltpu.roll(halves[1], 64, 1), halves[1], halves[0]]
    for a, part in enumerate(joined):
        width = 16 * (a + 1)
        right = pltpu.roll(part, (64 - width) % 128, 1)
        right = jnp.where((lane >= 64) & (lane < 80), right, 0.0)
        gram_low[16 * a : 16 * a + 16, :] = jnp.where(lane < width, part, right)
    gram_low[64:, :] = jnp.zeros((64, 128), F32)
    known = gram_low[...]
    row = lax.broadcasted_iota(jnp.int32, (64, 128), 0) // 16
    column = lax.broadcasted_iota(jnp.int32, (64, 128), 1) // 16
    system = jnp.where((row >= column) | (column >= 4), known[:64], known.T[:64])
    coeffs = pltpu.roll(solve_spd(system), 64, 1)
    empty = jnp.zeros((16, 128), F32)
    padded = jnp.concatenate([coeffs, empty], 0)
    mixed = padded + jnp.concatenate([empty, coeffs], 0) * (1.0 / GAIN)
    lane = lax.broadcasted_iota(jnp.int32, (80, 128), 1)
    both = jnp.where(lane < 16, padded, pltpu.roll(mixed, 16, 1))
    both = jnp.where(lane < 32, both, 0.0)
    both = jnp.concatenate([both, jnp.zeros((48, 128), F32)], 0).T[:32]
    mask_high, mask_low = split(both)
    change = jnp.dot(mask_high[:, :80], high, preferred_element_type=F32)
    change = change + jnp.dot(mask_high[:, :80], low, preferred_element_type=F32)
    change = change + jnp.dot(mask_low[:, :80], high, preferred_element_type=F32)
    mask = left_half((8, 128))
    for pair in range(ELEMS // 2):
        lanes = slice(pair * 128, pair * 128 + 128)
        top, bottom = change[0:8, lanes], change[8:16, lanes]
        tiled[0, 2 * pair] = jnp.where(mask, top, swap(bottom))
        tiled[0, 2 * pair + 1] = jnp.where(mask, swap(top), bottom)
        top, bottom = change[16:24, lanes], change[24:32, lanes]
        tiled[1, 2 * pair] = jnp.where(mask, top, swap(bottom))
        tiled[1, 2 * pair + 1] = jnp.where(mask, swap(top), bottom)
    for t in range(8):
        lanes = slice(t * 128, t * 128 + 128)
        solution[:, lanes] = guess[:, lanes] + tiled[0, :, t, :]
        residual[:, lanes] = first[:, lanes] - tiled[1, :, t, :]


def call(kernel, outs, scratch, specs, limit=32 * 1024):
    return pl.pallas_call(
        kernel,
        out_shape=outs,
        in_specs=specs,
        out_specs=[VMEM] * len(outs),
        scratch_shapes=scratch,
        compiler_params=pltpu.CompilerParams(vmem_limit_bytes=limit * 1024),
    )


def in_hbm(array):
    return pltpu.with_memory_space_constraint(array, pltpu.HBM)


def swapped(block, axes, first):
    lower = range(first, lax.axis_size(axes) - 1, 2)
    return lax.ppermute(block, axes, [(i, i + 1) for i in lower] + [(i + 1, i) for i in lower])


def local(right_side, start_guess, block_diag, face_lift, face_scale, neighbors, ghost_send, axes):
    sent = jax.ShapeDtypeStruct((GHOST, WIDTH), F32)
    message = jax.ShapeDtypeStruct((2 * GHOST, WIDTH), F32)
    to_other, to_pair, choose = call(
        pack_kernel,
        [message, message, jax.ShapeDtypeStruct((ELEMS, 1024), BF16)],
        [
            pltpu.VMEM((ELEMS, WIDTH), F32),
            pltpu.VMEM((FACES, ELEMS), jnp.int32),
            pltpu.VMEM((FACES, ELEMS), F32),
            pltpu.VMEM((1, 2 * GHOST), jnp.int32),
            pltpu.VMEM((ELEMS, 128), F32),
            pltpu.SMEM((1, 2 * GHOST), jnp.int32),
            pltpu.SemaphoreType.DMA((5,)),
        ],
        [HBM] * 4,
    )(*map(in_hbm, (ghost_send, start_guess, neighbors.T, face_scale.T)))
    from_other = swapped(to_other, axes, 1)
    from_pair = swapped(to_pair, axes, 0)
    block_parts, lift_parts = call(
        prep_kernel,
        [
            jax.ShapeDtypeStruct((256, ELEMS * NODES), BF16),
            jax.ShapeDtypeStruct((384, FACES * 128), BF16),
        ],
        [
            pltpu.VMEM((ELEMS, NODES * NODES), F32),
            pltpu.VMEM((FACES, NODES, NODES), F32),
            pltpu.VMEM((ELEMS, NODES, 128), F32),
            pltpu.SemaphoreType.DMA((2,)),
        ],
        [HBM] * 2,
    )(in_hbm(block_diag), in_hbm(face_lift))
    tile_scratch = pltpu.VMEM((ELEMS, 8, 128), F32)
    own_call = lambda *args: call(
        first_own_kernel, [FIELD], [tile_scratch] * 2, [VMEM] * 4
    )(*args)[0]
    own = own_call(choose, start_guess, block_parts, lift_parts)
    vector, to_other, to_pair, terms, pair_terms = call(
        first_ghost_kernel,
        [FIELD, sent, sent] + [jax.ShapeDtypeStruct((16, 3 * FACES * 2 * GHOST), BF16)] * 2,
        [],
        [VMEM] * 7,
    )(choose, own, from_other, from_pair, lift_parts, right_side, start_guess)
    basis = [vector]
    stack = lambda rows: jax.ShapeDtypeStruct((rows, ELEMS * NODES), BF16)
    from_pair = swapped(to_pair, axes, 0)
    own = own_call(choose, vector, block_parts, lift_parts)
    partial, outgoing = call(pair_kernel, [FIELD, message], [], [VMEM] * 5)(
        choose, own, from_pair, lift_parts, to_other
    )
    incoming = swapped(outgoing, axes, 1)
    missing = call(flight_kernel, [sent], [], [VMEM] * 3)(terms, lift_parts, to_other)[0]
    joint = [FIELD, FIELD, sent, message], [tile_scratch] * 2, [VMEM] * 6
    vector, own, to_pair, outgoing = call(other_own_kernel, *joint)(
        choose, partial, incoming, missing, block_parts, lift_parts
    )
    basis.append(vector)
    incoming = swapped(outgoing, axes, 0)
    missing = call(pair_flight_kernel, [sent], [], [VMEM] * 3)(pair_terms, lift_parts, to_pair)[0]
    vector, partial, to_other, outgoing = call(pair_own_kernel, *joint)(
        choose, own, incoming, missing, block_parts, lift_parts
    )
    basis.append(vector)
    incoming = swapped(outgoing, axes, 1)
    missing, high, low, gram = call(
        gram_flight_kernel,
        [sent, stack(48), stack(48), jax.ShapeDtypeStruct((48, 48), F32)],
        [tile_scratch],
        [VMEM] * 6,
    )(terms, lift_parts, to_other, *basis)
    vector, to_pair, next_other = call(other_kernel, [FIELD, sent, sent], [], [VMEM] * 5)(
        choose, partial, incoming, missing, lift_parts
    )
    from_pair = swapped(to_pair, axes, 0)
    own, high3, low3 = call(
        dense_own_kernel, [FIELD, stack(16), stack(16)], [tile_scratch] * 2, [VMEM] * 4
    )(choose, vector, block_parts, lift_parts)
    high4, low4, packed = call(
        last_kernel,
        [stack(16), stack(16), jax.ShapeDtypeStruct((2, 7, 2, 128), F32)],
        [pltpu.VMEM((ELEMS, WIDTH), F32), tile_scratch, pltpu.VMEM((128, 128), F32)],
        [VMEM] * 10,
    )(choose, own, next_other, from_pair, lift_parts, high, low, high3, low3, gram)
    outer, inner, narrow = (lax.axis_size(axis) for axis in axes)
    halves = jnp.broadcast_to(packed[None], (outer * narrow // 2, 2, 7, 2, 128))
    halves = halves.reshape(outer * narrow, 7, 2, 128)
    mine = lax.all_to_all(halves, (axes[0], axes[2]), 0, 0).sum(0)
    mine = jnp.broadcast_to(mine[None], (inner, 7, 2, 128))
    mine = lax.all_to_all(mine, axes[1], 0, 0).sum(0)
    theirs = swapped(mine, axes, 0)
    return tuple(
        call(
            solve_kernel,
            [FIELD, FIELD],
            [pltpu.VMEM((128, 128), F32), pltpu.VMEM((2, ELEMS, 8, 128), F32)],
            [VMEM] * 10,
        )(mine, theirs, high, low, high3, low3, high4, low4, basis[0], start_guess)
    )


def solution(mesh):
    wide, narrow = mesh.devices.shape
    inner = 16 if wide % 16 == 0 else 2
    axes = ("outer", "inner", "narrow")
    split_mesh = Mesh(mesh.devices.reshape(wide // inner, inner, narrow), axes)
    rows = P(axes, None)
    return jax.shard_map(
        functools.partial(local, axes=axes),
        mesh=split_mesh,
        in_specs=(rows, rows, rows, P(), rows, rows, rows),
        out_specs=(rows, rows),
        check_vma=False,
    )
```

```python
import functools

import jax
import jax.numpy as jnp
from jax import lax
from jax.experimental import pallas as pl
from jax.experimental.pallas import tpu as pltpu
from jax.sharding import Mesh, PartitionSpec as P

STEPS = 4
GAIN = 1.5
RHS = 16
NODES = 64
FACES = 6
ELEMS = 32
GHOST = 4
F32 = jnp.float32
BF16 = jnp.bfloat16

OWN, FROM, SEND = (0, 576), (640, 784), (896, 992)

VMEM = pl.BlockSpec(memory_space=pltpu.VMEM)
HBM = pl.BlockSpec(memory_space=pltpu.HBM)


WIDTH = RHS * NODES
FIELD = jax.ShapeDtypeStruct((ELEMS, WIDTH), F32)


def dot_nt(left, right):
    return lax.dot_general(left, right, (((1,), (1,)), ((), ())), preferred_element_type=F32)


def split(value):
    high = value.astype(BF16)
    low = (value - high.astype(F32)).astype(BF16)
    return high, low


def swap(value):
    return pltpu.roll(value, 64, 1)


def left_half(shape):
    return lax.broadcasted_iota(jnp.int32, shape, len(shape) - 1) < 64


def slab(t):
    return slice(t * 128, t * 128 + 128)


def to_tiles(ref, out):
    for t in range(8):
        out[:, t, :] = ref[:, slab(t)]


def selection(near, scale, first, count):
    columns = []
    for f in range(FACES):
        place = first(lax.broadcasted_iota(jnp.int32, (count, ELEMS), 0))
        columns.append(jnp.where(place == near[f : f + 1, :], scale[f : f + 1, :], 0.0))
    return jnp.concatenate(columns, 0)


def three_parts(chosen, axis):
    high = chosen.astype(BF16).astype(F32)
    return jnp.concatenate([high, high, chosen - high], axis)


def ghost_selection(near, scale, odd):
    place = lambda m: ELEMS + lax.rem(m + GHOST * odd, 2 * GHOST)
    return selection(near, scale, place, 2 * GHOST)


def pack_kernel(
    send_in, guess_in, near_in, scale_in, to_other, to_pair, guess, near, scale, terms, send, done
):
    pairs = [(send_in, send), (guess_in, guess), (near_in, near), (scale_in, scale)]
    copies = [pltpu.make_async_copy(a, b, done.at[i]) for i, (a, b) in enumerate(pairs)]
    for copy in copies:
        copy.start()
    for copy in copies:
        copy.wait()
    odd = lax.rem(lax.axis_index("narrow"), 2)
    ghosts = ghost_selection(near, scale, odd)
    terms[...] = jnp.zeros((ELEMS, 128), F32)
    terms[:, : FACES * 2 * GHOST] = ghosts.T
    for out, first in ((to_other, GHOST * odd), (to_pair, GHOST * (1 - odd))):
        out[GHOST:, :] = jnp.zeros((GHOST, WIDTH), F32)
        for k in range(GHOST):
            row = send[0, first + k]
            out[k : k + 1, :] = guess[pl.ds(row, 1), :]
            out[GHOST + k : GHOST + k + 1, :128] = terms[pl.ds(row, 1), :]


def prep_kernel(
    send_in, near_in, scale_in, lift_in, blocks_in, choose, block_parts, lift_parts,
    send_row, near, scale, lift, blocks, spread_blocks, done,
):
    pairs = [(send_in, send_row), (near_in, near), (scale_in, scale), (lift_in, lift), (blocks_in, blocks)]
    copies = [pltpu.make_async_copy(a, b, done.at[i]) for i, (a, b) in enumerate(pairs)]
    for copy in copies:
        copy.start()
    for copy in copies[:3]:
        copy.wait()
    odd = lax.rem(lax.axis_index("narrow"), 2)
    choose[...] = jnp.zeros((ELEMS, 1024), BF16)
    own = selection(near, scale, lambda n: n, ELEMS)
    choose[:, OWN[0] : OWN[1]] = three_parts(own, 0).T.astype(BF16)
    choose[:, FROM[0] : FROM[1]] = three_parts(ghost_selection(near, scale, odd), 0).T.astype(BF16)
    row = send_row[...]
    row = jnp.where(odd == 1, jnp.concatenate([row[:, GHOST:], row[:, :GHOST]], 1), row)
    rows = (lax.broadcasted_iota(jnp.int32, (ELEMS, 2 * GHOST), 0) == row).astype(F32)
    rows = jnp.concatenate([rows, jnp.zeros((ELEMS, ELEMS - 2 * GHOST), F32)], 1)
    choose[:, SEND[0] : SEND[1]] = jnp.concatenate([rows, rows, rows], 0).T.astype(BF16)
    copies[3].wait()
    for f in range(FACES):
        upper = jnp.concatenate([lift[f], jnp.zeros((NODES, NODES), F32)], 1)
        high, low = split(jnp.concatenate([upper, swap(upper)], 0).T)
        lift_parts[:128, slab(f)] = high
        lift_parts[128:256, slab(f)] = high
        lift_parts[256:, slab(f)] = low
    copies[4].wait()
    mask = left_half((ELEMS, 128))
    for pair in range(NODES // 2):
        two = blocks[:, pair * 128 : pair * 128 + 128]
        turned = swap(two)
        spread_blocks[:, 2 * pair, :] = jnp.where(mask, two, turned)
        spread_blocks[:, 2 * pair + 1, :] = jnp.where(mask, turned, two)
    for pair in range(ELEMS // 2):
        high, low = split(spread_blocks[2 * pair : 2 * pair + 2].reshape(128, 128).T)
        block_parts[:128, slab(pair)] = high
        block_parts[128:, slab(pair)] = low


def face_sum(vector, lift_parts, chosen):
    count = vector.shape[0]
    rows = jnp.concatenate([vector[:, slab(t)] for t in range(8)], 0)
    high, low = split(rows)
    both = jnp.concatenate([high, low, high], 1)
    moved = jnp.dot(both, lift_parts[...], preferred_element_type=F32)
    moved = jnp.concatenate(
        [
            jnp.concatenate([moved[t * count : (t + 1) * count, slab(f)] for t in range(8)], 1)
            for f in range(FACES)
        ],
        0,
    )
    high, low = split(moved)
    parts = jnp.concatenate([high, low, high], 0)
    return jnp.dot(chosen, parts, preferred_element_type=F32)


def from_sides(choose, lift_parts, other=None, pair=None):
    empty = jnp.zeros((GHOST, WIDTH), F32)
    ghosts = jnp.concatenate([empty if other is None else other, empty if pair is None else pair], 0)
    return face_sum(ghosts, lift_parts, choose[:, FROM[0] : FROM[1]])


def sent_rows(vector, choose):
    high = vector.astype(BF16)
    rest = vector - high.astype(F32)
    middle, low = split(rest)
    parts = jnp.concatenate([high, middle, low], 0)
    rows = jnp.dot(choose[:16, SEND[0] : SEND[1]], parts, preferred_element_type=F32)
    return rows[:GHOST], rows[GHOST : 2 * GHOST]


def dense(vector):
    upper, lower = [], []
    mask = left_half((8, 128))
    for pair in range(ELEMS // 2):
        first, second = vector[2 * pair], vector[2 * pair + 1]
        upper.append(jnp.where(mask, first, swap(second)))
        lower.append(jnp.where(mask, swap(first), second))
    return jnp.concatenate([jnp.concatenate(upper, 1), jnp.concatenate(lower, 1)], 0)


def own_part(vector, block_parts, lift_parts, choose, out, tiled, product):
    faces = face_sum(vector[...], lift_parts, choose[:, OWN[0] : OWN[1]])
    to_tiles(vector, tiled)
    value = tiled[...].reshape(ELEMS * 8, 128)
    mask = left_half((ELEMS * 8, 128))
    high, low = split(value)
    high, low = high.astype(F32), low.astype(F32)
    turned_high, turned_low = split(swap(value))
    turned_high, turned_low = turned_high.astype(F32), turned_low.astype(F32)
    first = jnp.where(mask, low, turned_high).astype(BF16)
    second = jnp.where(mask, turned_low, high).astype(BF16)
    first_rest = jnp.where(mask, high, 0.0).astype(BF16)
    second_rest = jnp.where(mask, 0.0, high).astype(BF16)
    first = jnp.concatenate([first, first_rest], 1)
    second = jnp.concatenate([second, second_rest], 1)
    mask = left_half((8, 128))
    for group in range(ELEMS // 4):
        rows = slice(group * 32, (group + 1) * 32)
        both = jnp.concatenate([first[rows], second[rows]], 0)
        columns = block_parts[:, group * 256 : (group + 1) * 256]
        result = jnp.dot(both, columns, preferred_element_type=F32)
        for part in range(4):
            lanes = slab(part // 2)
            top = result[part * 8 : part * 8 + 8, lanes]
            bottom = result[32 + part * 8 : 40 + part * 8, lanes]
            if part % 2 == 0:
                product[group * 4 + part] = jnp.where(mask, top, swap(bottom))
            else:
                product[group * 4 + part] = jnp.where(mask, swap(top), bottom)
    for t in range(8):
        out[:, slab(t)] = faces[:, slab(t)] + product[:, t, :]


def gram_of(left_high, left_low, high, low):
    count = left_high.shape[0]
    both = dot_nt(jnp.concatenate([left_high, left_low], 0), high)
    return both[:count] + both[count:] + dot_nt(left_high, low)


def first_own_kernel(choose, vector, block_parts, lift_parts, out, tiled, product):
    own_part(vector, block_parts, lift_parts, choose, out, tiled, product)


def dense_own_kernel(
    choose, vector, block_parts, lift_parts, out, high_out, low_out, tiled, product
):
    own_part(vector, block_parts, lift_parts, choose, out, tiled, product)
    high_out[...], low_out[...] = split(dense(tiled))


def first_ghost_kernel(
    choose, own, from_other, from_pair, lift_parts, right, guess,
    out, to_other, to_pair, terms, pair_terms,
):
    faces = from_sides(choose, lift_parts, from_other[:GHOST], from_pair[:GHOST])
    vector = right[...] - (guess[...] + (own[...] + faces))
    out[...] = vector
    to_other[...], to_pair[...] = sent_rows(vector, choose)
    for sent, out in ((from_other, terms), (from_pair, pair_terms)):
        theirs = three_parts(sent[GHOST:, : FACES * 2 * GHOST], 1)
        empty = jnp.zeros((16 - GHOST, theirs.shape[1]), F32)
        out[...] = jnp.concatenate([theirs, empty], 0).astype(BF16)


def pair_kernel(choose, own, from_pair, lift_parts, to_other, partial, message):
    total = own[...] + from_sides(choose, lift_parts, pair=from_pair[...])
    partial[...] = total
    message[:GHOST] = to_other[...]
    message[GHOST:] = sent_rows(GAIN * total, choose)[0]


def missing_terms(terms, lift_parts, to_other, missing):
    rows = jnp.concatenate([to_other[...], jnp.zeros((GHOST, WIDTH), F32)], 0)
    missing[...] = GAIN * face_sum(rows, lift_parts, terms[...])[:GHOST]


def flight_kernel(terms, lift_parts, to_other, missing):
    missing_terms(terms, lift_parts, to_other, missing)


def gram_flight_kernel(
    terms, lift_parts, to_other, first, second, third, missing, high, low, gram, tiled
):
    missing_terms(terms, lift_parts, to_other, missing)
    for a, vector in enumerate((first, second, third)):
        to_tiles(vector, tiled)
        high[16 * a : 16 * a + 16], low[16 * a : 16 * a + 16] = split(dense(tiled))
    gram[...] = gram_of(high[...], low[...], high[...], low[...])


def other_own_kernel(
    choose, partial, message, missing, block_parts, lift_parts, out, own, to_pair, outgoing, tiled, product
):
    vector = GAIN * (partial[...] + from_sides(choose, lift_parts, other=message[:GHOST]))
    out[...] = vector
    own_part(out, block_parts, lift_parts, choose, own, tiled, product)
    total = own[...] + from_sides(choose, lift_parts, other=message[GHOST:] + missing[...])
    own[...] = total
    rows = sent_rows(vector, choose)[1]
    to_pair[...] = rows
    outgoing[:GHOST] = rows
    outgoing[GHOST:] = sent_rows(GAIN * total, choose)[1]


def pair_flight_kernel(terms, lift_parts, to_pair, missing):
    rows = jnp.concatenate([jnp.zeros((GHOST, WIDTH), F32), to_pair[...]], 0)
    missing[...] = GAIN * face_sum(rows, lift_parts, terms[...])[:GHOST]


def pair_own_kernel(
    choose, own, message, missing, block_parts, lift_parts, out, partial, to_other, outgoing, tiled, product
):
    vector = GAIN * (own[...] + from_sides(choose, lift_parts, pair=message[:GHOST]))
    out[...] = vector
    own_part(out, block_parts, lift_parts, choose, partial, tiled, product)
    total = partial[...] + from_sides(choose, lift_parts, pair=message[GHOST:] + missing[...])
    partial[...] = total
    rows = sent_rows(vector, choose)[0]
    to_other[...] = rows
    outgoing[:GHOST] = rows
    outgoing[GHOST:] = sent_rows(GAIN * total, choose)[0]


def other_kernel(choose, partial, message, missing, lift_parts, out, to_pair, next_other):
    faces = from_sides(choose, lift_parts, other=message[:GHOST])
    vector = GAIN * (partial[...] + faces)
    out[...] = vector
    to_pair[...] = sent_rows(vector, choose)[1]
    next_other[...] = message[GHOST:] + missing[...]


def fold(blocks):
    lane = lax.broadcasted_iota(jnp.int32, (1, 128), 1)
    rows = []
    for k in range(14):
        part = pltpu.roll(blocks[14 + k // 7 : 15 + k // 7, :], (112 - 16 * (k % 7)) % 128, 1)
        rows.append(jnp.where(lane < 112, blocks[k : k + 1, :], part))
    return rows


def unfold(rows):
    lane = lax.broadcasted_iota(jnp.int32, (1, 128), 1) // 16
    ends = []
    for half in range(2):
        total = jnp.zeros((1, 128), F32)
        for b in range(7):
            part = pltpu.roll(rows[7 * half + b], 16 * b + 16, 1)
            total = jnp.where(lane == b, part, total)
        ends.append(total)
    return jnp.concatenate(rows + ends, 0)


def last_kernel(
    choose, own, from_other, from_pair, lift_parts, high, low, high3, low3, gram, high4, low4, packed, newest, tiled, gram_low,
):
    newest[...] = GAIN * (own[...] + from_sides(choose, lift_parts, from_other[...], from_pair[...]))
    to_tiles(newest, tiled)
    high4[...], low4[...] = split(dense(tiled))
    stack_high = jnp.concatenate([high[...], high3[...], high4[...]], 0)
    stack_low = jnp.concatenate([low[...], low3[...], low4[...]], 0)
    between = gram_of(high[32:48, :], low[32:48, :], high3[...], low3[...])
    rows = gram_of(stack_high[48:], stack_low[48:], stack_high, stack_low)
    gram_low[...] = jnp.zeros((128, 128), F32)
    gram_low[0:48, 0:64] = jnp.concatenate(
        [gram[...], jnp.concatenate([jnp.zeros((32, 16), F32), between], 0)], 1
    )
    gram_low[48:80, 0:80] = rows
    full = gram_low[...]
    weighted = full[:64] + full[16:80] * (1.0 / GAIN)
    normal = weighted + pltpu.roll(weighted, 112, 1) * (1.0 / GAIN)
    lane = lax.broadcasted_iota(jnp.int32, (16, 128), 1)
    joined = []
    for a in range(STEPS):
        part = slice(16 * a, 16 * a + 16)
        width = 16 * (a + 1)
        right = pltpu.roll(weighted[part], width, 1)
        joined.append(jnp.where(lane < width, normal[part], right))
    first = jnp.where(lane < 80, joined[3], pltpu.roll(joined[0], 80, 1))
    second = jnp.where(lane < 64, joined[2], pltpu.roll(joined[1], 64, 1))
    for half, blocks in enumerate((first, second)):
        folded = fold(blocks)
        for k in range(7):
            packed[half, k] = jnp.concatenate(folded[2 * k : 2 * k + 2], 0)


def solve_spd(system):
    size, block = 64, 16
    row_id = lax.broadcasted_iota(jnp.int32, (block, 128), 0)
    for start in range(0, size, block):
        stop = start + block
        columns = [jnp.broadcast_to(system[:, start + j : start + j + 1], (size, 128)) for j in range(block)]
        pivots = [column[start:stop, :] for column in columns]
        rows = system[start:stop, :]
        for j in range(block):
            here = row_id == j
            inverse = 1.0 / pivots[j][j : j + 1, :]
            factor = pivots[j]
            for l in range(j + 1, block):
                scaled = pivots[l][j : j + 1, :] * inverse
                pivots[l] = jnp.where(here, scaled, pivots[l] - factor * scaled)
            scaled = rows[j : j + 1, :] * inverse
            rows = jnp.where(here, scaled, rows - factor * scaled)
        terms = [columns[j] * rows[j : j + 1, :] for j in range(block)]
        while len(terms) > 1:
            terms = [a + b for a, b in zip(terms[::2], terms[1::2])]
        update = system - terms[0]
        parts = [update[:start], rows, update[stop:]]
        system = jnp.concatenate([part for part in parts if part.shape[0]], 0)
    return system


def solve_kernel(
    mine, theirs, high, low, high3, low3, high4, low4, first, guess,
    solution, residual, gram_low, tiled,
):
    high = jnp.concatenate([high[...], high3[...], high4[...]], 0)
    low = jnp.concatenate([low[...], low3[...], low4[...]], 0)
    odd = lax.rem(lax.axis_index("narrow"), 2) == 1
    halves = []
    for one, two in ((mine, theirs), (theirs, mine)):
        pairs = [jnp.where(odd, two[k], one[k]) for k in range(7)]
        halves.append(unfold([pair[i : i + 1, :] for pair in pairs for i in range(2)]))
    lane = lax.broadcasted_iota(jnp.int32, (16, 128), 1)
    joined = [pltpu.roll(halves[0], 48, 1), pltpu.roll(halves[1], 64, 1), halves[1], halves[0]]
    for a, part in enumerate(joined):
        width = 16 * (a + 1)
        right = pltpu.roll(part, (64 - width) % 128, 1)
        right = jnp.where((lane >= 64) & (lane < 80), right, 0.0)
        gram_low[16 * a : 16 * a + 16, :] = jnp.where(lane < width, part, right)
    gram_low[64:, :] = jnp.zeros((64, 128), F32)
    known = gram_low[...]
    row = lax.broadcasted_iota(jnp.int32, (64, 128), 0) // 16
    column = lax.broadcasted_iota(jnp.int32, (64, 128), 1) // 16
    system = jnp.where((row >= column) | (column >= 4), known[:64], known.T[:64])
    coeffs = pltpu.roll(solve_spd(system), 64, 1)
    empty = jnp.zeros((16, 128), F32)
    padded = jnp.concatenate([coeffs, empty], 0)
    mixed = padded + jnp.concatenate([empty, coeffs], 0) * (1.0 / GAIN)
    lane = lax.broadcasted_iota(jnp.int32, (80, 128), 1)
    both = jnp.where(lane < 16, padded, pltpu.roll(mixed, 16, 1))
    both = jnp.where(lane < 32, both, 0.0)
    both = jnp.concatenate([both, jnp.zeros((48, 128), F32)], 0).T[:32]
    mask_high, mask_low = split(both)
    change = jnp.dot(mask_high[:, :80], high, preferred_element_type=F32)
    change = change + jnp.dot(mask_high[:, :80], low, preferred_element_type=F32)
    change = change + jnp.dot(mask_low[:, :80], high, preferred_element_type=F32)
    mask = left_half((8, 128))
    for pair in range(ELEMS // 2):
        lanes = slice(pair * 128, pair * 128 + 128)
        top, bottom = change[0:8, lanes], change[8:16, lanes]
        tiled[0, 2 * pair] = jnp.where(mask, top, swap(bottom))
        tiled[0, 2 * pair + 1] = jnp.where(mask, swap(top), bottom)
        top, bottom = change[16:24, lanes], change[24:32, lanes]
        tiled[1, 2 * pair] = jnp.where(mask, top, swap(bottom))
        tiled[1, 2 * pair + 1] = jnp.where(mask, swap(top), bottom)
    for t in range(8):
        lanes = slice(t * 128, t * 128 + 128)
        solution[:, lanes] = guess[:, lanes] + tiled[0, :, t, :]
        residual[:, lanes] = first[:, lanes] - tiled[1, :, t, :]


def call(kernel, outs, scratch, specs, limit=32 * 1024):
    return pl.pallas_call(
        kernel,
        out_shape=outs,
        in_specs=specs,
        out_specs=[VMEM] * len(outs),
        scratch_shapes=scratch,
        compiler_params=pltpu.CompilerParams(vmem_limit_bytes=limit * 1024),
    )


def in_hbm(array):
    return pltpu.with_memory_space_constraint(array, pltpu.HBM)


def swapped(block, axes, first):
    lower = range(first, lax.axis_size(axes) - 1, 2)
    return lax.ppermute(block, axes, [(i, i + 1) for i in lower] + [(i + 1, i) for i in lower])


def local(right_side, start_guess, block_diag, face_lift, face_scale, neighbors, ghost_send, axes):
    sent = jax.ShapeDtypeStruct((GHOST, WIDTH), F32)
    message = jax.ShapeDtypeStruct((2 * GHOST, WIDTH), F32)
    send, near, scale = map(in_hbm, (ghost_send, neighbors.T, face_scale.T))
    tables = [pltpu.VMEM((FACES, ELEMS), jnp.int32), pltpu.VMEM((FACES, ELEMS), F32)]
    to_other, to_pair = call(
        pack_kernel,
        [message, message],
        [pltpu.VMEM((ELEMS, WIDTH), F32)]
        + tables
        + [
            pltpu.VMEM((ELEMS, 128), F32),
            pltpu.SMEM((1, 2 * GHOST), jnp.int32),
            pltpu.SemaphoreType.DMA((4,)),
        ],
        [HBM] * 4,
    )(send, in_hbm(start_guess), near, scale)
    from_other = swapped(to_other, axes, 1)
    from_pair = swapped(to_pair, axes, 0)
    choose, block_parts, lift_parts = call(
        prep_kernel,
        [
            jax.ShapeDtypeStruct((ELEMS, 1024), BF16),
            jax.ShapeDtypeStruct((256, ELEMS * NODES), BF16),
            jax.ShapeDtypeStruct((384, FACES * 128), BF16),
        ],
        [pltpu.VMEM((1, 2 * GHOST), jnp.int32)]
        + tables
        + [
            pltpu.VMEM((FACES, NODES, NODES), F32),
            pltpu.VMEM((ELEMS, NODES * NODES), F32),
            pltpu.VMEM((ELEMS, NODES, 128), F32),
            pltpu.SemaphoreType.DMA((5,)),
        ],
        [HBM] * 5,
    )(send, near, scale, in_hbm(face_lift), in_hbm(block_diag))
    tile_scratch = pltpu.VMEM((ELEMS, 8, 128), F32)
    own_call = lambda *args: call(
        first_own_kernel, [FIELD], [tile_scratch] * 2, [VMEM] * 4
    )(*args)[0]
    own = own_call(choose, start_guess, block_parts, lift_parts)
    vector, to_other, to_pair, terms, pair_terms = call(
        first_ghost_kernel,
        [FIELD, sent, sent] + [jax.ShapeDtypeStruct((16, 3 * FACES * 2 * GHOST), BF16)] * 2,
        [],
        [VMEM] * 7,
    )(choose, own, from_other, from_pair, lift_parts, right_side, start_guess)
    basis = [vector]
    stack = lambda rows: jax.ShapeDtypeStruct((rows, ELEMS * NODES), BF16)
    from_pair = swapped(to_pair, axes, 0)
    own = own_call(choose, vector, block_parts, lift_parts)
    partial, outgoing = call(pair_kernel, [FIELD, message], [], [VMEM] * 5)(
        choose, own, from_pair, lift_parts, to_other
    )
    incoming = swapped(outgoing, axes, 1)
    missing = call(flight_kernel, [sent], [], [VMEM] * 3)(terms, lift_parts, to_other)[0]
    joint = [FIELD, FIELD, sent, message], [tile_scratch] * 2, [VMEM] * 6
    vector, own, to_pair, outgoing = call(other_own_kernel, *joint)(
        choose, partial, incoming, missing, block_parts, lift_parts
    )
    basis.append(vector)
    incoming = swapped(outgoing, axes, 0)
    missing = call(pair_flight_kernel, [sent], [], [VMEM] * 3)(pair_terms, lift_parts, to_pair)[0]
    vector, partial, to_other, outgoing = call(pair_own_kernel, *joint)(
        choose, own, incoming, missing, block_parts, lift_parts
    )
    basis.append(vector)
    incoming = swapped(outgoing, axes, 1)
    missing, high, low, gram = call(
        gram_flight_kernel,
        [sent, stack(48), stack(48), jax.ShapeDtypeStruct((48, 48), F32)],
        [tile_scratch],
        [VMEM] * 6,
    )(terms, lift_parts, to_other, *basis)
    vector, to_pair, next_other = call(other_kernel, [FIELD, sent, sent], [], [VMEM] * 5)(
        choose, partial, incoming, missing, lift_parts
    )
    from_pair = swapped(to_pair, axes, 0)
    own, high3, low3 = call(
        dense_own_kernel, [FIELD, stack(16), stack(16)], [tile_scratch] * 2, [VMEM] * 4
    )(choose, vector, block_parts, lift_parts)
    high4, low4, packed = call(
        last_kernel,
        [stack(16), stack(16), jax.ShapeDtypeStruct((2, 7, 2, 128), F32)],
        [pltpu.VMEM((ELEMS, WIDTH), F32), tile_scratch, pltpu.VMEM((128, 128), F32)],
        [VMEM] * 10,
    )(choose, own, next_other, from_pair, lift_parts, high, low, high3, low3, gram)
    outer, inner, narrow = (lax.axis_size(axis) for axis in axes)
    halves = jnp.broadcast_to(packed[None], (outer * narrow // 2, 2, 7, 2, 128))
    halves = halves.reshape(outer * narrow, 7, 2, 128)
    mine = lax.all_to_all(halves, (axes[0], axes[2]), 0, 0).sum(0)
    mine = jnp.broadcast_to(mine[None], (inner, 7, 2, 128))
    mine = lax.all_to_all(mine, axes[1], 0, 0).sum(0)
    theirs = swapped(mine, axes, 0)
    return tuple(
        call(
            solve_kernel,
            [FIELD, FIELD],
            [pltpu.VMEM((128, 128), F32), pltpu.VMEM((2, ELEMS, 8, 128), F32)],
            [VMEM] * 10,
        )(mine, theirs, high, low, high3, low3, high4, low4, basis[0], start_guess)
    )


def solution(mesh):
    wide, narrow = mesh.devices.shape
    inner = 16 if wide % 16 == 0 else 2
    axes = ("outer", "inner", "narrow")
    split_mesh = Mesh(mesh.devices.reshape(wide // inner, inner, narrow), axes)
    rows = P(axes, None)
    return jax.shard_map(
        functools.partial(local, axes=axes),
        mesh=split_mesh,
        in_specs=(rows, rows, rows, P(), rows, rows, rows),
        out_specs=(rows, rows),
        check_vma=False,
    )
```
